32 devices in a mesh: path: 8 (over y, x, core), shard: 4 (over z).
Axes of the slice: x: 2, y: 2, z: 4, core: 2. Of those that a mesh axis runs over, the one named last changes fastest.
Arguments:
- path_delta: float32 [8, 2, 512, 1024], P('path', None, 'shard'), may hold values from -500 to 500
- assign: int32 [8, 2], replicated, may hold values from 0 to 15
- params: float32 [32, 4, 128, 1024], P(None, 'shard', 'path'), may hold values from -6 to 6
- momentum: float32 [32, 4, 128, 1024], P(None, 'shard', 'path'), may hold values from -3 to 3
Outputs:
- path_params: float32 [8, 2, 512, 1024], P('path', None, 'shard')
- new_params: float32 [32, 4, 128, 1024], P(None, 'shard', 'path')
- new_momentum: float32 [32, 4, 128, 1024], P(None, 'shard', 'path')
The draws below stay inside these ranges and needn't reach their ends.
All inputs are finite; a program needn't handle non-finite values.
Results may differ from the reference program's by a relative error of at most 0.00007.
Values sent between devices are 32-bit elements; how exact they have to be, the bound alone decides.
No kernel may reach another device: no remote copies, remote signals or barrier semaphores. Data moves between devices by JAX's collectives and lax.ppermute only.
A program may use at most 128 MiB of HBM per device.

```python
import math
import jax
import jax.numpy as jnp
import numpy as np
from jax import lax

D = 1024
LEVEL_MODULES = 16
LEVELS = 2
ROWS = 512
PATHS = 8
MODULES = 32
BLOCK = 128
N_SHARD = 4


def draw_path_delta(key, part):
    key_base = jax.random.fold_in(key, 11)
    key_cols = jax.random.fold_in(key, 12)
    shape = (PATHS, LEVELS, ROWS, D)
    ramp = jnp.arange(ROWS, dtype=jnp.float32) / float(ROWS - 1)
    row_scale = jnp.exp(ramp * math.log(10.0))
    col_scale = jnp.exp(jax.random.uniform(key_cols, (PATHS, LEVELS, 1, D), jnp.float32) * math.log(10.0))
    base = jnp.clip(jax.random.normal(key_base, shape, jnp.float32), -4.0, 4.0)
    return base * row_scale[None, None, :, None] * col_scale


def place_ends(result, own_key, smallest, high):
    shape = result.shape
    spot = [jax.random.randint(jax.random.fold_in(own_key, axis), (), 0, shape[axis]) for axis in range(len(shape))]
    result = result.at[tuple(spot)].set(smallest)
    longest = shape.index(max(shape))
    spot[longest] = (spot[longest] + 1) % shape[longest]
    return result.at[tuple(spot)].set(high)


def block_scale(stream_key, extent, shards, least, largest):
    factor_of = 1.0
    for dim, shards_of in shards:
        heights = jax.random.uniform(jax.random.fold_in(jax.random.fold_in(stream_key, 6), dim), (shards_of,), jnp.float32, least / len(shards), largest / len(shards))
        factor_of = factor_of * jnp.repeat(jnp.exp(heights), extent[dim] // shards_of).reshape((-1,) + (1,) * (len(extent) - 1 - dim))
    return factor_of


def cumulative_ranks(amount, lean):
    portions = [(1 << 20) // math.isqrt(standing ** lean) + 1 for standing in range(1, amount + 1)]
    scale = 1 + sum(portions) // (1 << 30)
    return np.cumsum(np.array([max(1, weight // scale) for weight in portions]))


def ranked_ids(key, dims, count, skew):
    grid = cumulative_ranks(count, skew)
    pick = jax.random.randint(jax.random.fold_in(key, 1), dims, 0, int(grid[count - 1]))
    grade = jnp.searchsorted(jnp.asarray(grid, jnp.int32), pick, side="right")
    return jax.random.permutation(jax.random.fold_in(key, 2), count)[grade].astype(jnp.int32)


def bell_draw(key, shape, spread, limit, pieces=(), kind=jnp.bfloat16):
    level = block_scale(key, shape, pieces, -0.22, 0.18) if pieces else 1.0
    result = jax.random.normal(key, shape, jnp.float32) * spread * level
    return jnp.minimum(jnp.maximum(result, -limit), limit).astype(kind)


def setup_inputs(seed: int = 0) -> dict:
    keys = jax.random.split(jax.random.key(seed), 5)
    path_delta = draw_path_delta(jax.random.fold_in(keys[4], 71), 0)
    assign = place_ends(ranked_ids(keys[1], (PATHS, LEVELS), LEVEL_MODULES, 2), jax.random.fold_in(keys[1], 3), 0, LEVEL_MODULES - 1).astype(jnp.int32)
    params = bell_draw(keys[2], (MODULES, N_SHARD, BLOCK, D), 1.0, 6.0, ((1, 4), (2, 8)), jnp.float32)
    momentum = bell_draw(keys[3], (MODULES, N_SHARD, BLOCK, D), 0.5, 3.0, ((1, 4), (2, 8)), jnp.float32)
    return {"path_delta": path_delta, "assign": assign, "params": params, "momentum": momentum}


outer_rate = 0.7
beta_coef = 0.9

def reference(path_delta, assign, params, momentum):
    norm_sq = lax.optimization_barrier(jnp.sum(path_delta * path_delta, axis=(1, 2, 3)))
    rescale = 1.0 / jnp.sqrt(norm_sq / (LEVELS * ROWS * D) + 1e-06)
    scaled = path_delta * rescale[:, None, None, None]
    offsets = (jnp.arange(LEVELS, dtype=jnp.int32) * LEVEL_MODULES).astype(jnp.int32)
    module_id = (assign + offsets[None, :]).astype(jnp.int32)
    flat_ids = module_id.reshape(-1)
    sharers = lax.optimization_barrier(jnp.sum((flat_ids[:, None] == jnp.arange(MODULES, dtype=jnp.int32)[None, :]).astype(jnp.int32), axis=0))
    totals = jax.ops.segment_sum(scaled.reshape(PATHS * LEVELS, ROWS * D), flat_ids, num_segments=MODULES)
    divisor = jnp.maximum(sharers, 1).astype(totals.dtype)
    outer_grad = (totals / divisor[:, None]).reshape(MODULES, N_SHARD, BLOCK, D)
    new_momentum = beta_coef * momentum + outer_grad
    new_params = params - outer_rate * (outer_grad + beta_coef * new_momentum)
    path_params = jnp.take(new_params.reshape(MODULES, ROWS, D), flat_ids, axis=0).reshape(PATHS, LEVELS, ROWS, D)
    return (path_params, new_params, new_momentum)
```

```python
import jax
import jax.numpy as jnp
from jax import lax
from jax.experimental import pallas as pl
from jax.experimental.pallas import tpu as pltpu
from jax.sharding import PartitionSpec as P

LEVEL_MODULES = 16
LEVELS = 2

outer_rate = 0.7
beta_coef = 0.9
moment_coef = outer_rate * beta_coef * beta_coef
grad_coef = outer_rate * (1.0 + beta_coef)

VMEM_LIMIT = 48 * 1024 * 1024


def params_of():
    return pltpu.CompilerParams(vmem_limit_bytes=VMEM_LIMIT)


def squares_kernel(delta_ref, out_ref):
    total = jnp.zeros(out_ref.shape, jnp.float32)
    for level in range(delta_ref.shape[0]):
        block = delta_ref[level]
        block = block * block
        folded = block.reshape(block.shape[0] // 8, 8, block.shape[1]).sum(axis=0)
        for lane in range(0, block.shape[1], 128):
            total = total + folded[:, lane : lane + 128]
    out_ref[...] = total


def gather_kernel(ids_ref, params_ref, momentum_ref, out_ref, param_rows, moment_rows, sems):
    path_count = out_ref.shape[1]
    copies = []
    for level in range(LEVELS):
        for path in range(path_count):
            module = ids_ref[path, level] + level * LEVEL_MODULES
            copies.append(
                (
                    pltpu.make_async_copy(params_ref.at[module], param_rows.at[level, path], sems.at[0, level, path]),
                    pltpu.make_async_copy(momentum_ref.at[module], moment_rows.at[level, path], sems.at[1, level, path]),
                )
            )
    for first, second in copies:
        first.start()
        second.start()
    for level in range(LEVELS):
        for path in range(path_count):
            first, second = copies[level * path_count + path]
            first.wait()
            second.wait()
            out_ref[level, path] = param_rows[level, path] - moment_coef * moment_rows[level, path]


def rescales(norm_ref, path_count, entries):
    shards = norm_ref.shape[0] // path_count
    result = []
    for path in range(path_count):
        tile = norm_ref[path * shards]
        for shard in range(1, shards):
            tile = tile + norm_ref[path * shards + shard]
        total = jnp.sum(tile, keepdims=True)
        result.append(1.0 / jnp.sqrt(total / entries + 1e-06))
    return result


def sharers_of(ids_ref, level, module):
    count = 0
    for path in range(ids_ref.shape[0]):
        count = count + (ids_ref[path, level] == module).astype(jnp.int32)
    return count


def outgoing_kernel(level, entries, ids_ref, norm_ref, received_ref, base_ref, out_ref):
    path_count = received_ref.shape[0]
    scale = rescales(norm_ref, path_count, entries)
    for path in range(path_count):
        module = ids_ref[path, level]
        weight = grad_coef / sharers_of(ids_ref, level, module).astype(jnp.float32)
        total = base_ref[path]
        for other in range(path_count):
            factor = jnp.where(ids_ref[other, level] == module, weight, 0.0)
            total = total - (scale[other] * factor) * received_ref[other]
        out_ref[path] = total


def state_kernel(level, entries, ids_ref, norm_ref, received_ref, params_ref, momentum_ref, *outs):
    new_params_ref, new_momentum_ref = outs[-2:]
    path_count = received_ref.shape[0]
    scale = rescales(norm_ref, path_count, entries)
    count = params_ref.shape[0]
    for place in range(count):
        module = pl.program_id(0) * count + place
        sharers = jnp.maximum(sharers_of(ids_ref, level, module), 1)
        weight = 1.0 / sharers.astype(jnp.float32)
        grad = jnp.zeros(received_ref.shape[1:], jnp.float32)
        for other in range(path_count):
            factor = jnp.where(ids_ref[other, level] == module, weight, 0.0)
            grad = grad + (scale[other] * factor) * received_ref[other]
        new_moment = beta_coef * momentum_ref[place] + grad
        new_momentum_ref[place] = new_moment
        new_params_ref[place] = params_ref[place] - outer_rate * (grad + beta_coef * new_moment)


def local(path_delta, assign, params, momentum):
    own_slab = path_delta[0]
    path_count = assign.shape[0]
    module_count = params.shape[0]
    own_rows = params.shape[2]
    width = own_slab.shape[2]
    shards = lax.axis_size("shard")
    entries = float(own_slab.shape[0] * own_slab.shape[1] * width * shards)
    state_in = params.reshape(module_count, own_rows, width)
    moment_in = momentum.reshape(module_count, own_rows, width)
    vmem = pl.BlockSpec(memory_space=pltpu.VMEM)
    smem = pl.BlockSpec(memory_space=pltpu.SMEM)
    anywhere = pl.BlockSpec(memory_space=pl.ANY)

    squares = pl.pallas_call(
        squares_kernel,
        out_shape=jax.ShapeDtypeStruct((8, 128), jnp.float32),
        in_specs=[vmem],
        out_specs=vmem,
        compiler_params=params_of(),
    )(own_slab)
    norms = lax.all_to_all(
        jnp.broadcast_to(squares[None], (path_count * shards, 8, 128)),
        ("path", "shard"),
        split_axis=0,
        concat_axis=0,
        tiled=True,
    )
    received = [
        lax.all_to_all(
            own_slab[level].reshape(path_count, own_rows, width), "path", split_axis=0, concat_axis=0, tiled=True
        )
        for level in range(LEVELS)
    ]
    base = pl.pallas_call(
        gather_kernel,
        out_shape=jax.ShapeDtypeStruct((LEVELS, path_count, own_rows, width), jnp.float32),
        in_specs=[smem, anywhere, anywhere],
        out_specs=vmem,
        scratch_shapes=[
            pltpu.VMEM((LEVELS, path_count, own_rows, width), jnp.float32),
            pltpu.VMEM((LEVELS, path_count, own_rows, width), jnp.float32),
            pltpu.SemaphoreType.DMA((2, LEVELS, path_count)),
        ],
        compiler_params=params_of(),
    )(assign, state_in, moment_in)
    returned = []
    for level in range(LEVELS):
        outgoing = pl.pallas_call(
            lambda *refs, level=level: outgoing_kernel(level, entries, *refs),
            out_shape=jax.ShapeDtypeStruct((path_count, own_rows, width), jnp.float32),
            in_specs=[smem, vmem, vmem, vmem],
            out_specs=vmem,
            compiler_params=params_of(),
        )(assign, norms, received[level], base[level])
        returned.append(
            lax.all_to_all(outgoing, "path", split_axis=0, concat_axis=0, tiled=True).reshape(
                path_count * own_rows, width
            )
        )
    new_state, new_moment = None, None
    block = 4
    steps = LEVEL_MODULES // block
    for level in range(LEVELS):
        level_block = pl.BlockSpec((block, own_rows, width), lambda i, level=level: (i + level * steps, 0, 0))
        call_in = [assign, norms, received[level], state_in, moment_in]
        in_specs = [smem, vmem, vmem, level_block, level_block]
        kernel = lambda *refs, level=level: state_kernel(level, entries, *refs)
        aliases = {}
        if level:
            call_in += [new_state, new_moment]
            in_specs += [anywhere, anywhere]
            aliases = {5: 0, 6: 1}
        new_state, new_moment = pl.pallas_call(
            kernel,
            grid=(steps,),
            out_shape=[jax.ShapeDtypeStruct(state_in.shape, jnp.float32)] * 2,
            in_specs=in_specs,
            out_specs=[level_block, level_block],
            input_output_aliases=aliases,
            compiler_params=params_of(),
        )(*call_in)
    return (jnp.stack(returned)[None], new_state[:, None], new_moment[:, None])


def solution(mesh):
    in_specs = (
        P("path", None, "shard", None),
        P(),
        P(None, "shard", "path", None),
        P(None, "shard", "path", None),
    )
    out_specs = (
        P("path", None, "shard", None),
        P(None, "shard", "path", None),
        P(None, "shard", "path", None),
    )
    return jax.shard_map(local, mesh=mesh, in_specs=in_specs, out_specs=out_specs, check_vma=False)
```

```python
import jax
import jax.numpy as jnp
from jax import lax
from jax.experimental import pallas as pl
from jax.experimental.pallas import tpu as pltpu
from jax.sharding import PartitionSpec as P

LEVEL_MODULES = 16
LEVELS = 2

outer_rate = 0.7
beta_coef = 0.9
moment_coef = outer_rate * beta_coef * beta_coef
grad_coef = outer_rate * (1.0 + beta_coef)

VMEM_LIMIT = 48 * 1024 * 1024

vmem = pl.BlockSpec(memory_space=pltpu.VMEM)
smem = pl.BlockSpec(memory_space=pltpu.SMEM)
anywhere = pl.BlockSpec(memory_space=pl.ANY)


def call(kernel, out_shape, in_specs, out_specs, **more):
    return pl.pallas_call(
        kernel,
        out_shape=out_shape,
        in_specs=in_specs,
        out_specs=out_specs,
        compiler_params=pltpu.CompilerParams(vmem_limit_bytes=VMEM_LIMIT),
        **more,
    )


def exchange(arrays, axis):
    size = lax.axis_size(axis)
    return [arrays[0]] + [
        lax.ppermute(arrays[k], axis, [(i, i ^ k) for i in range(size)]) for k in range(1, size)
    ]


def squares_kernel(delta_ref, out_ref):
    total = jnp.zeros(out_ref.shape, jnp.float32)
    for level in range(delta_ref.shape[0]):
        block = delta_ref[level]
        block = block * block
        folded = block.reshape(block.shape[0] // 8, 8, block.shape[1]).sum(axis=0)
        for lane in range(0, block.shape[1], 128):
            total = total + folded[:, lane : lane + 128]
    out_ref[...] = total


def pack_kernel(entries, shards, here_ref, delta_ref, *refs):
    tiles, outs = refs[:shards], refs[shards:]
    tile = tiles[0][...]
    for other in tiles[1:]:
        tile = tile + other[...]
    rescale = 1.0 / jnp.sqrt(jnp.sum(tile, keepdims=True) / entries + 1e-06)
    for k, out in enumerate(outs):
        for level in range(LEVELS):
            out[level] = delta_ref[level, here_ref[0] ^ k] * rescale


def gather_kernel(here_ref, ids_ref, params_ref, momentum_ref, out_ref, param_rows, moment_rows, sems):
    path_count = out_ref.shape[1]
    copies = []
    for level in range(LEVELS):
        for k in range(path_count):
            module = ids_ref[here_ref[0] ^ k, level] + level * LEVEL_MODULES
            copies.append(
                (
                    pltpu.make_async_copy(params_ref.at[module], param_rows.at[level, k], sems.at[0, level, k]),
                    pltpu.make_async_copy(momentum_ref.at[module], moment_rows.at[level, k], sems.at[1, level, k]),
                )
            )
    for first, second in copies:
        first.start()
        second.start()
    for level in range(LEVELS):
        for k in range(path_count):
            first, second = copies[level * path_count + k]
            first.wait()
            second.wait()
            out_ref[level, k] = param_rows[level, k] - moment_coef * moment_rows[level, k]


def sharers_of(ids_ref, level, module):
    count = 0
    for path in range(ids_ref.shape[0]):
        count = count + (ids_ref[path, level] == module).astype(jnp.int32)
    return jnp.maximum(count, 1).astype(jnp.float32)


def outgoing_kernel(path_count, here_ref, ids_ref, base_ref, *refs):
    received, outs = refs[:path_count], refs[path_count:]
    here = here_ref[0]
    for level in range(LEVELS):
        for k in range(path_count):
            module = ids_ref[here ^ k, level]
            weight = grad_coef / sharers_of(ids_ref, level, module)
            total = base_ref[level, k]
            for other in range(path_count):
                factor = jnp.where(ids_ref[here ^ other, level] == module, weight, 0.0)
                total = total - factor * received[other][level]
            outs[k][level] = total


def state_kernel(path_count, here_ref, ids_ref, *refs):
    received = refs[:path_count]
    params_ref, momentum_ref, new_params_ref, new_momentum_ref = refs[path_count:]
    here = here_ref[0]
    count = params_ref.shape[0]
    first = pl.program_id(0) * count
    level = first // LEVEL_MODULES
    for place in range(count):
        module = first + place - level * LEVEL_MODULES
        weight = 1.0 / sharers_of(ids_ref, level, module)
        grad = jnp.zeros(params_ref.shape[1:], jnp.float32)
        for other in range(path_count):
            factor = jnp.where(ids_ref[here ^ other, level] == module, weight, 0.0)
            grad = grad + factor * received[other][level]
        new_moment = beta_coef * momentum_ref[place] + grad
        new_momentum_ref[place] = new_moment
        new_params_ref[place] = params_ref[place] - outer_rate * (grad + beta_coef * new_moment)


def assemble_kernel(path_count, here_ref, *refs):
    returned, out_ref, sems = refs[:path_count], refs[path_count], refs[path_count + 1]
    copies = []
    for k in range(path_count):
        copies.append(pltpu.make_async_copy(returned[k], out_ref.at[:, here_ref[0] ^ k], sems.at[k]))
    for copy in copies:
        copy.start()
    for copy in copies:
        copy.wait()


def local(path_delta, assign, params, momentum):
    own_slab = path_delta[0]
    path_count = assign.shape[0]
    module_count, _, own_rows, width = params.shape
    shards = lax.axis_size("shard")
    entries = float(own_slab.size * shards)
    state_in = params.reshape(module_count, own_rows, width)
    moment_in = momentum.reshape(module_count, own_rows, width)
    split_slab = own_slab.reshape(LEVELS, path_count, own_rows, width)
    here = lax.axis_index("path").astype(jnp.int32).reshape(1)
    rows_shape = jax.ShapeDtypeStruct((LEVELS, own_rows, width), jnp.float32)

    squares = call(squares_kernel, jax.ShapeDtypeStruct((8, 128), jnp.float32), [vmem], vmem)(own_slab)
    tiles = exchange([squares] * shards, "shard")
    packed = call(
        lambda *refs: pack_kernel(entries, shards, *refs),
        [rows_shape] * path_count,
        [smem, vmem] + [vmem] * shards,
        [vmem] * path_count,
    )(here, split_slab, *tiles)
    received = exchange(packed, "path")
    base = call(
        gather_kernel,
        jax.ShapeDtypeStruct((LEVELS, path_count, own_rows, width), jnp.float32),
        [smem, smem, anywhere, anywhere],
        vmem,
        scratch_shapes=[
            pltpu.VMEM((LEVELS, path_count, own_rows, width), jnp.float32),
            pltpu.VMEM((LEVELS, path_count, own_rows, width), jnp.float32),
            pltpu.SemaphoreType.DMA((2, LEVELS, path_count)),
        ],
    )(here, assign, state_in, moment_in)
    outgoing = call(
        lambda *refs: outgoing_kernel(path_count, *refs),
        [rows_shape] * path_count,
        [smem, smem, vmem] + [vmem] * path_count,
        [vmem] * path_count,
    )(here, assign, base, *received)
    returned = exchange(outgoing, "path")
    block = LEVEL_MODULES // 4
    state_block = pl.BlockSpec((block, own_rows, width), lambda i: (i, 0, 0))
    new_state, new_moment = call(
        lambda *refs: state_kernel(path_count, *refs),
        [jax.ShapeDtypeStruct(state_in.shape, jnp.float32)] * 2,
        [smem, smem] + [vmem] * path_count + [state_block, state_block],
        [state_block, state_block],
        grid=(module_count // block,),
    )(here, assign, *received, state_in, moment_in)
    path_params = call(
        lambda *refs: assemble_kernel(path_count, *refs),
        jax.ShapeDtypeStruct(split_slab.shape, jnp.float32),
        [smem] + [anywhere] * path_count,
        anywhere,
        scratch_shapes=[pltpu.SemaphoreType.DMA((path_count,))],
    )(here, *returned)
    return (path_params.reshape(path_delta.shape), new_state[:, None], new_moment[:, None])


def solution(mesh):
    in_specs = (
        P("path", None, "shard", None),
        P(),
        P(None, "shard", "path", None),
        P(None, "shard", "path", None),
    )
    out_specs = (
        P("path", None, "shard", None),
        P(None, "shard", "path", None),
        P(None, "shard", "path", None),
    )
    return jax.shard_map(local, mesh=mesh, in_specs=in_specs, out_specs=out_specs, check_vma=False)
```

```python
import jax
import jax.numpy as jnp
from jax import lax
from jax.experimental import pallas as pl
from jax.experimental.pallas import tpu as pltpu
from jax.sharding import PartitionSpec as P

LEVEL_MODULES = 16
LEVELS = 2

outer_rate = 0.7
beta_coef = 0.9
moment_coef = outer_rate * beta_coef * beta_coef
grad_coef = outer_rate * (1.0 + beta_coef)

VMEM_LIMIT = 48 * 1024 * 1024

vmem = pl.BlockSpec(memory_space=pltpu.VMEM)
smem = pl.BlockSpec(memory_space=pltpu.SMEM)
anywhere = pl.BlockSpec(memory_space=pl.ANY)
hbm = pl.BlockSpec(memory_space=pltpu.HBM)


def call(kernel, out_shape, in_specs, out_specs, **more):
    return pl.pallas_call(
        kernel,
        out_shape=out_shape,
        in_specs=in_specs,
        out_specs=out_specs,
        compiler_params=pltpu.CompilerParams(vmem_limit_bytes=VMEM_LIMIT),
        **more,
    )


def exchange(arrays, axis):
    size = lax.axis_size(axis)
    moved = dict(enumerate(arrays))
    for k in sorted(range(1, size), key=lambda k: (-bin(k // 2).count("1"), k)):
        moved[k] = lax.ppermute(arrays[k], axis, [(i, i ^ k) for i in range(size)])
    return [moved[k] for k in range(size)]


def pack_kernel(here_ref, delta_ref, *refs):
    outs, sems = refs[:-1], refs[-1]
    copies = []
    for k, out in enumerate(outs):
        copies.append(pltpu.make_async_copy(delta_ref.at[:, here_ref[0] ^ k], out, sems.at[k]))
    for copy in copies:
        copy.start()
    for copy in copies:
        copy.wait()


def squares_kernel(*refs):
    out_ref = refs[-1]
    total = jnp.zeros((8, 128), jnp.float32)
    for ref in refs[:-1]:
        for level in range(ref.shape[0]):
            block = ref[level]
            block = block * block
            if block.shape[0] % 8:
                block = jnp.concatenate([block, jnp.zeros((8 - block.shape[0], block.shape[1]), jnp.float32)], axis=0)
            folded = block.reshape(block.shape[0] // 8, 8, block.shape[1]).sum(axis=0)
            for lane in range(0, block.shape[1], 128):
                total = total + folded[:, lane : lane + 128]
    for place in range(out_ref.shape[0]):
        out_ref[place] = total


def rescales(entries, norms_ref, here, path_count):
    shards = norms_ref.shape[0] // path_count
    result = []
    for k in range(path_count):
        first = (here ^ k) * shards
        tile = norms_ref[first]
        for shard in range(1, shards):
            tile = tile + norms_ref[first + shard]
        result.append(1.0 / jnp.sqrt(jnp.sum(tile, keepdims=True) / entries + 1e-06))
    return result


def gather_kernel(here_ref, ids_ref, params_ref, momentum_ref, out_ref, param_rows, moment_rows, sems):
    path_count = out_ref.shape[1]
    copies = []
    for level in range(LEVELS):
        for k in range(path_count):
            module = ids_ref[here_ref[0] ^ k, level] + level * LEVEL_MODULES
            copies.append(
                (
                    pltpu.make_async_copy(params_ref.at[module], param_rows.at[level, k], sems.at[0, level, k]),
                    pltpu.make_async_copy(momentum_ref.at[module], moment_rows.at[level, k], sems.at[1, level, k]),
                )
            )
    for first, second in copies:
        first.start()
        second.start()
    for level in range(LEVELS):
        for k in range(path_count):
            first, second = copies[level * path_count + k]
            first.wait()
            second.wait()
            out_ref[level, k] = param_rows[level, k] - moment_coef * moment_rows[level, k]


def sharers_of(ids_ref, level, module):
    count = 0
    for path in range(ids_ref.shape[0]):
        count = count + (ids_ref[path, level] == module).astype(jnp.int32)
    return jnp.maximum(count, 1).astype(jnp.float32)


def outgoing_kernel(path_count, entries, here_ref, ids_ref, norms_ref, base_ref, *refs):
    received, outs = refs[:path_count], refs[path_count:]
    here = here_ref[0]
    scale = rescales(entries, norms_ref, here, path_count)
    for level in range(LEVELS):
        for k in range(path_count):
            module = ids_ref[here ^ k, level]
            weight = grad_coef / sharers_of(ids_ref, level, module)
            total = base_ref[level, k]
            for other in range(path_count):
                factor = jnp.where(ids_ref[here ^ other, level] == module, weight, 0.0)
                total = total - (scale[other] * factor) * received[other][level]
            outs[k][level] = total


def state_kernel(path_count, entries, here_ref, ids_ref, norms_ref, *refs):
    received = refs[:path_count]
    params_ref, momentum_ref, new_params_ref, new_momentum_ref = refs[path_count:]
    here = here_ref[0]
    scale = rescales(entries, norms_ref, here, path_count)
    count = params_ref.shape[0]
    first = pl.program_id(0) * count
    level = first // LEVEL_MODULES
    for place in range(count):
        module = first + place - level * LEVEL_MODULES
        weight = 1.0 / sharers_of(ids_ref, level, module)
        grad = jnp.zeros(params_ref.shape[1:], jnp.float32)
        for other in range(path_count):
            factor = jnp.where(ids_ref[here ^ other, level] == module, weight, 0.0)
            grad = grad + (scale[other] * factor) * received[other][level]
        new_moment = beta_coef * momentum_ref[place] + grad
        new_momentum_ref[place] = new_moment
        new_params_ref[place] = params_ref[place] - outer_rate * (grad + beta_coef * new_moment)


def assemble_kernel(path_count, here_ref, *refs):
    returned, out_ref, sems = refs[:path_count], refs[path_count], refs[path_count + 1]
    copies = []
    for k in range(path_count):
        copies.append(pltpu.make_async_copy(returned[k], out_ref.at[:, here_ref[0] ^ k], sems.at[k]))
    for copy in copies:
        copy.start()
    for copy in copies:
        copy.wait()


def local(path_delta, assign, params, momentum):
    own_slab = path_delta[0]
    path_count = assign.shape[0]
    module_count, _, own_rows, width = params.shape
    shards = lax.axis_size("shard")
    entries = float(own_slab.size * shards)
    state_in = params.reshape(module_count, own_rows, width)
    moment_in = momentum.reshape(module_count, own_rows, width)
    split_slab = own_slab.reshape(LEVELS, path_count, own_rows, width)
    here = lax.axis_index("path").astype(jnp.int32).reshape(1)
    rows_shape = jax.ShapeDtypeStruct((LEVELS, own_rows, width), jnp.float32)

    packed = call(
        pack_kernel,
        [rows_shape] * path_count,
        [smem, hbm],
        [vmem] * path_count,
        scratch_shapes=[pltpu.SemaphoreType.DMA((path_count,))],
    )(here, split_slab)
    received = exchange(packed, "path")
    squares = call(
        squares_kernel,
        jax.ShapeDtypeStruct((path_count * shards, 8, 128), jnp.float32),
        [vmem] * path_count,
        vmem,
    )(*packed)
    norms = lax.all_to_all(squares, ("path", "shard"), split_axis=0, concat_axis=0, tiled=True)
    base = call(
        gather_kernel,
        jax.ShapeDtypeStruct((LEVELS, path_count, own_rows, width), jnp.float32),
        [smem, smem, hbm, hbm],
        vmem,
        scratch_shapes=[
            pltpu.VMEM((LEVELS, path_count, own_rows, width), jnp.float32),
            pltpu.VMEM((LEVELS, path_count, own_rows, width), jnp.float32),
            pltpu.SemaphoreType.DMA((2, LEVELS, path_count)),
        ],
    )(here, assign, state_in, moment_in)
    outgoing = call(
        lambda *refs: outgoing_kernel(path_count, entries, *refs),
        [rows_shape] * path_count,
        [smem, smem, vmem, vmem] + [vmem] * path_count,
        [vmem] * path_count,
    )(here, assign, norms, base, *received)
    returned = exchange(outgoing, "path")
    block = LEVEL_MODULES // 4
    state_block = pl.BlockSpec((block, own_rows, width), lambda i: (i, 0, 0))
    new_state, new_moment = call(
        lambda *refs: state_kernel(path_count, entries, *refs),
        [jax.ShapeDtypeStruct(state_in.shape, jnp.float32)] * 2,
        [smem, smem, vmem] + [vmem] * path_count + [state_block, state_block],
        [state_block, state_block],
        grid=(module_count // block,),
    )(here, assign, norms, *received, state_in, moment_in)
    path_params = call(
        lambda *refs: assemble_kernel(path_count, *refs),
        jax.ShapeDtypeStruct(split_slab.shape, jnp.float32),
        [smem] + [anywhere] * path_count,
        anywhere,
        scratch_shapes=[pltpu.SemaphoreType.DMA((path_count,))],
    )(here, *returned)
    return (path_params.reshape(path_delta.shape), new_state[:, None], new_moment[:, None])


def solution(mesh):
    in_specs = (
        P("path", None, "shard", None),
        P(),
        P(None, "shard", "path", None),
        P(None, "shard", "path", None),
    )
    out_specs = (
        P("path", None, "shard", None),
        P(None, "shard", "path", None),
        P(None, "shard", "path", None),
    )
    return jax.shard_map(local, mesh=mesh, in_specs=in_specs, out_specs=out_specs, check_vma=False)
```

```python
import jax
import jax.numpy as jnp
from jax import lax
from jax.experimental import pallas as pl
from jax.experimental.pallas import tpu as pltpu
from jax.sharding import PartitionSpec as P

LEVEL_MODULES = 16
LEVELS = 2
MOST_UNROLLED = 16

outer_rate = 0.7
beta_coef = 0.9
moment_coef = outer_rate * beta_coef * beta_coef
grad_coef = outer_rate * (1.0 + beta_coef)

VMEM_LIMIT = 16 * 1024 * 1024

vmem = pl.BlockSpec(memory_space=pltpu.VMEM)
smem = pl.BlockSpec(memory_space=pltpu.SMEM)
anywhere = pl.BlockSpec(memory_space=pl.ANY)


def call(kernel, out_shape, in_specs, out_specs, **more):
    return pl.pallas_call(
        kernel,
        out_shape=out_shape,
        in_specs=in_specs,
        out_specs=out_specs,
        compiler_params=pltpu.CompilerParams(vmem_limit_bytes=VMEM_LIMIT),
        **more,
    )


def mirrored(k, size):
    if size < 8:
        return k
    return (k & ~6) | ((k & 2) << 1) | ((k & 4) >> 1)


def target(here, k, size):
    if isinstance(here, int):
        return here ^ (mirrored(k, size) if here & 1 else k)
    return here ^ jnp.where(here & 1 == 1, mirrored(k, size), k)


def origin(here, k, size):
    if isinstance(here, int):
        return here ^ (mirrored(k, size) if (here ^ k) & 1 else k)
    return here ^ jnp.where((here ^ k) & 1 == 1, mirrored(k, size), k)


def exchange(arrays):
    size = len(arrays)
    moved = dict(enumerate(arrays))
    first = [1, 6, 7, 2, 4, 3, 5] if size == 8 else list(range(1, size))
    for k in first:
        moved[k] = lax.ppermute(arrays[k], "path", [(i, target(i, k, size)) for i in range(size)])
    return [moved[k] for k in range(size)]


def squares_kernel(delta_ref, out_ref):
    total = jnp.zeros(out_ref.shape, jnp.float32)
    for level in range(delta_ref.shape[0]):
        block = delta_ref[level]
        block = block * block
        folded = block.reshape(block.shape[0] // 8, 8, block.shape[1]).sum(axis=0)
        for lane in range(0, block.shape[1], 128):
            total = total + folded[:, lane : lane + 128]
    out_ref[...] = total


def pack_kernel(entries, shards, here_ref, delta_ref, *refs):
    tiles, outs = refs[:shards], refs[shards:]
    tile = tiles[0][...]
    for other in tiles[1:]:
        tile = tile + other[...]
    rescale = 1.0 / jnp.sqrt(jnp.sum(tile, keepdims=True) / entries + 1e-06)
    for k, out in enumerate(outs):
        place = target(here_ref[0], k, len(outs))
        for level in range(LEVELS):
            out[level] = delta_ref[level, place] * rescale


def gather_kernel(here_ref, ids_ref, params_ref, momentum_ref, out_ref, param_rows, moment_rows, sems):
    path_count = out_ref.shape[1]
    copies = []
    for level in range(LEVELS):
        for k in range(path_count):
            module = ids_ref[target(here_ref[0], k, path_count), level] + level * LEVEL_MODULES
            copies.append(
                (
                    pltpu.make_async_copy(params_ref.at[module], param_rows.at[level, k], sems.at[0, level, k]),
                    pltpu.make_async_copy(momentum_ref.at[module], moment_rows.at[level, k], sems.at[1, level, k]),
                )
            )
    for first, second in copies:
        first.start()
        second.start()
    for level in range(LEVELS):
        for k in range(path_count):
            first, second = copies[level * path_count + k]
            first.wait()
            second.wait()
            out_ref[level, k] = param_rows[level, k] - moment_coef * moment_rows[level, k]


def sharers_of(ids_ref, level, module):
    count = 0
    for path in range(ids_ref.shape[0]):
        count = count + (ids_ref[path, level] == module).astype(jnp.int32)
    return jnp.maximum(count, 1).astype(jnp.float32)


def outgoing_kernel(path_count, here_ref, ids_ref, base_ref, *refs):
    received, outs = refs[:path_count], refs[path_count:]
    here = here_ref[0]
    for level in range(LEVELS):
        for k in range(path_count):
            module = ids_ref[target(here, k, path_count), level]
            weight = grad_coef / sharers_of(ids_ref, level, module)
            total = base_ref[level, k]
            for other in range(path_count):
                owner = origin(here, other, path_count)
                factor = jnp.where(ids_ref[owner, level] == module, weight, 0.0)
                total = total - factor * received[other][level]
            outs[k][level] = total


def state_kernel(path_count, here_ref, ids_ref, *refs):
    received = refs[:path_count]
    params_ref, momentum_ref, new_params_ref, new_momentum_ref = refs[path_count:]
    here = here_ref[0]
    count = params_ref.shape[0]
    first = pl.program_id(0) * count
    level = first // LEVEL_MODULES
    for place in range(count):
        module = first + place - level * LEVEL_MODULES
        weight = 1.0 / sharers_of(ids_ref, level, module)
        grad = jnp.zeros(params_ref.shape[1:], jnp.float32)
        for other in range(path_count):
            owner = origin(here, other, path_count)
            factor = jnp.where(ids_ref[owner, level] == module, weight, 0.0)
            grad = grad + factor * received[other][level]
        new_moment = beta_coef * momentum_ref[place] + grad
        new_momentum_ref[place] = new_moment
        new_params_ref[place] = params_ref[place] - outer_rate * (grad + beta_coef * new_moment)


def assemble_kernel(path_count, here_ref, *refs):
    returned, out_ref, sems = refs[:path_count], refs[path_count], refs[path_count + 1]
    copies = []
    for k in range(path_count):
        place = origin(here_ref[0], k, path_count)
        copies.append(pltpu.make_async_copy(returned[k], out_ref.at[:, place], sems.at[k]))
    for copy in copies:
        copy.start()
    for copy in copies:
        copy.wait()


def local(path_delta, assign, params, momentum):
    own_slab = path_delta[0]
    path_count = assign.shape[0]
    module_count, _, own_rows, width = params.shape
    shards = lax.axis_size("shard")
    entries = float(own_slab.size * shards)
    state_in = params.reshape(module_count, own_rows, width)
    moment_in = momentum.reshape(module_count, own_rows, width)
    split_slab = own_slab.reshape(LEVELS, path_count, own_rows, width)
    here = lax.axis_index("path").astype(jnp.int32).reshape(1)
    rows_shape = jax.ShapeDtypeStruct((LEVELS, own_rows, width), jnp.float32)

    squares = call(squares_kernel, jax.ShapeDtypeStruct((8, 128), jnp.float32), [vmem], vmem)(own_slab)
    tiles = [squares] + [
        lax.ppermute(squares, "shard", [(i, (i + step) % shards) for i in range(shards)])
        for step in range(1, shards)
    ]
    packed = call(
        lambda *refs: pack_kernel(entries, shards, *refs),
        [rows_shape] * path_count,
        [smem, vmem] + [vmem] * shards,
        [vmem] * path_count,
    )(here, split_slab, *tiles)
    received = exchange(packed)
    base = call(
        gather_kernel,
        jax.ShapeDtypeStruct((LEVELS, path_count, own_rows, width), jnp.float32),
        [smem, smem, anywhere, anywhere],
        vmem,
        scratch_shapes=[
            pltpu.VMEM((LEVELS, path_count, own_rows, width), jnp.float32),
            pltpu.VMEM((LEVELS, path_count, own_rows, width), jnp.float32),
            pltpu.SemaphoreType.DMA((2, LEVELS, path_count)),
        ],
    )(here, assign, state_in, moment_in)
    outgoing = call(
        lambda *refs: outgoing_kernel(path_count, *refs),
        [rows_shape] * path_count,
        [smem, smem, vmem] + [vmem] * path_count,
        [vmem] * path_count,
    )(here, assign, base, *received)
    returned = exchange(outgoing)
    block = LEVEL_MODULES // 4
    state_block = pl.BlockSpec((block, own_rows, width), lambda i: (i, 0, 0))
    new_state, new_moment = call(
        lambda *refs: state_kernel(path_count, *refs),
        [jax.ShapeDtypeStruct(state_in.shape, jnp.float32)] * 2,
        [smem, smem] + [vmem] * path_count + [state_block, state_block],
        [state_block, state_block],
        grid=(module_count // block,),
    )(here, assign, *received, state_in, moment_in)
    path_params = call(
        lambda *refs: assemble_kernel(path_count, *refs),
        jax.ShapeDtypeStruct(split_slab.shape, jnp.float32),
        [smem] + [anywhere] * path_count,
        anywhere,
        scratch_shapes=[pltpu.SemaphoreType.DMA((path_count,))],
    )(here, *returned)
    return (path_params.reshape(path_delta.shape), new_state[:, None], new_moment[:, None])


def local_wide(path_delta, assign, params, momentum):
    own_slab = path_delta[0]
    path_count = assign.shape[0]
    module_count, _, own_rows, width = params.shape
    entries = float(own_slab.size * lax.axis_size("shard"))
    total_sq = lax.psum(jnp.sum(own_slab * own_slab), "shard")
    scaled = own_slab * (1.0 / jnp.sqrt(total_sq / entries + 1e-06))
    received = lax.all_to_all(
        scaled.reshape(LEVELS, path_count, own_rows, width), "path", split_axis=1, concat_axis=1, tiled=True
    )
    flat_ids = (assign + LEVEL_MODULES * jnp.arange(LEVELS, dtype=jnp.int32)[None, :]).T.reshape(-1)
    member = (jnp.arange(module_count, dtype=jnp.int32)[:, None] == flat_ids[None, :]).astype(jnp.float32)
    mean = member / jnp.maximum(jnp.sum(member, axis=1), 1.0)[:, None]
    grad = jnp.einsum(
        "mp,prd->mrd", mean, received.reshape(-1, own_rows, width), precision=lax.Precision.HIGHEST
    )
    new_moment = beta_coef * momentum[:, 0] + grad
    new_state = params[:, 0] - outer_rate * (grad + beta_coef * new_moment)
    outgoing = jnp.take(new_state, flat_ids, axis=0).reshape(LEVELS, path_count, own_rows, width)
    returned = lax.all_to_all(outgoing, "path", split_axis=1, concat_axis=1, tiled=True)
    return (returned.reshape(path_delta.shape), new_state[:, None], new_moment[:, None])


def solution(mesh):
    in_specs = (
        P("path", None, "shard", None),
        P(),
        P(None, "shard", "path", None),
        P(None, "shard", "path", None),
    )
    out_specs = (
        P("path", None, "shard", None),
        P(None, "shard", "path", None),
        P(None, "shard", "path", None),
    )
    chosen = local if mesh.shape["path"] <= MOST_UNROLLED else local_wide
    return jax.shard_map(chosen, mesh=mesh, in_specs=in_specs, out_specs=out_specs, check_vma=False)
```

```python
import jax
import jax.numpy as jnp
from jax import lax
from jax.experimental import pallas as pl
from jax.experimental.pallas import tpu as pltpu
from jax.sharding import PartitionSpec as P

LEVEL_MODULES = 16
LEVELS = 2
MOST_UNROLLED = 16

outer_rate = 0.7
beta_coef = 0.9
moment_coef = outer_rate * beta_coef * beta_coef
grad_coef = outer_rate * (1.0 + beta_coef)

VMEM_LIMIT = 16 * 1024 * 1024

vmem = pl.BlockSpec(memory_space=pltpu.VMEM)
smem = pl.BlockSpec(memory_space=pltpu.SMEM)
anywhere = pl.BlockSpec(memory_space=pl.ANY)


def call(kernel, out_shape, in_specs, out_specs, **more):
    return pl.pallas_call(
        kernel,
        out_shape=out_shape,
        in_specs=in_specs,
        out_specs=out_specs,
        compiler_params=pltpu.CompilerParams(vmem_limit_bytes=VMEM_LIMIT),
        **more,
    )


def mirrored(k, size):
    if size < 8:
        return k
    return (k & ~6) | ((k & 2) << 1) | ((k & 4) >> 1)


def target(here, k, size):
    if isinstance(here, int):
        return here ^ (mirrored(k, size) if here & 1 else k)
    return here ^ jnp.where(here & 1 == 1, mirrored(k, size), k)


def origin(here, k, size):
    if isinstance(here, int):
        return here ^ (mirrored(k, size) if (here ^ k) & 1 else k)
    return here ^ jnp.where((here ^ k) & 1 == 1, mirrored(k, size), k)


def order_of(size):
    return [6, 7, 2, 4, 1, 3, 5, 0] if size == 8 else [*range(1, size), 0]


def exchange(arrays):
    size = len(arrays)
    moved = dict(enumerate(arrays))
    for k in order_of(size)[:-1]:
        moved[k] = lax.ppermute(arrays[k], "path", [(i, target(i, k, size)) for i in range(size)])
    return [moved[k] for k in range(size)]


def squares_kernel(delta_ref, out_ref):
    total = jnp.zeros(out_ref.shape, jnp.float32)
    for level in range(delta_ref.shape[0]):
        block = delta_ref[level]
        block = block * block
        folded = block.reshape(block.shape[0] // 8, 8, block.shape[1]).sum(axis=0)
        for lane in range(0, block.shape[1], 128):
            total = total + folded[:, lane : lane + 128]
    out_ref[...] = total


def pack_kernel(here_ref, delta_ref, *outs):
    for k, out in enumerate(outs):
        place = target(here_ref[0], k, len(outs))
        for level in range(LEVELS):
            out[level] = delta_ref[level, place]


def scale_kernel(entries, shards, *refs):
    tiles, refs = refs[:shards], refs[shards:]
    tile = tiles[0][...]
    for other in tiles[1:]:
        tile = tile + other[...]
    rescale = 1.0 / jnp.sqrt(jnp.sum(tile, keepdims=True) / entries + 1e-06)
    count = len(refs) // 2
    for block, out in zip(refs[:count], refs[count:]):
        out[...] = block[...] * rescale


def gather_kernel(here_ref, ids_ref, params_ref, momentum_ref, out_ref, param_rows, moment_rows, sems):
    path_count = out_ref.shape[1]
    copies = []
    for level in range(LEVELS):
        for k in range(path_count):
            module = ids_ref[target(here_ref[0], k, path_count), level] + level * LEVEL_MODULES
            copies.append(
                (
                    pltpu.make_async_copy(params_ref.at[module], param_rows.at[level, k], sems.at[0, level, k]),
                    pltpu.make_async_copy(momentum_ref.at[module], moment_rows.at[level, k], sems.at[1, level, k]),
                )
            )
    for first, second in copies:
        first.start()
        second.start()
    for level in range(LEVELS):
        for k in range(path_count):
            first, second = copies[level * path_count + k]
            first.wait()
            second.wait()
            out_ref[level, k] = param_rows[level, k] - moment_coef * moment_rows[level, k]


def sharers_of(ids_ref, level, module):
    count = 0
    for path in range(ids_ref.shape[0]):
        count = count + (ids_ref[path, level] == module).astype(jnp.int32)
    return jnp.maximum(count, 1).astype(jnp.float32)


def outgoing_kernel(path_count, rounds, here_ref, ids_ref, base_ref, *refs):
    received, outs = refs[:path_count], refs[path_count:]
    here = here_ref[0]
    for level in range(LEVELS):
        for k, out in zip(rounds, outs):
            module = ids_ref[target(here, k, path_count), level]
            weight = grad_coef / sharers_of(ids_ref, level, module)
            total = base_ref[level, k]
            for other in range(path_count):
                owner = origin(here, other, path_count)
                factor = jnp.where(ids_ref[owner, level] == module, weight, 0.0)
                total = total - factor * received[other][level]
            out[level] = total


def state_kernel(path_count, here_ref, ids_ref, *refs):
    received = refs[:path_count]
    params_ref, momentum_ref, new_params_ref, new_momentum_ref = refs[path_count:]
    here = here_ref[0]
    count = params_ref.shape[0]
    first = pl.program_id(0) * count
    level = first // LEVEL_MODULES
    for place in range(count):
        module = first + place - level * LEVEL_MODULES
        weight = 1.0 / sharers_of(ids_ref, level, module)
        grad = jnp.zeros(params_ref.shape[1:], jnp.float32)
        for other in range(path_count):
            owner = origin(here, other, path_count)
            factor = jnp.where(ids_ref[owner, level] == module, weight, 0.0)
            grad = grad + factor * received[other][level]
        new_moment = beta_coef * momentum_ref[place] + grad
        new_momentum_ref[place] = new_moment
        new_params_ref[place] = params_ref[place] - outer_rate * (grad + beta_coef * new_moment)


def assemble_kernel(path_count, here_ref, *refs):
    returned, out_ref, sems = refs[:path_count], refs[path_count], refs[path_count + 1]
    copies = []
    for k in range(path_count):
        place = origin(here_ref[0], k, path_count)
        copies.append(pltpu.make_async_copy(returned[k], out_ref.at[:, place], sems.at[k]))
    for copy in copies:
        copy.start()
    for copy in copies:
        copy.wait()


def local(path_delta, assign, params, momentum):
    own_slab = path_delta[0]
    path_count = assign.shape[0]
    module_count, _, own_rows, width = params.shape
    shards = lax.axis_size("shard")
    entries = float(own_slab.size * shards)
    state_in = params.reshape(module_count, own_rows, width)
    moment_in = momentum.reshape(module_count, own_rows, width)
    split_slab = own_slab.reshape(LEVELS, path_count, own_rows, width)
    here = lax.axis_index("path").astype(jnp.int32).reshape(1)
    rows_shape = jax.ShapeDtypeStruct((LEVELS, own_rows, width), jnp.float32)

    squares = call(squares_kernel, jax.ShapeDtypeStruct((8, 128), jnp.float32), [vmem], vmem)(own_slab)
    tiles = [squares] + [
        lax.ppermute(squares, "shard", [(i, (i + step) % shards) for i in range(shards)])
        for step in range(1, shards)
    ]
    raw = call(
        pack_kernel, [rows_shape] * path_count, [smem, vmem], [vmem] * path_count
    )(here, split_slab)
    packed = call(
        lambda *refs: scale_kernel(entries, shards, *refs),
        [rows_shape] * path_count,
        [vmem] * (shards + path_count),
        [vmem] * path_count,
    )(*tiles, *raw)
    received = exchange(packed)
    base = call(
        gather_kernel,
        jax.ShapeDtypeStruct((LEVELS, path_count, own_rows, width), jnp.float32),
        [smem, smem, anywhere, anywhere],
        vmem,
        scratch_shapes=[
            pltpu.VMEM((LEVELS, path_count, own_rows, width), jnp.float32),
            pltpu.VMEM((LEVELS, path_count, own_rows, width), jnp.float32),
            pltpu.SemaphoreType.DMA((2, LEVELS, path_count)),
        ],
    )(here, assign, state_in, moment_in)
    outgoing = {}
    order = order_of(path_count)
    half = path_count // 2
    for rounds in (order[:half], order[half:]):
        outs = call(
            lambda *refs, rounds=rounds: outgoing_kernel(path_count, rounds, *refs),
            [rows_shape] * len(rounds),
            [smem, smem, vmem] + [vmem] * path_count,
            [vmem] * len(rounds),
        )(here, assign, base, *received)
        outgoing.update(zip(rounds, outs))
    outgoing = [outgoing[k] for k in range(path_count)]
    returned = exchange(outgoing)
    block = LEVEL_MODULES // 4
    state_block = pl.BlockSpec((block, own_rows, width), lambda i: (i, 0, 0))
    new_state, new_moment = call(
        lambda *refs: state_kernel(path_count, *refs),
        [jax.ShapeDtypeStruct(state_in.shape, jnp.float32)] * 2,
        [smem, smem] + [vmem] * path_count + [state_block, state_block],
        [state_block, state_block],
        grid=(module_count // block,),
    )(here, assign, *received, state_in, moment_in)
    path_params = call(
        lambda *refs: assemble_kernel(path_count, *refs),
        jax.ShapeDtypeStruct(split_slab.shape, jnp.float32),
        [smem] + [anywhere] * path_count,
        anywhere,
        scratch_shapes=[pltpu.SemaphoreType.DMA((path_count,))],
    )(here, *returned)
    return (path_params.reshape(path_delta.shape), new_state[:, None], new_moment[:, None])


def local_wide(path_delta, assign, params, momentum):
    own_slab = path_delta[0]
    path_count = assign.shape[0]
    module_count, _, own_rows, width = params.shape
    entries = float(own_slab.size * lax.axis_size("shard"))
    total_sq = lax.psum(jnp.sum(own_slab * own_slab), "shard")
    scaled = own_slab * (1.0 / jnp.sqrt(total_sq / entries + 1e-06))
    received = lax.all_to_all(
        scaled.reshape(LEVELS, path_count, own_rows, width), "path", split_axis=1, concat_axis=1, tiled=True
    )
    flat_ids = (assign + LEVEL_MODULES * jnp.arange(LEVELS, dtype=jnp.int32)[None, :]).T.reshape(-1)
    member = (jnp.arange(module_count, dtype=jnp.int32)[:, None] == flat_ids[None, :]).astype(jnp.float32)
    mean = member / jnp.maximum(jnp.sum(member, axis=1), 1.0)[:, None]
    grad = jnp.einsum(
        "mp,prd->mrd", mean, received.reshape(-1, own_rows, width), precision=lax.Precision.HIGHEST
    )
    new_moment = beta_coef * momentum[:, 0] + grad
    new_state = params[:, 0] - outer_rate * (grad + beta_coef * new_moment)
    outgoing = jnp.take(new_state, flat_ids, axis=0).reshape(LEVELS, path_count, own_rows, width)
    returned = lax.all_to_all(outgoing, "path", split_axis=1, concat_axis=1, tiled=True)
    return (returned.reshape(path_delta.shape), new_state[:, None], new_moment[:, None])


def solution(mesh):
    in_specs = (
        P("path", None, "shard", None),
        P(),
        P(None, "shard", "path", None),
        P(None, "shard", "path", None),
    )
    out_specs = (
        P("path", None, "shard", None),
        P(None, "shard", "path", None),
        P(None, "shard", "path", None),
    )
    chosen = local if mesh.shape["path"] <= MOST_UNROLLED else local_wide
    return jax.shard_map(chosen, mesh=mesh, in_specs=in_specs, out_specs=out_specs, check_vma=False)
```

```python
import jax
import jax.numpy as jnp
from jax import lax
from jax.experimental import pallas as pl
from jax.experimental.pallas import tpu as pltpu
from jax.sharding import PartitionSpec as P

LEVEL_MODULES = 16
LEVELS = 2
MOST_UNROLLED = 16

outer_rate = 0.7
beta_coef = 0.9
moment_coef = outer_rate * beta_coef * beta_coef
grad_coef = outer_rate * (1.0 + beta_coef)

VMEM_LIMIT = 16 * 1024 * 1024

vmem = pl.BlockSpec(memory_space=pltpu.VMEM)
smem = pl.BlockSpec(memory_space=pltpu.SMEM)
anywhere = pl.BlockSpec(memory_space=pl.ANY)


def call(kernel, out_shape, in_specs, out_specs, **more):
    return pl.pallas_call(
        kernel,
        out_shape=out_shape,
        in_specs=in_specs,
        out_specs=out_specs,
        compiler_params=pltpu.CompilerParams(vmem_limit_bytes=VMEM_LIMIT),
        **more,
    )


def mirrored(k, size):
    if size < 8:
        return k
    return (k & ~6) | ((k & 2) << 1) | ((k & 4) >> 1)


def target(here, k, size):
    if isinstance(here, int):
        return here ^ (mirrored(k, size) if here & 1 else k)
    return here ^ jnp.where(here & 1 == 1, mirrored(k, size), k)


def origin(here, k, size):
    if isinstance(here, int):
        return here ^ (mirrored(k, size) if (here ^ k) & 1 else k)
    return here ^ jnp.where((here ^ k) & 1 == 1, mirrored(k, size), k)


def order_of(size):
    return [6, 7, 2, 4, 1, 3, 5, 0] if size == 8 else [*range(1, size), 0]


def exchange(arrays):
    size = len(arrays)
    return [
        lax.ppermute(array, "path", [(i, target(i, k, size)) for i in range(size)]) if k else array
        for k, array in zip(order_of(size), arrays)
    ]


def squares_kernel(delta_ref, out_ref):
    total = jnp.zeros(out_ref.shape, jnp.float32)
    for level in range(delta_ref.shape[0]):
        block = delta_ref[level]
        block = block * block
        folded = block.reshape(block.shape[0] // 8, 8, block.shape[1]).sum(axis=0)
        for lane in range(0, block.shape[1], 128):
            total = total + folded[:, lane : lane + 128]
    out_ref[...] = total


def pack_kernel(here_ref, delta_ref, *outs):
    for k, out in zip(order_of(len(outs)), outs):
        place = target(here_ref[0], k, len(outs))
        for level in range(LEVELS):
            out[level] = delta_ref[level, place]


def scale_kernel(entries, shards, *refs):
    tiles, refs = refs[:shards], refs[shards:]
    tile = tiles[0][...]
    for other in tiles[1:]:
        tile = tile + other[...]
    total = jnp.broadcast_to(jnp.sum(tile, keepdims=True), (8, 128))
    rescale = 1.0 / jnp.sqrt(total / entries + 1e-06)
    count = len(refs) // 2
    for block, out in zip(refs[:count], refs[count:]):
        levels, rows, width = block.shape
        for level in range(levels):
            for row in range(0, rows, 8):
                for lane in range(0, width, 128):
                    here = (level, slice(row, row + 8), slice(lane, lane + 128))
                    out[here] = block[here] * rescale


def weights_kernel(here_ref, ids_ref, chosen_ref, outgoing_ref, state_ref):
    size = ids_ref.shape[0]
    order = order_of(size)
    here = here_ref[0]
    for level in range(LEVELS):
        ids = [ids_ref[origin(here, k, size), level] for k in order]
        for local_module in range(LEVEL_MODULES):
            count = jnp.int32(0)
            for i in range(size):
                count = count + jnp.where(ids[i] == local_module, 1, 0)
            share = 1.0 / jnp.maximum(count, 1).astype(jnp.float32)
            for i in range(size):
                state_ref[level * LEVEL_MODULES + local_module, i] = jnp.where(ids[i] == local_module, share, 0.0)
        for j, k in enumerate(order):
            module = ids_ref[target(here, k, size), level] + level * LEVEL_MODULES
            chosen_ref[level, j] = module
            for i in range(size):
                outgoing_ref[level * size + j, i] = grad_coef * state_ref[module, i]


def base_kernel(chosen_ref, params_ref, momentum_ref, out_ref):
    for level in range(out_ref.shape[0]):
        for j in range(out_ref.shape[1]):
            module = chosen_ref[level, j]
            out_ref[level, j] = params_ref[module] - moment_coef * momentum_ref[module]


def outgoing_kernel(size, weight_ref, base_ref, *refs):
    received, outs = refs[:size], refs[size:]
    for level in range(LEVELS):
        for j, out in enumerate(outs):
            total = base_ref[level, j]
            for i in range(size):
                total = total - weight_ref[level * size + j, i] * received[i][level]
            out[level] = total


def state_kernel(size, weight_ref, *refs):
    received = refs[:size]
    params_ref, momentum_ref, new_params_ref, new_momentum_ref = refs[size:]
    count = new_params_ref.shape[0]
    first = pl.program_id(0) * count
    level = first // LEVEL_MODULES
    for place in range(count):
        module = first + place
        grad = weight_ref[module, 0] * received[0][level]
        for i in range(1, size):
            grad = grad + weight_ref[module, i] * received[i][level]
        new_moment = beta_coef * momentum_ref[module] + grad
        new_momentum_ref[place] = new_moment
        new_params_ref[place] = params_ref[module] - outer_rate * (grad + beta_coef * new_moment)


def assemble_kernel(size, here_ref, *refs):
    returned, out_ref, sems = refs[:size], refs[size], refs[size + 1]
    copies = []
    for j, k in enumerate(order_of(size)):
        place = origin(here_ref[0], k, size)
        copies.append(pltpu.make_async_copy(returned[j], out_ref.at[:, place], sems.at[j]))
    for copy in copies:
        copy.start()
    for copy in copies:
        copy.wait()


def local(path_delta, assign, params, momentum):
    own_slab = path_delta[0]
    path_count = assign.shape[0]
    module_count, _, own_rows, width = params.shape
    shards = lax.axis_size("shard")
    entries = float(own_slab.size * shards)
    state_in = params.reshape(module_count, own_rows, width)
    moment_in = momentum.reshape(module_count, own_rows, width)
    split_slab = own_slab.reshape(LEVELS, path_count, own_rows, width)
    here = lax.axis_index("path").astype(jnp.int32).reshape(1)
    rows_shape = jax.ShapeDtypeStruct((LEVELS, own_rows, width), jnp.float32)

    squares = call(squares_kernel, jax.ShapeDtypeStruct((8, 128), jnp.float32), [vmem], vmem)(own_slab)
    tiles = [squares] + [
        lax.ppermute(squares, "shard", [(i, (i + step) % shards) for i in range(shards)])
        for step in range(1, shards)
    ]
    raw = call(
        pack_kernel, [rows_shape] * path_count, [smem, vmem], [vmem] * path_count
    )(here, split_slab)
    packed = call(
        lambda *refs: scale_kernel(entries, shards, *refs),
        [rows_shape] * path_count,
        [vmem] * (shards + path_count),
        [vmem] * path_count,
    )(*tiles, *raw)
    received = exchange(packed)
    chosen, outgoing_weight, state_weight = call(
        weights_kernel,
        [
            jax.ShapeDtypeStruct((LEVELS, path_count), jnp.int32),
            jax.ShapeDtypeStruct((LEVELS * path_count, path_count), jnp.float32),
            jax.ShapeDtypeStruct((module_count, path_count), jnp.float32),
        ],
        [smem, smem],
        [smem, smem, smem],
    )(here, assign)
    base = call(
        base_kernel,
        jax.ShapeDtypeStruct((LEVELS, path_count, own_rows, width), jnp.float32),
        [smem, vmem, vmem],
        vmem,
    )(chosen, state_in, moment_in)
    outgoing = call(
        lambda *refs: outgoing_kernel(path_count, *refs),
        [rows_shape] * path_count,
        [smem, vmem] + [vmem] * path_count,
        [vmem] * path_count,
    )(outgoing_weight, base, *received)
    returned = exchange(outgoing)
    block = LEVEL_MODULES // 4
    state_block = pl.BlockSpec((block, own_rows, width), lambda i: (i, 0, 0))
    new_state, new_moment = call(
        lambda *refs: state_kernel(path_count, *refs),
        [jax.ShapeDtypeStruct(state_in.shape, jnp.float32)] * 2,
        [smem] + [vmem] * (path_count + 2),
        [state_block, state_block],
        grid=(module_count // block,),
    )(state_weight, *received, state_in, moment_in)
    path_params = call(
        lambda *refs: assemble_kernel(path_count, *refs),
        jax.ShapeDtypeStruct(split_slab.shape, jnp.float32),
        [smem] + [anywhere] * path_count,
        anywhere,
        scratch_shapes=[pltpu.SemaphoreType.DMA((path_count,))],
    )(here, *returned)
    return (path_params.reshape(path_delta.shape), new_state[:, None], new_moment[:, None])


def local_wide(path_delta, assign, params, momentum):
    own_slab = path_delta[0]
    path_count = assign.shape[0]
    module_count, _, own_rows, width = params.shape
    entries = float(own_slab.size * lax.axis_size("shard"))
    total_sq = lax.psum(jnp.sum(own_slab * own_slab), "shard")
    scaled = own_slab * (1.0 / jnp.sqrt(total_sq / entries + 1e-06))
    received = lax.all_to_all(
        scaled.reshape(LEVELS, path_count, own_rows, width), "path", split_axis=1, concat_axis=1, tiled=True
    )
    flat_ids = (assign + LEVEL_MODULES * jnp.arange(LEVELS, dtype=jnp.int32)[None, :]).T.reshape(-1)
    member = (jnp.arange(module_count, dtype=jnp.int32)[:, None] == flat_ids[None, :]).astype(jnp.float32)
    mean = member / jnp.maximum(jnp.sum(member, axis=1), 1.0)[:, None]
    grad = jnp.einsum(
        "mp,prd->mrd", mean, received.reshape(-1, own_rows, width), precision=lax.Precision.HIGHEST
    )
    new_moment = beta_coef * momentum[:, 0] + grad
    new_state = params[:, 0] - outer_rate * (grad + beta_coef * new_moment)
    outgoing = jnp.take(new_state, flat_ids, axis=0).reshape(LEVELS, path_count, own_rows, width)
    returned = lax.all_to_all(outgoing, "path", split_axis=1, concat_axis=1, tiled=True)
    return (returned.reshape(path_delta.shape), new_state[:, None], new_moment[:, None])


def solution(mesh):
    in_specs = (
        P("path", None, "shard", None),
        P(),
        P(None, "shard", "path", None),
        P(None, "shard", "path", None),
    )
    out_specs = (
        P("path", None, "shard", None),
        P(None, "shard", "path", None),
        P(None, "shard", "path", None),
    )
    chosen = local if mesh.shape["path"] <= MOST_UNROLLED else local_wide
    return jax.shard_map(chosen, mesh=mesh, in_specs=in_specs, out_specs=out_specs, check_vma=False)
```

```python
import jax
import jax.numpy as jnp
from jax import lax
from jax.experimental import pallas as pl
from jax.experimental.pallas import tpu as pltpu
from jax.sharding import PartitionSpec as P

LEVEL_MODULES = 16
LEVELS = 2
MOST_UNROLLED = 16

outer_rate = 0.7
beta_coef = 0.9
moment_coef = outer_rate * beta_coef * beta_coef
grad_coef = outer_rate * (1.0 + beta_coef)

VMEM_LIMIT = 16 * 1024 * 1024

vmem = pl.BlockSpec(memory_space=pltpu.VMEM)
smem = pl.BlockSpec(memory_space=pltpu.SMEM)
anywhere = pl.BlockSpec(memory_space=pl.ANY)


def call(kernel, out_shape, in_specs, out_specs, **more):
    return pl.pallas_call(
        kernel,
        out_shape=out_shape,
        in_specs=in_specs,
        out_specs=out_specs,
        compiler_params=pltpu.CompilerParams(vmem_limit_bytes=VMEM_LIMIT),
        **more,
    )


def mirrored(k, size):
    if size < 8:
        return k
    return (k & ~6) | ((k & 2) << 1) | ((k & 4) >> 1)


def target(here, k, size):
    if isinstance(here, int):
        return here ^ (mirrored(k, size) if here & 1 else k)
    return here ^ jnp.where(here & 1 == 1, mirrored(k, size), k)


def origin(here, k, size):
    if isinstance(here, int):
        return here ^ (mirrored(k, size) if (here ^ k) & 1 else k)
    return here ^ jnp.where((here ^ k) & 1 == 1, mirrored(k, size), k)


def order_of(size):
    return [6, 7, 2, 4, 3, 5, 1, 0] if size == 8 else [*range(1, size), 0]


def exchange(arrays):
    size = len(arrays)
    return [
        lax.ppermute(array, "path", [(i, target(i, k, size)) for i in range(size)]) if k else array
        for k, array in zip(order_of(size), arrays)
    ]


def squares_kernel(delta_ref, out_ref):
    total = jnp.zeros(out_ref.shape, jnp.float32)
    for level in range(delta_ref.shape[0]):
        block = delta_ref[level]
        block = block * block
        folded = block.reshape(block.shape[0] // 8, 8, block.shape[1]).sum(axis=0)
        for lane in range(0, block.shape[1], 128):
            total = total + folded[:, lane : lane + 128]
    out_ref[...] = total


def pack_kernel(here_ref, delta_ref, *outs):
    for k, out in zip(order_of(len(outs)), outs):
        place = target(here_ref[0], k, len(outs))
        for level in range(LEVELS):
            out[level] = delta_ref[level, place]


def scale_kernel(entries, shards, here_ref, ids_ref, *refs):
    tiles, refs = refs[:shards], refs[shards:]
    tile = tiles[0][...]
    for other in tiles[1:]:
        tile = tile + other[...]
    total = jnp.broadcast_to(jnp.sum(tile, keepdims=True), (8, 128))
    rescale = 1.0 / jnp.sqrt(total / entries + 1e-06)
    count = len(refs) // 2
    for level in range(LEVELS):
        own = ids_ref[here_ref[0], level]
        sharers = jnp.int32(0)
        for path in range(ids_ref.shape[0]):
            sharers = sharers + jnp.where(ids_ref[path, level] == own, 1, 0)
        factor = rescale / jnp.full((8, 128), sharers, jnp.int32).astype(jnp.float32)
        for block, out in zip(refs[:count], refs[count:]):
            _, rows, width = block.shape
            for row in range(0, rows, 8):
                for lane in range(0, width, 128):
                    here = (level, slice(row, row + 8), slice(lane, lane + 128))
                    out[here] = block[here] * factor


def plan_kernel(here_ref, ids_ref, chosen_ref, sender_ref, target_ref, module_ref):
    size = ids_ref.shape[0]
    order = order_of(size)
    here = here_ref[0]
    for level in range(LEVELS):
        for module in range(LEVEL_MODULES):
            module_ref[level * LEVEL_MODULES + module] = -1
        for j in reversed(range(size)):
            module_ref[ids_ref[origin(here, order[j], size), level] + level * LEVEL_MODULES] = j
        for j, k in enumerate(order):
            sender_ref[level, j] = module_ref[ids_ref[origin(here, k, size), level] + level * LEVEL_MODULES]
            module = ids_ref[target(here, k, size), level] + level * LEVEL_MODULES
            chosen_ref[level, j] = module
            target_ref[level, j] = module_ref[module]


def base_kernel(chosen_ref, params_ref, momentum_ref, out_ref):
    for level in range(out_ref.shape[0]):
        for j in range(out_ref.shape[1]):
            module = chosen_ref[level, j]
            out_ref[level, j] = params_ref[module] - moment_coef * momentum_ref[module]


def outgoing_kernel(size, sender_ref, target_ref, base_ref, *refs):
    received, outs, grad_ref = refs[:size], refs[size:-1], refs[-1]
    for level in range(LEVELS):
        for i in range(size):
            grad_ref[level, i] = received[i][level]
        for i in range(1, size):
            leader = sender_ref[level, i]

            @pl.when(leader != i)
            def _():
                grad_ref[level, leader] += received[i][level]

        for j, out in enumerate(outs):
            out[level] = base_ref[level, j] - grad_coef * grad_ref[level, target_ref[level, j]]


def state_kernel(module_ref, grad_ref, params_ref, momentum_ref, new_params_ref, new_momentum_ref):
    count = new_params_ref.shape[0]
    first = pl.program_id(0) * count
    level = first // LEVEL_MODULES
    for place in range(count):
        module = first + place
        leader = module_ref[module]
        taken = jnp.where(leader < 0, 0.0, 1.0)
        grad = taken * grad_ref[level, jnp.maximum(leader, 0)]
        new_moment = beta_coef * momentum_ref[module] + grad
        new_momentum_ref[place] = new_moment
        new_params_ref[place] = params_ref[module] - outer_rate * (grad + beta_coef * new_moment)


def assemble_kernel(size, here_ref, *refs):
    returned, out_ref, sems = refs[:size], refs[size], refs[size + 1]
    copies = []
    for j, k in enumerate(order_of(size)):
        place = origin(here_ref[0], k, size)
        copies.append(pltpu.make_async_copy(returned[j], out_ref.at[:, place], sems.at[j]))
    for copy in copies:
        copy.start()
    for copy in copies:
        copy.wait()


def local(path_delta, assign, params, momentum):
    own_slab = path_delta[0]
    path_count = assign.shape[0]
    module_count, _, own_rows, width = params.shape
    shards = lax.axis_size("shard")
    entries = float(own_slab.size * shards)
    state_in = params.reshape(module_count, own_rows, width)
    moment_in = momentum.reshape(module_count, own_rows, width)
    split_slab = own_slab.reshape(LEVELS, path_count, own_rows, width)
    here = lax.axis_index("path").astype(jnp.int32).reshape(1)
    rows_shape = jax.ShapeDtypeStruct((LEVELS, own_rows, width), jnp.float32)

    squares = call(squares_kernel, jax.ShapeDtypeStruct((8, 128), jnp.float32), [vmem], vmem)(own_slab)
    tiles = [squares] + [
        lax.ppermute(squares, "shard", [(i, (i + step) % shards) for i in range(shards)])
        for step in range(1, shards)
    ]
    raw = call(
        pack_kernel, [rows_shape] * path_count, [smem, vmem], [vmem] * path_count
    )(here, split_slab)
    packed = call(
        lambda *refs: scale_kernel(entries, shards, *refs),
        [rows_shape] * path_count,
        [smem, smem] + [vmem] * (shards + path_count),
        [vmem] * path_count,
    )(here, assign, *tiles, *raw)
    received = exchange(packed)
    by_round = jax.ShapeDtypeStruct((LEVELS, path_count), jnp.int32)
    chosen, sender, receiver, leaders = call(
        plan_kernel,
        [by_round, by_round, by_round, jax.ShapeDtypeStruct((module_count,), jnp.int32)],
        [smem, smem],
        [smem] * 4,
    )(here, assign)
    base = call(
        base_kernel,
        jax.ShapeDtypeStruct((LEVELS, path_count, own_rows, width), jnp.float32),
        [smem, vmem, vmem],
        vmem,
    )(chosen, state_in, moment_in)
    *outgoing, grad = call(
        lambda *refs: outgoing_kernel(path_count, *refs),
        [rows_shape] * path_count + [jax.ShapeDtypeStruct(base.shape, jnp.float32)],
        [smem, smem, vmem] + [vmem] * path_count,
        [vmem] * (path_count + 1),
    )(sender, receiver, base, *received)
    returned = exchange(outgoing)
    block = LEVEL_MODULES // 4
    state_block = pl.BlockSpec((block, own_rows, width), lambda i: (i, 0, 0))
    new_state, new_moment = call(
        state_kernel,
        [jax.ShapeDtypeStruct(state_in.shape, jnp.float32)] * 2,
        [smem, vmem, vmem, vmem],
        [state_block, state_block],
        grid=(module_count // block,),
    )(leaders, grad, state_in, moment_in)
    path_params = call(
        lambda *refs: assemble_kernel(path_count, *refs),
        jax.ShapeDtypeStruct(split_slab.shape, jnp.float32),
        [smem] + [anywhere] * path_count,
        anywhere,
        scratch_shapes=[pltpu.SemaphoreType.DMA((path_count,))],
    )(here, *returned)
    return (path_params.reshape(path_delta.shape), new_state[:, None], new_moment[:, None])


def local_wide(path_delta, assign, params, momentum):
    own_slab = path_delta[0]
    path_count = assign.shape[0]
    module_count, _, own_rows, width = params.shape
    entries = float(own_slab.size * lax.axis_size("shard"))
    total_sq = lax.psum(jnp.sum(own_slab * own_slab), "shard")
    scaled = own_slab * (1.0 / jnp.sqrt(total_sq / entries + 1e-06))
    received = lax.all_to_all(
        scaled.reshape(LEVELS, path_count, own_rows, width), "path", split_axis=1, concat_axis=1, tiled=True
    )
    flat_ids = (assign + LEVEL_MODULES * jnp.arange(LEVELS, dtype=jnp.int32)[None, :]).T.reshape(-1)
    member = (jnp.arange(module_count, dtype=jnp.int32)[:, None] == flat_ids[None, :]).astype(jnp.float32)
    mean = member / jnp.maximum(jnp.sum(member, axis=1), 1.0)[:, None]
    grad = jnp.einsum(
        "mp,prd->mrd", mean, received.reshape(-1, own_rows, width), precision=lax.Precision.HIGHEST
    )
    new_moment = beta_coef * momentum[:, 0] + grad
    new_state = params[:, 0] - outer_rate * (grad + beta_coef * new_moment)
    outgoing = jnp.take(new_state, flat_ids, axis=0).reshape(LEVELS, path_count, own_rows, width)
    returned = lax.all_to_all(outgoing, "path", split_axis=1, concat_axis=1, tiled=True)
    return (returned.reshape(path_delta.shape), new_state[:, None], new_moment[:, None])


def solution(mesh):
    in_specs = (
        P("path", None, "shard", None),
        P(),
        P(None, "shard", "path", None),
        P(None, "shard", "path", None),
    )
    out_specs = (
        P("path", None, "shard", None),
        P(None, "shard", "path", None),
        P(None, "shard", "path", None),
    )
    chosen = local if mesh.shape["path"] <= MOST_UNROLLED else local_wide
    return jax.shard_map(chosen, mesh=mesh, in_specs=in_specs, out_specs=out_specs, check_vma=False)
```

```python
import jax
import jax.numpy as jnp
from jax import lax
from jax.experimental import pallas as pl
from jax.experimental.pallas import tpu as pltpu
from jax.sharding import PartitionSpec as P

LEVEL_MODULES = 16
LEVELS = 2
MOST_UNROLLED = 16

outer_rate = 0.7
beta_coef = 0.9
moment_coef = outer_rate * beta_coef * beta_coef
grad_coef = outer_rate * (1.0 + beta_coef)

VMEM_LIMIT = 16 * 1024 * 1024

vmem = pl.BlockSpec(memory_space=pltpu.VMEM)
smem = pl.BlockSpec(memory_space=pltpu.SMEM)
anywhere = pl.BlockSpec(memory_space=pl.ANY)


def call(kernel, out_shape, in_specs, out_specs, **more):
    return pl.pallas_call(
        kernel,
        out_shape=out_shape,
        in_specs=in_specs,
        out_specs=out_specs,
        compiler_params=pltpu.CompilerParams(vmem_limit_bytes=VMEM_LIMIT),
        **more,
    )


def mirrored(k, size):
    if size < 8:
        return k
    return (k & ~6) | ((k & 2) << 1) | ((k & 4) >> 1)


def target(here, k, size):
    if isinstance(here, int):
        return here ^ (mirrored(k, size) if here & 1 else k)
    return here ^ jnp.where(here & 1 == 1, mirrored(k, size), k)


def origin(here, k, size):
    if isinstance(here, int):
        return here ^ (mirrored(k, size) if (here ^ k) & 1 else k)
    return here ^ jnp.where((here ^ k) & 1 == 1, mirrored(k, size), k)


def order_of(size):
    return [6, 7, 2, 4, 3, 5, 1, 0] if size == 8 else [*range(1, size), 0]


def early_of(size):
    return 2 if size == 8 else 0


def move(array, k, size):
    if k == 0:
        return array
    return lax.ppermute(array, "path", [(i, target(i, k, size)) for i in range(size)])


def pack_kernel(here_ref, delta_ref, square_ref, *outs):
    total = jnp.zeros(square_ref.shape, jnp.float32)
    for k, out in zip(order_of(len(outs)), outs):
        place = target(here_ref[0], k, len(outs))
        for level in range(LEVELS):
            block = delta_ref[level, place]
            out[level] = block
            block = block * block
            folded = block.reshape(block.shape[0] // 8, 8, block.shape[1]).sum(axis=0)
            for lane in range(0, block.shape[1], 128):
                total = total + folded[:, lane : lane + 128]
    square_ref[...] = total


def tiles_of(shape):
    rows, width = shape[-2:]
    return [(slice(row, row + 8), slice(lane, lane + 128)) for row in range(0, rows, 8) for lane in range(0, width, 128)]


def scale_kernel(entries, shards, here_ref, ids_ref, plan_ref, decayed_ref, *refs):
    del plan_ref, decayed_ref
    tiles, refs = refs[:shards], refs[shards:]
    tile = tiles[0][...]
    for other in tiles[1:]:
        tile = tile + other[...]
    total = jnp.broadcast_to(jnp.sum(tile, keepdims=True), (8, 128))
    rescale = 1.0 / jnp.sqrt(total / entries + 1e-06)
    factor_ref, refs = refs[-1], refs[:-1]
    count = len(refs) // 2
    for level in range(LEVELS):
        own = ids_ref[here_ref[0], level]
        sharers = jnp.int32(0)
        for path in range(ids_ref.shape[0]):
            sharers = sharers + jnp.where(ids_ref[path, level] == own, 1, 0)
        factor = rescale / jnp.full((8, 128), sharers, jnp.int32).astype(jnp.float32)
        factor_ref[level] = factor
        for block, out in zip(refs[:count], refs[count:]):
            for tile in tiles_of(block.shape):
                out[(level, *tile)] = block[(level, *tile)] * factor


def plan_kernel(here_ref, ids_ref, chosen_ref, sender_ref, target_ref, module_ref):
    size = ids_ref.shape[0]
    order = order_of(size)
    here = here_ref[0]
    for level in range(LEVELS):
        for module in range(LEVEL_MODULES):
            module_ref[level * LEVEL_MODULES + module] = -1
        for j in reversed(range(size)):
            module_ref[ids_ref[origin(here, order[j], size), level] + level * LEVEL_MODULES] = j
        for j, k in enumerate(order):
            sender_ref[level, j] = module_ref[ids_ref[origin(here, k, size), level] + level * LEVEL_MODULES]
            module = ids_ref[target(here, k, size), level] + level * LEVEL_MODULES
            chosen_ref[level, j] = module
            target_ref[level, j] = module_ref[module]


def outgoing_kernel(size, chosen_ref, sender_ref, target_ref, decayed_ref, *refs):
    early = early_of(size)
    factors = refs[2 * early : 3 * early]
    received = refs[: 2 * early] + refs[3 * early : early + size]
    outs, grad_ref = refs[early + size : -1], refs[-1]
    for level in range(LEVELS):
        for i in range(early):
            factor = factors[i][level]
            for tile in tiles_of(received[i].shape):
                grad_ref[(level, i, *tile)] = received[i][(level, *tile)] * factor
        for i in range(early, size):
            grad_ref[level, i] = received[i][level]
        for i in range(1, size):
            leader = sender_ref[level, i]

            @pl.when(leader != i)
            def _():
                grad_ref[level, leader] += grad_ref[level, i]

        for j, out in enumerate(outs):
            out[level] = decayed_ref[chosen_ref[level, j]] - grad_coef * grad_ref[level, target_ref[level, j]]


def state_kernel(module_ref, grad_ref, decayed_ref, momentum_ref, new_params_ref, new_momentum_ref):
    count = new_params_ref.shape[0]
    first = pl.program_id(0) * count
    level = first // LEVEL_MODULES
    for place in range(count):
        module = first + place
        leader = module_ref[module]
        taken = jnp.where(leader < 0, 0.0, 1.0)
        grad = taken * grad_ref[level, jnp.maximum(leader, 0)]
        new_momentum_ref[place] = beta_coef * momentum_ref[module] + grad
        new_params_ref[place] = decayed_ref[module] - grad_coef * grad


def assemble_kernel(size, rounds, here_ref, *refs):
    returned, out_ref, sems = refs[: len(rounds)], refs[-2], refs[-1]
    copies = []
    for j, k in enumerate(rounds):
        place = origin(here_ref[0], k, size)
        copies.append(pltpu.make_async_copy(returned[j], out_ref.at[:, place], sems.at[j]))
    for copy in copies:
        copy.start()
    for copy in copies:
        copy.wait()


def local(path_delta, assign, params, momentum):
    own_slab = path_delta[0]
    path_count = assign.shape[0]
    module_count, _, own_rows, width = params.shape
    shards = lax.axis_size("shard")
    entries = float(own_slab.size * shards)
    state_in = params.reshape(module_count, own_rows, width)
    moment_in = momentum.reshape(module_count, own_rows, width)
    split_slab = own_slab.reshape(LEVELS, path_count, own_rows, width)
    here = lax.axis_index("path").astype(jnp.int32).reshape(1)
    rows_shape = jax.ShapeDtypeStruct((LEVELS, own_rows, width), jnp.float32)

    order = order_of(path_count)
    early = early_of(path_count)
    squares, *raw = call(
        pack_kernel,
        [jax.ShapeDtypeStruct((8, 128), jnp.float32)] + [rows_shape] * path_count,
        [smem, vmem],
        [vmem] * (1 + path_count),
    )(here, split_slab)
    received = [move(raw[j], order[j], path_count) for j in range(early)]
    tiles = [squares] + [
        lax.ppermute(squares, "shard", [(i, (i + step) % shards) for i in range(shards)])
        for step in range(1, shards)
    ]
    by_round = jax.ShapeDtypeStruct((LEVELS, path_count), jnp.int32)
    chosen, sender, receiver, leaders = call(
        plan_kernel,
        [by_round, by_round, by_round, jax.ShapeDtypeStruct((module_count,), jnp.int32)],
        [smem, smem],
        [smem] * 4,
    )(here, assign)
    decayed = state_in - moment_coef * moment_in
    *scaled, factor = call(
        lambda *refs: scale_kernel(entries, shards, *refs),
        [rows_shape] * (path_count - early) + [jax.ShapeDtypeStruct((LEVELS, 8, 128), jnp.float32)],
        [smem, smem, smem, anywhere] + [vmem] * (shards + path_count - early),
        [vmem] * (path_count - early + 1),
    )(here, assign, chosen, decayed, *tiles, *raw[early:])
    received += [move(scaled[j - early], order[j], path_count) for j in range(early, path_count)]
    factors = [move(factor, order[j], path_count) for j in range(early)]
    *outgoing, grad = call(
        lambda *refs: outgoing_kernel(path_count, *refs),
        [rows_shape] * path_count + [jax.ShapeDtypeStruct((LEVELS, path_count, own_rows, width), jnp.float32)],
        [smem, smem, smem, vmem] + [vmem] * (early + path_count),
        [vmem] * (path_count + 1),
    )(chosen, sender, receiver, decayed, *received[: 2 * early], *factors, *received[2 * early :])
    returned = [move(outgoing[j], order[j], path_count) for j in range(path_count)]
    block = LEVEL_MODULES // 2
    state_block = pl.BlockSpec((block, own_rows, width), lambda i: (i, 0, 0))
    new_state, new_moment = call(
        state_kernel,
        [jax.ShapeDtypeStruct(state_in.shape, jnp.float32)] * 2,
        [smem, vmem, vmem, vmem],
        [state_block, state_block],
        grid=(module_count // block,),
    )(leaders, grad, decayed, moment_in)
    path_params = None
    last = path_count // 2
    for part in ([*range(last), path_count - 1], [*range(last, path_count - 1)]):
        rounds = [order[j] for j in part]
        held = [] if path_params is None else [path_params]
        path_params = call(
            lambda *refs, rounds=rounds: assemble_kernel(path_count, rounds, *refs),
            jax.ShapeDtypeStruct(split_slab.shape, jnp.float32),
            [smem] + [anywhere] * (len(part) + len(held)),
            anywhere,
            scratch_shapes=[pltpu.SemaphoreType.DMA((len(part),))],
            input_output_aliases={1 + len(part): 0} if held else {},
        )(here, *[returned[j] for j in part], *held)
    return (path_params.reshape(path_delta.shape), new_state[:, None], new_moment[:, None])


def local_wide(path_delta, assign, params, momentum):
    own_slab = path_delta[0]
    path_count = assign.shape[0]
    module_count, _, own_rows, width = params.shape
    entries = float(own_slab.size * lax.axis_size("shard"))
    total_sq = lax.psum(jnp.sum(own_slab * own_slab), "shard")
    scaled = own_slab * (1.0 / jnp.sqrt(total_sq / entries + 1e-06))
    received = lax.all_to_all(
        scaled.reshape(LEVELS, path_count, own_rows, width), "path", split_axis=1, concat_axis=1, tiled=True
    )
    flat_ids = (assign + LEVEL_MODULES * jnp.arange(LEVELS, dtype=jnp.int32)[None, :]).T.reshape(-1)
    member = (jnp.arange(module_count, dtype=jnp.int32)[:, None] == flat_ids[None, :]).astype(jnp.float32)
    mean = member / jnp.maximum(jnp.sum(member, axis=1), 1.0)[:, None]
    grad = jnp.einsum(
        "mp,prd->mrd", mean, received.reshape(-1, own_rows, width), precision=lax.Precision.HIGHEST
    )
    new_moment = beta_coef * momentum[:, 0] + grad
    new_state = params[:, 0] - outer_rate * (grad + beta_coef * new_moment)
    outgoing = jnp.take(new_state, flat_ids, axis=0).reshape(LEVELS, path_count, own_rows, width)
    returned = lax.all_to_all(outgoing, "path", split_axis=1, concat_axis=1, tiled=True)
    return (returned.reshape(path_delta.shape), new_state[:, None], new_moment[:, None])


def solution(mesh):
    in_specs = (
        P("path", None, "shard", None),
        P(),
        P(None, "shard", "path", None),
        P(None, "shard", "path", None),
    )
    out_specs = (
        P("path", None, "shard", None),
        P(None, "shard", "path", None),
        P(None, "shard", "path", None),
    )
    chosen = local if mesh.shape["path"] <= MOST_UNROLLED else local_wide
    return jax.shard_map(chosen, mesh=mesh, in_specs=in_specs, out_specs=out_specs, check_vma=False)
```

```python
import jax
import jax.numpy as jnp
from jax import lax
from jax.experimental import pallas as pl
from jax.experimental.pallas import tpu as pltpu
from jax.sharding import PartitionSpec as P

LEVEL_MODULES = 16
LEVELS = 2
MOST_UNROLLED = 16

outer_rate = 0.7
beta_coef = 0.9
moment_coef = outer_rate * beta_coef * beta_coef
grad_coef = outer_rate * (1.0 + beta_coef)

VMEM_LIMIT = 16 * 1024 * 1024

vmem = pl.BlockSpec(memory_space=pltpu.VMEM)
smem = pl.BlockSpec(memory_space=pltpu.SMEM)
anywhere = pl.BlockSpec(memory_space=pl.ANY)


def call(kernel, out_shape, in_specs, out_specs, **more):
    return pl.pallas_call(
        kernel,
        out_shape=out_shape,
        in_specs=in_specs,
        out_specs=out_specs,
        compiler_params=pltpu.CompilerParams(vmem_limit_bytes=VMEM_LIMIT),
        **more,
    )


def mirrored(k, size):
    if size < 8:
        return k
    return (k & ~6) | ((k & 2) << 1) | ((k & 4) >> 1)


def target(here, k, size):
    if isinstance(here, int):
        return here ^ (mirrored(k, size) if here & 1 else k)
    return here ^ jnp.where(here & 1 == 1, mirrored(k, size), k)


def origin(here, k, size):
    if isinstance(here, int):
        return here ^ (mirrored(k, size) if (here ^ k) & 1 else k)
    return here ^ jnp.where((here ^ k) & 1 == 1, mirrored(k, size), k)


def order_of(size):
    return sorted(range(2, size, 2), key=lambda k: (-bin(k).count("1"), k)) + [0]


def move(array, k, size):
    if k == 0:
        return array
    return lax.ppermute(array, "path", [(i, target(i, k, size)) for i in range(size)])


def pack_kernel(size, here_ref, delta_ref, square_ref, *outs):
    total = jnp.zeros(square_ref.shape, jnp.float32)
    order = order_of(size)
    for level in range(LEVELS):
        for j, k in enumerate(order):
            block = delta_ref[level, target(here_ref[0], k, size) // 2]
            outs[level * len(order) + j][...] = block
            block = block * block
            folded = block.reshape(-1, 8, block.shape[-1]).sum(axis=0)
            for lane in range(0, block.shape[-1], 128):
                total = total + folded[:, lane : lane + 128]
    square_ref[...] = total


def scale_kernel(entries, shards, here_ref, ids_ref, plan_ref, *refs):
    del plan_ref
    tiles, refs = refs[:shards], refs[shards:]
    tile = tiles[0][...]
    for other in tiles[1:]:
        tile = tile + other[...]
    total = jnp.broadcast_to(jnp.sum(tile, keepdims=True), (8, 128))
    rescale = 1.0 / jnp.sqrt(total / entries + 1e-06)
    count = len(refs) // 2
    rounds = count // LEVELS
    for level in range(LEVELS):
        own = ids_ref[here_ref[0], level]
        sharers = jnp.int32(0)
        for path in range(ids_ref.shape[0]):
            sharers = sharers + jnp.where(ids_ref[path, level] == own, 1, 0)
        factor = rescale / jnp.full((8, 128), sharers, jnp.int32).astype(jnp.float32)
        for j in range(level * rounds, (level + 1) * rounds):
            block, out = refs[j], refs[count + j]
            halves, rows, width = block.shape
            for half in range(halves):
                for row in range(0, rows, 8):
                    for lane in range(0, width, 128):
                        here = (half, slice(row, row + 8), slice(lane, lane + 128))
                        out[here] = block[here] * factor


def plan_kernel(here_ref, ids_ref, chosen_ref, sibling_ref, sender_ref, receiver_ref, module_ref):
    size = ids_ref.shape[0]
    order = order_of(size)
    rounds = len(order)
    here = here_ref[0]
    for level in range(LEVELS):
        first = level * LEVEL_MODULES
        for module in range(LEVEL_MODULES):
            module_ref[first + module] = -1
        sources = [ids_ref[origin(core, k, size), level] + first for core in (here, here ^ 1) for k in order]
        for i in reversed(range(size)):
            module_ref[sources[i]] = i
        for i in range(size):
            sender_ref[level, i] = module_ref[sources[i]]
        for j, k in enumerate(order):
            module = ids_ref[target(here, k, size), level] + first
            chosen_ref[level, j] = module
            receiver_ref[level, j] = module_ref[module]
            sibling_ref[level, j] = ids_ref[target(here ^ 1, k, size), level] + first


def base_kernel(sibling_ref, decayed_ref, out_ref):
    for level in range(out_ref.shape[0]):
        for j in range(out_ref.shape[1]):
            out_ref[level, j] = decayed_ref[sibling_ref[level, j]]


def join_kernel(rounds, *refs):
    for j in range(rounds):
        refs[-1][j] = refs[j][...]


def outgoing_kernel(
    level, here_ref, chosen_ref, sender_ref, receiver_ref, decayed_ref, base_ref, mine_ref, theirs_ref, *refs
):
    outs, grad_ref = refs[:-1], refs[-1]
    rounds = len(outs)
    core = here_ref[0] & 1
    for j in range(rounds):
        grad_ref[j] = mine_ref[j]
        grad_ref[rounds + j] = theirs_ref[j]
    for i in range(1, 2 * rounds):
        leader = sender_ref[level, i]

        @pl.when(leader != i)
        def _():
            grad_ref[leader] += grad_ref[i]

    for j, out in enumerate(outs):
        leader = receiver_ref[level, j]
        out[core] = decayed_ref[chosen_ref[level, j]] - grad_coef * grad_ref[leader, core]
        out[1 - core] = base_ref[level, j] - grad_coef * grad_ref[leader, 1 - core]


def state_kernel(level, here_ref, module_ref, grad_ref, decayed_ref, momentum_ref, *outs):
    new_params_ref, new_momentum_ref = outs[-2:]
    core = here_ref[0] & 1
    count = new_params_ref.shape[0]
    first = level * LEVEL_MODULES + pl.program_id(0) * count
    for place in range(count):
        module = first + place
        leader = module_ref[module]
        taken = jnp.where(leader < 0, 0.0, 1.0)
        grad = taken * grad_ref[jnp.maximum(leader, 0), core]
        new_momentum_ref[place] = beta_coef * momentum_ref[module] + grad
        new_params_ref[place] = decayed_ref[module] - grad_coef * grad


def assemble_kernel(size, level, here_ref, *refs):
    order = order_of(size)
    out_ref, sems = refs[-2:]
    copies = []
    for j, k in enumerate(order):
        place = origin(here_ref[0], k, size) // 2
        copies.append(pltpu.make_async_copy(refs[j], out_ref.at[level, place], sems.at[j]))
    for copy in copies:
        copy.start()
    for copy in copies:
        copy.wait()


def local(path_delta, assign, params, momentum):
    own_slab = path_delta[0]
    size = assign.shape[0]
    module_count, _, own_rows, width = params.shape
    shards = lax.axis_size("shard")
    entries = float(own_slab.size * shards)
    state_in = params.reshape(module_count, own_rows, width)
    moment_in = momentum.reshape(module_count, own_rows, width)
    split_slab = own_slab.reshape(LEVELS, size // 2, 2, own_rows, width)
    here = lax.axis_index("path").astype(jnp.int32).reshape(1)
    order = order_of(size)
    rounds = len(order)
    chip_rows = jax.ShapeDtypeStruct((2, own_rows, width), jnp.float32)

    squares, *raw = call(
        lambda *refs: pack_kernel(size, *refs),
        [jax.ShapeDtypeStruct((8, 128), jnp.float32)] + [chip_rows] * (LEVELS * rounds),
        [smem, vmem],
        [vmem] * (1 + LEVELS * rounds),
    )(here, split_slab)
    tiles = [squares] + [
        lax.ppermute(squares, "shard", [(i, (i + step) % shards) for i in range(shards)])
        for step in range(1, shards)
    ]
    by_round = jax.ShapeDtypeStruct((LEVELS, rounds), jnp.int32)
    chosen, sibling, sender, receiver, leaders = call(
        plan_kernel,
        [
            by_round,
            by_round,
            jax.ShapeDtypeStruct((LEVELS, size), jnp.int32),
            by_round,
            jax.ShapeDtypeStruct((module_count,), jnp.int32),
        ],
        [smem, smem],
        [smem] * 5,
    )(here, assign)
    scaled = call(
        lambda *refs: scale_kernel(entries, shards, *refs),
        [chip_rows] * (LEVELS * rounds),
        [smem, smem, smem] + [vmem] * (shards + LEVELS * rounds),
        [vmem] * (LEVELS * rounds),
    )(here, assign, chosen, *tiles, *raw)
    decayed = state_in - moment_coef * moment_in
    base = call(
        base_kernel,
        jax.ShapeDtypeStruct((LEVELS, rounds, own_rows, width), jnp.float32),
        [smem, vmem],
        vmem,
    )(sibling, decayed)
    swap = [(i, i ^ 1) for i in range(size)]
    base = lax.ppermute(base, "path", swap)

    path_params, new_state, new_moment, before = None, None, None, []
    block = LEVEL_MODULES // 2
    for level in range(LEVELS):
        received = [move(scaled[level * rounds + j], k, size) for j, k in enumerate(order)]
        mine = call(
            lambda *refs: join_kernel(rounds, *refs),
            jax.ShapeDtypeStruct((rounds, 2, own_rows, width), jnp.float32),
            [vmem] * rounds + [anywhere] * len(before),
            vmem,
        )(*received, *before)
        theirs = lax.ppermute(mine, "path", swap)
        *outgoing, grad = call(
            lambda *refs, level=level: outgoing_kernel(level, *refs),
            [chip_rows] * rounds + [jax.ShapeDtypeStruct((size, 2, own_rows, width), jnp.float32)],
            [smem] * 4 + [vmem] * 4,
            [vmem] * (rounds + 1),
        )(here, chosen, sender, receiver, decayed, base, mine, theirs)
        before = [grad]
        returned = [move(outgoing[j], k, size) for j, k in enumerate(order)]
        held = [] if level == 0 else [path_params]
        path_params = call(
            lambda *refs, level=level: assemble_kernel(size, level, *refs),
            jax.ShapeDtypeStruct(split_slab.shape, jnp.float32),
            [smem] + [anywhere] * (rounds + len(held)),
            anywhere,
            scratch_shapes=[pltpu.SemaphoreType.DMA((rounds,))],
            input_output_aliases={1 + rounds: 0} if held else {},
        )(here, *returned, *held)
        held = [] if level == 0 else [new_state, new_moment]
        steps = LEVEL_MODULES // block
        state_block = pl.BlockSpec((block, own_rows, width), lambda i, level=level: (i + level * steps, 0, 0))
        new_state, new_moment = call(
            lambda *refs, level=level: state_kernel(level, *refs),
            [jax.ShapeDtypeStruct(state_in.shape, jnp.float32)] * 2,
            [smem, smem, vmem, vmem, vmem] + [anywhere] * len(held),
            [state_block, state_block],
            grid=(steps,),
            input_output_aliases={5: 0, 6: 1} if held else {},
        )(here, leaders, grad, decayed, moment_in, *held)
    return (path_params.reshape(path_delta.shape), new_state[:, None], new_moment[:, None])


def local_wide(path_delta, assign, params, momentum):
    own_slab = path_delta[0]
    path_count = assign.shape[0]
    module_count, _, own_rows, width = params.shape
    entries = float(own_slab.size * lax.axis_size("shard"))
    total_sq = lax.psum(jnp.sum(own_slab * own_slab), "shard")
    scaled = own_slab * (1.0 / jnp.sqrt(total_sq / entries + 1e-06))
    received = lax.all_to_all(
        scaled.reshape(LEVELS, path_count, own_rows, width), "path", split_axis=1, concat_axis=1, tiled=True
    )
    flat_ids = (assign + LEVEL_MODULES * jnp.arange(LEVELS, dtype=jnp.int32)[None, :]).T.reshape(-1)
    member = (jnp.arange(module_count, dtype=jnp.int32)[:, None] == flat_ids[None, :]).astype(jnp.float32)
    mean = member / jnp.maximum(jnp.sum(member, axis=1), 1.0)[:, None]
    grad = jnp.einsum(
        "mp,prd->mrd", mean, received.reshape(-1, own_rows, width), precision=lax.Precision.HIGHEST
    )
    new_moment = beta_coef * momentum[:, 0] + grad
    new_state = params[:, 0] - outer_rate * (grad + beta_coef * new_moment)
    outgoing = jnp.take(new_state, flat_ids, axis=0).reshape(LEVELS, path_count, own_rows, width)
    returned = lax.all_to_all(outgoing, "path", split_axis=1, concat_axis=1, tiled=True)
    return (returned.reshape(path_delta.shape), new_state[:, None], new_moment[:, None])


def solution(mesh):
    in_specs = (
        P("path", None, "shard", None),
        P(),
        P(None, "shard", "path", None),
        P(None, "shard", "path", None),
    )
    out_specs = (
        P("path", None, "shard", None),
        P(None, "shard", "path", None),
        P(None, "shard", "path", None),
    )
    chosen = local if 4 <= mesh.shape["path"] <= MOST_UNROLLED else local_wide
    return jax.shard_map(chosen, mesh=mesh, in_specs=in_specs, out_specs=out_specs, check_vma=False)
```

```python
import jax
import jax.numpy as jnp
from jax import lax
from jax.experimental import pallas as pl
from jax.experimental.pallas import tpu as pltpu
from jax.sharding import PartitionSpec as P

LEVEL_MODULES = 16
LEVELS = 2
MOST_UNROLLED = 16

outer_rate = 0.7
beta_coef = 0.9
moment_coef = outer_rate * beta_coef * beta_coef
grad_coef = outer_rate * (1.0 + beta_coef)

VMEM_LIMIT = 16 * 1024 * 1024

vmem = pl.BlockSpec(memory_space=pltpu.VMEM)
smem = pl.BlockSpec(memory_space=pltpu.SMEM)
anywhere = pl.BlockSpec(memory_space=pl.ANY)


def call(kernel, out_shape, in_specs, out_specs, **more):
    return pl.pallas_call(
        kernel,
        out_shape=out_shape,
        in_specs=in_specs,
        out_specs=out_specs,
        compiler_params=pltpu.CompilerParams(vmem_limit_bytes=VMEM_LIMIT),
        **more,
    )


def mirrored(k, size):
    if size < 8:
        return k
    return (k & ~6) | ((k & 2) << 1) | ((k & 4) >> 1)


def target(here, k, size):
    if isinstance(here, int):
        return here ^ (mirrored(k, size) if here & 1 else k)
    return here ^ jnp.where(here & 1 == 1, mirrored(k, size), k)


def origin(here, k, size):
    if isinstance(here, int):
        return here ^ (mirrored(k, size) if (here ^ k) & 1 else k)
    return here ^ jnp.where((here ^ k) & 1 == 1, mirrored(k, size), k)


def order_of(size):
    return sorted(range(2, size, 2), key=lambda k: (-bin(k).count("1"), k)) + [0]


def move(array, k, size):
    if k == 0:
        return array
    return lax.ppermute(array, "path", [(i, target(i, k, size)) for i in range(size)])


def pack_kernel(size, here_ref, delta_ref, square_ref, give_ref, *outs):
    total = jnp.zeros(square_ref.shape, jnp.float32)
    order = order_of(size)
    here = here_ref[0]
    core = here & 1
    for level in range(LEVELS):
        for j, k in enumerate(order):
            chip = target(here, k, size) // 2
            kept = delta_ref[level, chip, core]
            given = delta_ref[level, chip, 1 - core]
            outs[level * len(order) + j][...] = kept
            give_ref[level, chip] = given
            block = kept * kept + given * given
            folded = block.reshape(-1, 8, block.shape[-1]).sum(axis=0)
            for lane in range(0, block.shape[-1], 128):
                total = total + folded[:, lane : lane + 128]
    square_ref[...] = total


def pair_kernel(here_ref, own_ref, other_ref, out_ref):
    core = here_ref[0] & 1
    out_ref[core] = own_ref[...]
    out_ref[1 - core] = other_ref[...]


def add_kernel(a_ref, b_ref, out_ref):
    out_ref[...] = a_ref[...] + b_ref[...]


def scale_kernel(entries, here_ref, ids_ref, plan_ref, squares_ref, other_ref, gift_ref, *refs):
    del plan_ref
    here = here_ref[0]
    count = len(refs) // 2
    rounds = count // LEVELS
    order = order_of(2 * rounds)
    for source in range(2):
        tile = squares_ref[source] + other_ref[source]
        total = jnp.broadcast_to(jnp.sum(tile, keepdims=True), (8, 128))
        rescale = 1.0 / jnp.sqrt(total / entries + 1e-06)
        path = (here // 2) * 2 + source
        for level in range(LEVELS):
            own = ids_ref[path, level]
            sharers = jnp.int32(0)
            for other in range(ids_ref.shape[0]):
                sharers = sharers + jnp.where(ids_ref[other, level] == own, 1, 0)
            factor = rescale / jnp.full((8, 128), sharers, jnp.int32).astype(jnp.float32)

            def scale(own_rows, level=level, source=source, factor=factor):
                for j, k in enumerate(order):
                    out = refs[count + level * rounds + j]
                    chip = target(here, k, 2 * rounds) // 2
                    _, rows, width = out.shape
                    for row in range(0, rows, 8):
                        for lane in range(0, width, 128):
                            at = (slice(row, row + 8), slice(lane, lane + 128))
                            if own_rows:
                                block = refs[level * rounds + j][at]
                            else:
                                block = gift_ref[(level, chip, *at)]
                            out[(source, *at)] = block * factor

            pl.when(here & 1 == source)(lambda scale=scale: scale(True))
            pl.when(here & 1 != source)(lambda scale=scale: scale(False))


def plan_kernel(here_ref, ids_ref, chosen_ref, sender_ref, receiver_ref, module_ref):
    size = ids_ref.shape[0]
    order = order_of(size)
    here = here_ref[0]
    for level in range(LEVELS):
        first = level * LEVEL_MODULES
        for module in range(LEVEL_MODULES):
            module_ref[first + module] = -1
        sources = [ids_ref[(origin(here, k, size) // 2) * 2 + half, level] + first for k in order for half in range(2)]
        for i in reversed(range(size)):
            module_ref[sources[i]] = i
        for i in range(size):
            sender_ref[level, i] = module_ref[sources[i]]
        for j, k in enumerate(order):
            for half in range(2):
                module = ids_ref[(target(here, k, size) // 2) * 2 + half, level] + first
                chosen_ref[level, 2 * j + half] = module
                receiver_ref[level, 2 * j + half] = module_ref[module]


def outgoing_kernel(level, rounds, chosen_ref, sender_ref, receiver_ref, decayed_ref, *refs):
    received, outs, grad_ref = refs[:rounds], refs[rounds:-1], refs[-1]
    for i in range(2 * rounds):
        grad_ref[i] = received[i // 2][i % 2]
    for i in range(1, 2 * rounds):
        leader = sender_ref[level, i]

        @pl.when(leader != i)
        def _():
            grad_ref[leader] += grad_ref[i]

    for i in range(2 * rounds):
        decayed = decayed_ref[chosen_ref[level, i]]
        outs[i // 2][i % 2] = decayed - grad_coef * grad_ref[receiver_ref[level, i]]


def state_kernel(level, module_ref, grad_ref, decayed_ref, momentum_ref, *outs):
    new_params_ref, new_momentum_ref = outs[-2:]
    count = new_params_ref.shape[0]
    first = level * LEVEL_MODULES + pl.program_id(0) * count
    for place in range(count):
        module = first + place
        leader = module_ref[module]
        taken = jnp.where(leader < 0, 0.0, 1.0)
        grad = taken * grad_ref[jnp.maximum(leader, 0)]
        new_momentum_ref[place] = beta_coef * momentum_ref[module] + grad
        new_params_ref[place] = decayed_ref[module] - grad_coef * grad


def give_back_kernel(size, here_ref, *refs):
    here = here_ref[0]
    for j, k in enumerate(order_of(size)):
        refs[-1][origin(here, k, size) // 2] = refs[j][1 - (here & 1)]


def assemble_kernel(size, level, here_ref, *refs):
    order = order_of(size)
    here = here_ref[0]
    core = here & 1
    out_ref, sems = refs[-2:]
    copies = []
    for j, k in enumerate(order):
        chip = origin(here, k, size) // 2
        copies.append(pltpu.make_async_copy(refs[j].at[core], out_ref.at[level, chip, core], sems.at[0, j]))
        copies.append(pltpu.make_async_copy(refs[len(order)].at[j], out_ref.at[level, j, 1 - core], sems.at[1, j]))
    for copy in copies:
        copy.start()
    for copy in copies:
        copy.wait()


def local(path_delta, assign, params, momentum):
    own_slab = path_delta[0]
    size = assign.shape[0]
    module_count, _, own_rows, width = params.shape
    shards = lax.axis_size("shard")
    entries = float(own_slab.size * shards)
    state_in = params.reshape(module_count, own_rows, width)
    moment_in = momentum.reshape(module_count, own_rows, width)
    split_slab = own_slab.reshape(LEVELS, size // 2, 2, own_rows, width)
    here = lax.axis_index("path").astype(jnp.int32).reshape(1)
    order = order_of(size)
    rounds = len(order)
    swap = [(i, i ^ 1) for i in range(size)]
    rows = jax.ShapeDtypeStruct((own_rows, width), jnp.float32)
    both = jax.ShapeDtypeStruct((2, own_rows, width), jnp.float32)
    by_chip = jax.ShapeDtypeStruct((rounds, own_rows, width), jnp.float32)
    by_path = jax.ShapeDtypeStruct((size, own_rows, width), jnp.float32)
    tile = jax.ShapeDtypeStruct((8, 128), jnp.float32)
    tiles = jax.ShapeDtypeStruct((2, 8, 128), jnp.float32)
    places = jax.ShapeDtypeStruct((LEVELS, size), jnp.int32)

    squares, give, *kept = call(
        lambda *refs: pack_kernel(size, *refs),
        [tile, jax.ShapeDtypeStruct((LEVELS, *by_chip.shape), jnp.float32)] + [rows] * (LEVELS * rounds),
        [smem, vmem],
        [vmem] * (2 + LEVELS * rounds),
    )(here, split_slab)
    other = lax.ppermute(squares, "path", swap)
    gift = lax.ppermute(give, "path", swap)
    squares = call(pair_kernel, tiles, [smem, vmem, vmem], vmem)(here, squares, other)
    other = jnp.zeros_like(squares)
    step = 1
    while step < shards:
        if step > 1:
            squares = call(add_kernel, tiles, [vmem, vmem], vmem)(squares, other)
        other = lax.ppermute(squares, "shard", [(i, i ^ step) for i in range(shards)])
        step *= 2
    chosen, sender, receiver, leaders = call(
        plan_kernel,
        [places, places, places, jax.ShapeDtypeStruct((module_count,), jnp.int32)],
        [smem, smem],
        [smem] * 4,
    )(here, assign)
    scaled = call(
        lambda *refs: scale_kernel(entries, *refs),
        [both] * (LEVELS * rounds),
        [smem, smem, smem] + [vmem] * (3 + LEVELS * rounds),
        [vmem] * (LEVELS * rounds),
    )(here, assign, chosen, squares, other, gift, *kept)
    decayed = state_in - moment_coef * moment_in

    path_params, new_state, new_moment = None, None, None
    block = LEVEL_MODULES // 2
    steps = LEVEL_MODULES // block
    for level in range(LEVELS):
        received = [move(scaled[level * rounds + j], k, size) for j, k in enumerate(order)]
        *outgoing, grad = call(
            lambda *refs, level=level: outgoing_kernel(level, rounds, *refs),
            [both] * rounds + [by_path],
            [smem] * 3 + [vmem] * (1 + rounds),
            [vmem] * (rounds + 1),
        )(chosen, sender, receiver, decayed, *received)
        returned = [move(outgoing[j], k, size) for j, k in enumerate(order)]
        held = [] if level == 0 else [new_state, new_moment]
        state_block = pl.BlockSpec((block, own_rows, width), lambda i, level=level: (i + level * steps, 0, 0))
        new_state, new_moment = call(
            lambda *refs, level=level: state_kernel(level, *refs),
            [jax.ShapeDtypeStruct(state_in.shape, jnp.float32)] * 2,
            [smem, vmem, vmem, vmem] + [anywhere] * len(held),
            [state_block, state_block],
            grid=(steps,),
            input_output_aliases={4: 0, 5: 1} if held else {},
        )(leaders, grad, decayed, moment_in, *held)
        before = [new_state] if level == LEVELS - 1 else []
        back = call(
            lambda *refs: give_back_kernel(size, *refs),
            by_chip,
            [smem] + [vmem] * rounds + [anywhere] * len(before),
            vmem,
        )(here, *returned, *before)
        back = lax.ppermute(back, "path", swap)
        held = [] if level == 0 else [path_params]
        path_params = call(
            lambda *refs, level=level: assemble_kernel(size, level, *refs),
            jax.ShapeDtypeStruct(split_slab.shape, jnp.float32),
            [smem] + [anywhere] * (rounds + 1 + len(held)),
            anywhere,
            scratch_shapes=[pltpu.SemaphoreType.DMA((2, rounds))],
            input_output_aliases={2 + rounds: 0} if held else {},
        )(here, *returned, back, *held)
    return (path_params.reshape(path_delta.shape), new_state[:, None], new_moment[:, None])


def local_wide(path_delta, assign, params, momentum):
    own_slab = path_delta[0]
    path_count = assign.shape[0]
    module_count, _, own_rows, width = params.shape
    entries = float(own_slab.size * lax.axis_size("shard"))
    total_sq = lax.psum(jnp.sum(own_slab * own_slab), "shard")
    scaled = own_slab * (1.0 / jnp.sqrt(total_sq / entries + 1e-06))
    received = lax.all_to_all(
        scaled.reshape(LEVELS, path_count, own_rows, width), "path", split_axis=1, concat_axis=1, tiled=True
    )
    flat_ids = (assign + LEVEL_MODULES * jnp.arange(LEVELS, dtype=jnp.int32)[None, :]).T.reshape(-1)
    member = (jnp.arange(module_count, dtype=jnp.int32)[:, None] == flat_ids[None, :]).astype(jnp.float32)
    mean = member / jnp.maximum(jnp.sum(member, axis=1), 1.0)[:, None]
    grad = jnp.einsum(
        "mp,prd->mrd", mean, received.reshape(-1, own_rows, width), precision=lax.Precision.HIGHEST
    )
    new_moment = beta_coef * momentum[:, 0] + grad
    new_state = params[:, 0] - outer_rate * (grad + beta_coef * new_moment)
    outgoing = jnp.take(new_state, flat_ids, axis=0).reshape(LEVELS, path_count, own_rows, width)
    returned = lax.all_to_all(outgoing, "path", split_axis=1, concat_axis=1, tiled=True)
    return (returned.reshape(path_delta.shape), new_state[:, None], new_moment[:, None])


def solution(mesh):
    in_specs = (
        P("path", None, "shard", None),
        P(),
        P(None, "shard", "path", None),
        P(None, "shard", "path", None),
    )
    out_specs = (
        P("path", None, "shard", None),
        P(None, "shard", "path", None),
        P(None, "shard", "path", None),
    )
    chosen = local if 4 <= mesh.shape["path"] <= MOST_UNROLLED else local_wide
    return jax.shard_map(chosen, mesh=mesh, in_specs=in_specs, out_specs=out_specs, check_vma=False)
```

```python
import jax
import jax.numpy as jnp
from jax import lax
from jax.experimental import pallas as pl
from jax.experimental.pallas import tpu as pltpu
from jax.sharding import PartitionSpec as P

LEVEL_MODULES = 16
LEVELS = 2
MOST_UNROLLED = 16

outer_rate = 0.7
beta_coef = 0.9
moment_coef = outer_rate * beta_coef * beta_coef
grad_coef = outer_rate * (1.0 + beta_coef)

VMEM_LIMIT = 16 * 1024 * 1024

vmem = pl.BlockSpec(memory_space=pltpu.VMEM)
smem = pl.BlockSpec(memory_space=pltpu.SMEM)
anywhere = pl.BlockSpec(memory_space=pl.ANY)


def call(kernel, out_shape, in_specs, out_specs, **more):
    return pl.pallas_call(
        kernel,
        out_shape=out_shape,
        in_specs=in_specs,
        out_specs=out_specs,
        compiler_params=pltpu.CompilerParams(vmem_limit_bytes=VMEM_LIMIT),
        **more,
    )


def mirrored(k, size):
    if size < 8:
        return k
    return (k & ~6) | ((k & 2) << 1) | ((k & 4) >> 1)


def target(here, k, size):
    if isinstance(here, int):
        return here ^ (mirrored(k, size) if here & 1 else k)
    return here ^ jnp.where(here & 1 == 1, mirrored(k, size), k)


def origin(here, k, size):
    if isinstance(here, int):
        return here ^ (mirrored(k, size) if (here ^ k) & 1 else k)
    return here ^ jnp.where((here ^ k) & 1 == 1, mirrored(k, size), k)


def order_of(size):
    return sorted(range(2, size, 2), key=lambda k: (-bin(k).count("1"), k)) + [0]


def move(array, k, size):
    if k == 0:
        return array
    return lax.ppermute(array, "path", [(i, target(i, k, size)) for i in range(size)])


def tiles_of(rows, width):
    return [(slice(row, row + 8), slice(lane, lane + 128)) for row in range(0, rows, 8) for lane in range(0, width, 128)]


def pack_kernel(here_ref, delta_ref, keep_ref, give_ref):
    levels, chips, halves, rows, width = delta_ref.shape
    spots = tiles_of(rows, width)

    def pack(core):
        totals = [jnp.zeros((8, 128), jnp.float32) for _ in range(4)]
        for level in range(levels):
            for chip in range(chips):
                for t, spot in enumerate(spots):
                    place = (level * chips + chip) * len(spots) + t
                    kept = delta_ref[(level, chip, core, *spot)]
                    given = delta_ref[(level, chip, 1 - core, *spot)]
                    keep_ref[place] = kept
                    give_ref[place] = given
                    totals[t % 4] = totals[t % 4] + (kept * kept + given * given)
        total = (totals[0] + totals[1]) + (totals[2] + totals[3])
        keep_ref[levels * chips * len(spots)] = total
        give_ref[levels * chips * len(spots)] = total

    for core in range(halves):
        pl.when(here_ref[0] & 1 == core)(lambda core=core: pack(core))


def merge_kernel(size, here_ref, keep_ref, gift_ref, *outs):
    order = order_of(size)
    chips = len(order)
    here = here_ref[0]
    core = here & 1
    last = keep_ref.shape[0] - 1
    count = last // (LEVELS * chips)
    for level in range(LEVELS):
        for j, k in enumerate(order):
            out = outs[level * chips + j]
            first = (level * chips + target(here, k, size) // 2) * count
            out[pl.ds(core * count, count)] = keep_ref[pl.ds(first, count)]
            out[pl.ds((1 - core) * count, count)] = gift_ref[pl.ds(first, count)]
            if level == 0:
                out[2 * count + core] = keep_ref[last]
                out[2 * count + 1 - core] = gift_ref[last]


def collect_kernel(size, here_ref, *refs):
    for j, k in enumerate(order_of(size)):
        block = refs[j]
        chip = origin(here_ref[0], k, size) // 2
        for source in range(2):
            refs[-1][2 * chip + source] = block[block.shape[0] - 2 + source]


def add_kernel(a_ref, b_ref, out_ref):
    out_ref[...] = a_ref[...] + b_ref[...]


def factor_kernel(entries, here_ref, ids_ref, squares_ref, other_ref, out_ref):
    size = ids_ref.shape[0]
    sources = [(origin(here_ref[0], k, size) // 2) * 2 + half for k in order_of(size) for half in range(2)]
    for i, path in enumerate(sources):
        tile = squares_ref[path] + other_ref[path]
        total = jnp.broadcast_to(jnp.sum(tile, keepdims=True), (8, 128))
        rescale = 1.0 / jnp.sqrt(total / entries + 1e-06)
        for level in range(LEVELS):
            sharers = jnp.int32(0)
            for other in range(size):
                sharers = sharers + jnp.where(ids_ref[other, level] == ids_ref[path, level], 1, 0)
            out_ref[level, i] = rescale / jnp.full((8, 128), sharers, jnp.int32).astype(jnp.float32)


def plan_kernel(here_ref, ids_ref, chosen_ref, sender_ref, receiver_ref, module_ref):
    size = ids_ref.shape[0]
    order = order_of(size)
    here = here_ref[0]
    for level in range(LEVELS):
        first = level * LEVEL_MODULES
        for module in range(LEVEL_MODULES):
            module_ref[first + module] = -1
        sources = [ids_ref[(origin(here, k, size) // 2) * 2 + half, level] + first for k in order for half in range(2)]
        for i in reversed(range(size)):
            module_ref[sources[i]] = i
        for i in range(size):
            sender_ref[level, i] = module_ref[sources[i]]
        for j, k in enumerate(order):
            for half in range(2):
                module = ids_ref[(target(here, k, size) // 2) * 2 + half, level] + first
                chosen_ref[level, 2 * j + half] = module
                receiver_ref[level, 2 * j + half] = module_ref[module]


def outgoing_kernel(level, rounds, chosen_ref, sender_ref, receiver_ref, factor_ref, decayed_ref, *refs):
    received, outs, (grad_ref, token_ref) = refs[:rounds], refs[rounds:-2], refs[-2:]
    token_ref[0] = 0
    spots = tiles_of(*grad_ref.shape[1:])
    for i in range(2 * rounds):
        factor = factor_ref[level, i]
        for t, spot in enumerate(spots):
            grad_ref[(i, *spot)] = received[i // 2][(i % 2) * len(spots) + t] * factor
    for i in range(1, 2 * rounds):
        leader = sender_ref[level, i]

        @pl.when(leader != i)
        def _():
            grad_ref[leader] += grad_ref[i]

    for i in range(2 * rounds):
        decayed = decayed_ref[chosen_ref[level, i]]
        outs[i // 2][i % 2] = decayed - grad_coef * grad_ref[receiver_ref[level, i]]


def state_kernel(level, module_ref, grad_ref, decayed_ref, momentum_ref, *refs):
    new_params_ref, new_momentum_ref, token_ref = refs[-3:]
    token_ref[0] = 0
    count = new_params_ref.shape[0]
    first = level * LEVEL_MODULES + pl.program_id(0) * count
    for place in range(count):
        module = first + place
        leader = module_ref[module]
        taken = jnp.where(leader < 0, 0.0, 1.0)
        grad = taken * grad_ref[jnp.maximum(leader, 0)]
        new_momentum_ref[place] = beta_coef * momentum_ref[module] + grad
        new_params_ref[place] = decayed_ref[module] - grad_coef * grad


def give_back_kernel(size, here_ref, *refs):
    here = here_ref[0]
    for j, k in enumerate(order_of(size)):
        refs[-1][origin(here, k, size) // 2] = refs[j][1 - (here & 1)]


def assemble_kernel(size, level, here_ref, *refs):
    order = order_of(size)
    here = here_ref[0]
    core = here & 1
    out_ref, sems = refs[-2:]
    copies = []
    for j, k in enumerate(order):
        chip = origin(here, k, size) // 2
        copies.append(pltpu.make_async_copy(refs[j].at[core], out_ref.at[level, chip, core], sems.at[0, j]))
        copies.append(pltpu.make_async_copy(refs[len(order)].at[j], out_ref.at[level, j, 1 - core], sems.at[1, j]))
    for copy in copies:
        copy.start()
    for copy in copies:
        copy.wait()


def local(path_delta, assign, params, momentum):
    own_slab = path_delta[0]
    size = assign.shape[0]
    module_count, _, own_rows, width = params.shape
    shards = lax.axis_size("shard")
    entries = float(own_slab.size * shards)
    state_in = params.reshape(module_count, own_rows, width)
    moment_in = momentum.reshape(module_count, own_rows, width)
    split_slab = own_slab.reshape(LEVELS, size // 2, 2, own_rows, width)
    here = lax.axis_index("path").astype(jnp.int32).reshape(1)
    order = order_of(size)
    rounds = len(order)
    swap = [(i, i ^ 1) for i in range(size)]
    count = own_rows * width // 1024
    shape = lambda *dims: jax.ShapeDtypeStruct(dims, jnp.float32)
    places = jax.ShapeDtypeStruct((LEVELS, size), jnp.int32)
    token = jax.ShapeDtypeStruct((1,), jnp.int32)

    keep, give = call(
        pack_kernel, [shape(LEVELS * rounds * count + 1, 8, 128)] * 2, [smem, vmem], [vmem] * 2
    )(here, split_slab)
    gift = lax.ppermute(give, "path", swap)
    messages = call(
        lambda *refs: merge_kernel(size, *refs),
        [shape(2 * count + 2 * (level == 0), 8, 128) for level in range(LEVELS) for _ in order],
        [smem, vmem, vmem],
        [vmem] * (LEVELS * rounds),
    )(here, keep, gift)
    received = [
        [move(messages[level * rounds + j], k, size) for j, k in enumerate(order)] for level in range(LEVELS)
    ]
    chosen, sender, receiver, leaders = call(
        plan_kernel,
        [places, places, places, jax.ShapeDtypeStruct((module_count,), jnp.int32)],
        [smem, smem],
        [smem] * 4,
    )(here, assign)
    decayed = state_in - moment_coef * moment_in

    squares = call(
        lambda *refs: collect_kernel(size, *refs),
        shape(size, 8, 128),
        [smem] + [vmem] * rounds + [smem, anywhere],
        vmem,
    )(here, *received[0], chosen, decayed)
    other = jnp.zeros_like(squares)
    step = 1
    while step < shards:
        if step > 1:
            squares = call(add_kernel, shape(size, 8, 128), [vmem, vmem], vmem)(squares, other)
        other = lax.ppermute(squares, "shard", [(i, i ^ step) for i in range(shards)])
        step *= 2
    factors = call(
        lambda *refs: factor_kernel(entries, *refs),
        shape(LEVELS, size, 8, 128),
        [smem, smem, vmem, vmem],
        vmem,
    )(here, assign, squares, other)

    returned, grads, updated = [], [], []
    for level in range(LEVELS):
        *outgoing, grad, done = call(
            lambda *refs, level=level: outgoing_kernel(level, rounds, *refs),
            [shape(2, own_rows, width)] * rounds + [shape(size, own_rows, width), token],
            [smem] * 3 + [vmem] * (2 + rounds),
            [vmem] * (rounds + 1) + [smem],
        )(chosen, sender, receiver, factors, decayed, *received[level])
        returned.append([move(outgoing[j], k, size) for j, k in enumerate(order)])
        grads.append(grad)
        updated.append(done)

    new_state, new_moment, tokens = None, None, []
    block = LEVEL_MODULES // 2
    steps = LEVEL_MODULES // block
    for level in range(LEVELS):
        held = [] if level == 0 else [new_state, new_moment]
        state_block = pl.BlockSpec((block, own_rows, width), lambda i, level=level: (i + level * steps, 0, 0))
        new_state, new_moment, done = call(
            lambda *refs, level=level: state_kernel(level, *refs),
            [shape(*state_in.shape)] * 2 + [token],
            [smem, vmem, vmem, vmem] + [anywhere] * len(held),
            [state_block, state_block, smem],
            grid=(steps,),
            input_output_aliases={4: 0, 5: 1} if held else {},
        )(leaders, grads[level], decayed, moment_in, *held)
        tokens.append(done)

    path_params = None
    before = updated[1:] + tokens
    for level in range(LEVELS):
        back = call(
            lambda *refs: give_back_kernel(size, *refs),
            shape(rounds, own_rows, width),
            [smem] + [vmem] * rounds + [smem] * len(before),
            vmem,
        )(here, *returned[level], *before)
        back = lax.ppermute(back, "path", swap)
        held = [] if level == 0 else [path_params]
        path_params = call(
            lambda *refs, level=level: assemble_kernel(size, level, *refs),
            shape(*split_slab.shape),
            [smem] + [anywhere] * (rounds + 1 + len(held)),
            anywhere,
            scratch_shapes=[pltpu.SemaphoreType.DMA((2, rounds))],
            input_output_aliases={2 + rounds: 0} if held else {},
        )(here, *returned[level], back, *held)
        before = tokens
    return (path_params.reshape(path_delta.shape), new_state[:, None], new_moment[:, None])


def local_wide(path_delta, assign, params, momentum):
    own_slab = path_delta[0]
    path_count = assign.shape[0]
    module_count, _, own_rows, width = params.shape
    entries = float(own_slab.size * lax.axis_size("shard"))
    total_sq = lax.psum(jnp.sum(own_slab * own_slab), "shard")
    scaled = own_slab * (1.0 / jnp.sqrt(total_sq / entries + 1e-06))
    received = lax.all_to_all(
        scaled.reshape(LEVELS, path_count, own_rows, width), "path", split_axis=1, concat_axis=1, tiled=True
    )
    flat_ids = (assign + LEVEL_MODULES * jnp.arange(LEVELS, dtype=jnp.int32)[None, :]).T.reshape(-1)
    member = (jnp.arange(module_count, dtype=jnp.int32)[:, None] == flat_ids[None, :]).astype(jnp.float32)
    mean = member / jnp.maximum(jnp.sum(member, axis=1), 1.0)[:, None]
    grad = jnp.einsum(
        "mp,prd->mrd", mean, received.reshape(-1, own_rows, width), precision=lax.Precision.HIGHEST
    )
    new_moment = beta_coef * momentum[:, 0] + grad
    new_state = params[:, 0] - outer_rate * (grad + beta_coef * new_moment)
    outgoing = jnp.take(new_state, flat_ids, axis=0).reshape(LEVELS, path_count, own_rows, width)
    returned = lax.all_to_all(outgoing, "path", split_axis=1, concat_axis=1, tiled=True)
    return (returned.reshape(path_delta.shape), new_state[:, None], new_moment[:, None])


def solution(mesh):
    in_specs = (
        P("path", None, "shard", None),
        P(),
        P(None, "shard", "path", None),
        P(None, "shard", "path", None),
    )
    out_specs = (
        P("path", None, "shard", None),
        P(None, "shard", "path", None),
        P(None, "shard", "path", None),
    )
    chosen = local if 4 <= mesh.shape["path"] <= MOST_UNROLLED else local_wide
    return jax.shard_map(chosen, mesh=mesh, in_specs=in_specs, out_specs=out_specs, check_vma=False)
```

```python
import jax
import jax.numpy as jnp
from jax import lax
from jax.experimental import pallas as pl
from jax.experimental.pallas import tpu as pltpu
from jax.sharding import PartitionSpec as P

LEVEL_MODULES = 16
LEVELS = 2
MOST_UNROLLED = 16

outer_rate = 0.7
beta_coef = 0.9
moment_coef = outer_rate * beta_coef * beta_coef
grad_coef = outer_rate * (1.0 + beta_coef)

VMEM_LIMIT = 16 * 1024 * 1024

vmem = pl.BlockSpec(memory_space=pltpu.VMEM)
smem = pl.BlockSpec(memory_space=pltpu.SMEM)
anywhere = pl.BlockSpec(memory_space=pl.ANY)


def call(kernel, out_shape, in_specs, out_specs, **more):
    return pl.pallas_call(
        kernel,
        out_shape=out_shape,
        in_specs=in_specs,
        out_specs=out_specs,
        compiler_params=pltpu.CompilerParams(vmem_limit_bytes=VMEM_LIMIT),
        **more,
    )


def mirrored(k, size):
    if size < 8:
        return k
    return (k & ~6) | ((k & 2) << 1) | ((k & 4) >> 1)


def target(here, k, size):
    if isinstance(here, int):
        return here ^ (mirrored(k, size) if here & 1 else k)
    return here ^ jnp.where(here & 1 == 1, mirrored(k, size), k)


def origin(here, k, size):
    if isinstance(here, int):
        return here ^ (mirrored(k, size) if (here ^ k) & 1 else k)
    return here ^ jnp.where((here ^ k) & 1 == 1, mirrored(k, size), k)


def order_of(size):
    return sorted(range(2, size, 2), key=lambda k: (-bin(k).count("1"), k)) + [0]


def move(array, k, size):
    if k == 0:
        return array
    return lax.ppermute(array, "path", [(i, target(i, k, size)) for i in range(size)])


def tiles_of(rows, width):
    return [(slice(row, row + 8), slice(lane, lane + 128)) for row in range(0, rows, 8) for lane in range(0, width, 128)]


def pack_kernel(here_ref, delta_ref, square_ref, keep_ref, give_ref):
    levels, chips, halves, rows, width = delta_ref.shape

    def pack(core):
        totals = [jnp.zeros((8, 128), jnp.float32) for _ in range(4)]
        for level in range(levels):
            for chip in range(chips):
                for t, spot in enumerate(tiles_of(rows, width)):
                    kept = delta_ref[(level, chip, core, *spot)]
                    given = delta_ref[(level, chip, 1 - core, *spot)]
                    keep_ref[(level, chip, *spot)] = kept
                    give_ref[(level, chip, *spot)] = given
                    totals[t % 4] = totals[t % 4] + (kept * kept + given * given)
        total = jnp.sum((totals[0] + totals[1]) + (totals[2] + totals[3]), axis=0, keepdims=True)
        for first in range(0, square_ref.shape[0], 8):
            row = lax.broadcasted_iota(jnp.int32, (8, 128), 0) + first
            square_ref[first : first + 8] = jnp.where(row == here_ref[0], total, 0.0)

    for core in range(halves):
        pl.when(here_ref[0] & 1 == core)(lambda core=core: pack(core))


def merge_kernel(size, here_ref, square_ref, keep_ref, gift_ref, plan_ref, square_out, *outs):
    del plan_ref
    here = here_ref[0]
    core = here & 1
    square_out[...] = square_ref[...]
    for k, out in zip(order_of(size), outs):
        chip = target(here, k, size) // 2
        for level in range(LEVELS):
            out[core, level] = keep_ref[level, chip]
            out[1 - core, level] = gift_ref[level, chip]


def factor_kernel(entries, here_ref, ids_ref, square_ref, out_ref, rescale_ref):
    size = ids_ref.shape[0]
    total = jnp.sum(square_ref[...], axis=1, keepdims=True)
    rescale_ref[...] = jnp.broadcast_to(1.0 / jnp.sqrt(total / entries + 1e-06), square_ref.shape)
    sources = [(origin(here_ref[0], k, size) // 2) * 2 + half for k in order_of(size) for half in range(2)]
    for i, path in enumerate(sources):
        rescale = jnp.broadcast_to(rescale_ref[pl.ds(path, 1), :], (8, 128))
        for level in range(LEVELS):
            sharers = jnp.int32(0)
            for other in range(size):
                sharers = sharers + jnp.where(ids_ref[other, level] == ids_ref[path, level], 1, 0)
            out_ref[level, i] = rescale / jnp.full((8, 128), sharers, jnp.int32).astype(jnp.float32)


def plan_kernel(here_ref, ids_ref, plan_ref, module_ref):
    size = ids_ref.shape[0]
    order = order_of(size)
    here = here_ref[0]
    for level in range(LEVELS):
        first = level * LEVEL_MODULES
        for module in range(LEVEL_MODULES):
            module_ref[first + module] = -1
        sources = [ids_ref[(origin(here, k, size) // 2) * 2 + half, level] + first for k in order for half in range(2)]
        for i in reversed(range(size)):
            module_ref[sources[i]] = i
        for i in range(size):
            plan_ref[level, i] = module_ref[sources[i]]
        for j, k in enumerate(order):
            for half in range(2):
                module = ids_ref[(target(here, k, size) // 2) * 2 + half, level] + first
                plan_ref[level, size + 2 * j + half] = module
                plan_ref[level, 2 * size + 2 * j + half] = module_ref[module]


def outgoing_kernel(level, rounds, plan_ref, factor_ref, decayed_ref, *refs):
    received, outs, grad_ref = refs[:rounds], refs[rounds:-1], refs[-1]
    size = 2 * rounds
    for i in range(size):
        factor = factor_ref[level, i]
        for spot in tiles_of(*grad_ref.shape[1:]):
            grad_ref[(i, *spot)] = received[i // 2][(i % 2, level, *spot)] * factor
    for i in range(1, size):
        leader = plan_ref[level, i]

        @pl.when(leader != i)
        def _():
            grad_ref[leader] += grad_ref[i]

    for i in range(size):
        decayed = decayed_ref[plan_ref[level, size + i]]
        outs[i // 2][i % 2] = decayed - grad_coef * grad_ref[plan_ref[level, 2 * size + i]]


def state_kernel(level, module_ref, grad_ref, decayed_ref, momentum_ref, *refs):
    new_params_ref, new_momentum_ref, token_ref = refs[-3:]
    token_ref[...] = jnp.zeros_like(token_ref)
    count = new_params_ref.shape[0]
    first = level * LEVEL_MODULES + pl.program_id(0) * count
    for place in range(count):
        module = first + place
        leader = module_ref[module]
        taken = jnp.where(leader < 0, 0.0, 1.0)
        grad = taken * grad_ref[jnp.maximum(leader, 0)]
        new_momentum_ref[place] = beta_coef * momentum_ref[module] + grad
        new_params_ref[place] = decayed_ref[module] - grad_coef * grad


def give_back_kernel(size, here_ref, *refs):
    here = here_ref[0]
    for j, k in enumerate(order_of(size)):
        refs[-1][origin(here, k, size) // 2] = refs[j][1 - (here & 1)]


def assemble_kernel(size, here_ref, *refs):
    order = order_of(size)
    rounds = len(order)
    here = here_ref[0]
    core = here & 1
    out_ref, sems = refs[-2:]
    copies = []
    for level in range(LEVELS):
        blocks = refs[level * (rounds + 1) : (level + 1) * (rounds + 1)]
        for j, k in enumerate(order):
            chip = origin(here, k, size) // 2
            copies.append(pltpu.make_async_copy(blocks[j].at[core], out_ref.at[level, chip, core], sems.at[level, j]))
        for chip in range(rounds):
            copies.append(
                pltpu.make_async_copy(
                    blocks[rounds].at[chip], out_ref.at[level, chip, 1 - core], sems.at[level, rounds + chip]
                )
            )
    for copy in copies:
        copy.start()
    for copy in copies:
        copy.wait()


def local(path_delta, assign, params, momentum):
    own_slab = path_delta[0]
    size = assign.shape[0]
    module_count, _, own_rows, width = params.shape
    shards = lax.axis_size("shard")
    entries = float(own_slab.size * shards)
    state_in = params.reshape(module_count, own_rows, width)
    moment_in = momentum.reshape(module_count, own_rows, width)
    split_slab = own_slab.reshape(LEVELS, size // 2, 2, own_rows, width)
    here = lax.axis_index("path").astype(jnp.int32).reshape(1)
    order = order_of(size)
    rounds = len(order)
    swap = [(i, i ^ 1) for i in range(size)]
    shape = lambda *dims: jax.ShapeDtypeStruct(dims, jnp.float32)
    squares_shape = shape(-(-size // 8) * 8, 128)

    squares, keep, give = call(
        pack_kernel, [squares_shape] + [shape(LEVELS, rounds, own_rows, width)] * 2, [smem, vmem], [vmem] * 3
    )(here, split_slab)
    gift = lax.ppermute(give, "path", swap)
    plan, leaders = call(
        plan_kernel,
        [jax.ShapeDtypeStruct((LEVELS, 3 * size), jnp.int32), jax.ShapeDtypeStruct((module_count,), jnp.int32)],
        [smem, smem],
        [smem] * 2,
    )(here, assign)
    squares, *messages = call(
        lambda *refs: merge_kernel(size, *refs),
        [squares_shape] + [shape(2, LEVELS, own_rows, width)] * rounds,
        [smem, vmem, vmem, vmem, anywhere],
        [vmem] * (1 + rounds),
    )(here, squares, keep, gift, plan)
    received = [move(messages[j], k, size) for j, k in enumerate(order)]
    squares = lax.psum(squares, ("path", "shard"))
    factors = call(
        lambda *refs: factor_kernel(entries, *refs),
        shape(LEVELS, size, 8, 128),
        [smem, smem, vmem],
        vmem,
        scratch_shapes=[pltpu.VMEM(squares_shape.shape, jnp.float32)],
    )(here, assign, squares)
    decayed = state_in - moment_coef * moment_in

    returned, grads = [], []
    for level in range(LEVELS):
        *outgoing, grad = call(
            lambda *refs, level=level: outgoing_kernel(level, rounds, *refs),
            [shape(2, own_rows, width)] * rounds + [shape(size, own_rows, width)],
            [smem] + [vmem] * (2 + rounds),
            [vmem] * (rounds + 1),
        )(plan, factors, decayed, *received)
        returned.append([move(outgoing[j], k, size) for j, k in enumerate(order)])
        grads.append(grad)

    new_state, new_moment, tokens = None, None, []
    block = LEVEL_MODULES // 2
    steps = LEVEL_MODULES // block
    for level in range(LEVELS):
        held = [] if level == 0 else [new_state, new_moment]
        state_block = pl.BlockSpec((block, own_rows, width), lambda i, level=level: (i + level * steps, 0, 0))
        new_state, new_moment, done = call(
            lambda *refs, level=level: state_kernel(level, *refs),
            [shape(*state_in.shape)] * 2 + [shape(8, 128)],
            [smem, vmem, vmem, vmem] + [anywhere] * len(held),
            [state_block, state_block, vmem],
            grid=(steps,),
            input_output_aliases={4: 0, 5: 1} if held else {},
        )(leaders, grads[level], decayed, moment_in, *held)
        tokens.append(done)

    blocks = []
    for level in range(LEVELS):
        before = tokens if level == LEVELS - 1 else []
        back = call(
            lambda *refs: give_back_kernel(size, *refs),
            shape(rounds, own_rows, width),
            [smem] + [vmem] * rounds + [anywhere] * len(before),
            vmem,
        )(here, *returned[level], *before)
        blocks += [*returned[level], lax.ppermute(back, "path", swap)]
    path_params = call(
        lambda *refs: assemble_kernel(size, *refs),
        shape(*split_slab.shape),
        [smem] + [anywhere] * len(blocks),
        anywhere,
        scratch_shapes=[pltpu.SemaphoreType.DMA((LEVELS, 2 * rounds))],
    )(here, *blocks)
    return (path_params.reshape(path_delta.shape), new_state[:, None], new_moment[:, None])


def local_wide(path_delta, assign, params, momentum):
    own_slab = path_delta[0]
    path_count = assign.shape[0]
    module_count, _, own_rows, width = params.shape
    entries = float(own_slab.size * lax.axis_size("shard"))
    total_sq = lax.psum(jnp.sum(own_slab * own_slab), "shard")
    scaled = own_slab * (1.0 / jnp.sqrt(total_sq / entries + 1e-06))
    received = lax.all_to_all(
        scaled.reshape(LEVELS, path_count, own_rows, width), "path", split_axis=1, concat_axis=1, tiled=True
    )
    flat_ids = (assign + LEVEL_MODULES * jnp.arange(LEVELS, dtype=jnp.int32)[None, :]).T.reshape(-1)
    member = (jnp.arange(module_count, dtype=jnp.int32)[:, None] == flat_ids[None, :]).astype(jnp.float32)
    mean = member / jnp.maximum(jnp.sum(member, axis=1), 1.0)[:, None]
    grad = jnp.einsum(
        "mp,prd->mrd", mean, received.reshape(-1, own_rows, width), precision=lax.Precision.HIGHEST
    )
    new_moment = beta_coef * momentum[:, 0] + grad
    new_state = params[:, 0] - outer_rate * (grad + beta_coef * new_moment)
    outgoing = jnp.take(new_state, flat_ids, axis=0).reshape(LEVELS, path_count, own_rows, width)
    returned = lax.all_to_all(outgoing, "path", split_axis=1, concat_axis=1, tiled=True)
    return (returned.reshape(path_delta.shape), new_state[:, None], new_moment[:, None])


def solution(mesh):
    in_specs = (
        P("path", None, "shard", None),
        P(),
        P(None, "shard", "path", None),
        P(None, "shard", "path", None),
    )
    out_specs = (
        P("path", None, "shard", None),
        P(None, "shard", "path", None),
        P(None, "shard", "path", None),
    )
    chosen = local if 4 <= mesh.shape["path"] <= MOST_UNROLLED else local_wide
    return jax.shard_map(chosen, mesh=mesh, in_specs=in_specs, out_specs=out_specs, check_vma=False)
```

```python
import jax
import jax.numpy as jnp
from jax import lax
from jax.experimental import pallas as pl
from jax.experimental.pallas import tpu as pltpu
from jax.sharding import PartitionSpec as P

LEVEL_MODULES = 16
LEVELS = 2
MOST_UNROLLED = 16

outer_rate = 0.7
beta_coef = 0.9
moment_coef = outer_rate * beta_coef * beta_coef
grad_coef = outer_rate * (1.0 + beta_coef)

VMEM_LIMIT = 16 * 1024 * 1024

vmem = pl.BlockSpec(memory_space=pltpu.VMEM)
smem = pl.BlockSpec(memory_space=pltpu.SMEM)
anywhere = pl.BlockSpec(memory_space=pl.ANY)


def call(kernel, out_shape, in_specs, out_specs, **more):
    return pl.pallas_call(
        kernel,
        out_shape=out_shape,
        in_specs=in_specs,
        out_specs=out_specs,
        compiler_params=pltpu.CompilerParams(vmem_limit_bytes=VMEM_LIMIT),
        **more,
    )


def mirrored(k, size):
    if size < 8:
        return k
    return (k & ~6) | ((k & 2) << 1) | ((k & 4) >> 1)


def target(here, k, size):
    if isinstance(here, int):
        return here ^ (mirrored(k, size) if here & 1 else k)
    return here ^ jnp.where(here & 1 == 1, mirrored(k, size), k)


def origin(here, k, size):
    if isinstance(here, int):
        return here ^ (mirrored(k, size) if (here ^ k) & 1 else k)
    return here ^ jnp.where((here ^ k) & 1 == 1, mirrored(k, size), k)


def order_of(size):
    return sorted(range(2, size, 2), key=lambda k: (-bin(k).count("1"), k)) + [0]


def move(array, k, size):
    if k == 0:
        return array
    return lax.ppermute(array, "path", [(i, target(i, k, size)) for i in range(size)])


def tiles_of(rows, width):
    return [(slice(row, row + 8), slice(lane, lane + 128)) for row in range(0, rows, 8) for lane in range(0, width, 128)]


def pack_kernel(here_ref, delta_ref, square_ref, keep_ref, give_ref):
    levels, chips, halves, rows, width = delta_ref.shape

    def pack(core):
        totals = [jnp.zeros((8, 128), jnp.float32) for _ in range(4)]
        for level in range(levels):
            for chip in range(chips):
                for t, spot in enumerate(tiles_of(rows, width)):
                    kept = delta_ref[(level, chip, core, *spot)]
                    given = delta_ref[(level, chip, 1 - core, *spot)]
                    keep_ref[(level, chip, *spot)] = kept
                    give_ref[(level, chip, *spot)] = given
                    totals[t % 4] = totals[t % 4] + (kept * kept + given * given)
        total = jnp.sum((totals[0] + totals[1]) + (totals[2] + totals[3]), axis=0, keepdims=True)
        for first in range(0, square_ref.shape[0], 8):
            row = lax.broadcasted_iota(jnp.int32, (8, 128), 0) + first
            square_ref[first : first + 8] = jnp.where(row == here_ref[0], total, 0.0)

    for core in range(halves):
        pl.when(here_ref[0] & 1 == core)(lambda core=core: pack(core))


def merge_kernel(size, here_ref, square_ref, other_ref, keep_ref, gift_ref, plan_ref, square_out, *outs):
    del plan_ref
    here = here_ref[0]
    core = here & 1
    square_out[...] = square_ref[...] + other_ref[...]
    for k, out in zip(order_of(size), outs):
        chip = target(here, k, size) // 2
        for level in range(LEVELS):
            out[core, level] = keep_ref[level, chip]
            out[1 - core, level] = gift_ref[level, chip]


def sum_kernel(*refs):
    total = refs[0][...]
    for ref in refs[1:-1]:
        total = total + ref[...]
    refs[-1][...] = total


def factor_kernel(entries, here_ref, ids_ref, *refs):
    squares, (out_ref, rescale_ref) = refs[:-2], refs[-2:]
    size = ids_ref.shape[0]
    total = squares[0][...]
    for square_ref in squares[1:]:
        total = total + square_ref[...]
    total = jnp.sum(total, axis=1, keepdims=True)
    rescale_ref[...] = jnp.broadcast_to(1.0 / jnp.sqrt(total / entries + 1e-06), rescale_ref.shape)
    sources = [(origin(here_ref[0], k, size) // 2) * 2 + half for k in order_of(size) for half in range(2)]
    for i, path in enumerate(sources):
        rescale = jnp.broadcast_to(rescale_ref[pl.ds(path, 1), :], (8, 128))
        for level in range(LEVELS):
            sharers = jnp.int32(0)
            for other in range(size):
                sharers = sharers + jnp.where(ids_ref[other, level] == ids_ref[path, level], 1, 0)
            out_ref[level, i] = rescale / jnp.full((8, 128), sharers, jnp.int32).astype(jnp.float32)


def plan_kernel(here_ref, ids_ref, plan_ref, module_ref):
    size = ids_ref.shape[0]
    order = order_of(size)
    here = here_ref[0]
    for level in range(LEVELS):
        first = level * LEVEL_MODULES
        for module in range(LEVEL_MODULES):
            module_ref[first + module] = -1
        sources = [ids_ref[(origin(here, k, size) // 2) * 2 + half, level] + first for k in order for half in range(2)]
        for i in reversed(range(size)):
            module_ref[sources[i]] = i
        for i in range(size):
            plan_ref[level, i] = module_ref[sources[i]]
        for j, k in enumerate(order):
            for half in range(2):
                module = ids_ref[(target(here, k, size) // 2) * 2 + half, level] + first
                plan_ref[level, size + 2 * j + half] = module
                plan_ref[level, 2 * size + 2 * j + half] = module_ref[module]


def outgoing_kernel(rounds, plan_ref, factor_ref, decayed_ref, *refs):
    received, outs, grad_ref = refs[:rounds], refs[rounds:-1], refs[-1]
    size = 2 * rounds
    for level in range(LEVELS):
        for i in range(size):
            factor = factor_ref[level, i]
            for spot in tiles_of(*grad_ref.shape[2:]):
                grad_ref[(level, i, *spot)] = received[i // 2][(i % 2, level, *spot)] * factor
        for i in range(1, size):
            leader = plan_ref[level, i]

            @pl.when(leader != i)
            def _():
                grad_ref[level, leader] += grad_ref[level, i]

        for i in range(size):
            decayed = decayed_ref[plan_ref[level, size + i]]
            outs[i // 2][i % 2, level] = decayed - grad_coef * grad_ref[level, plan_ref[level, 2 * size + i]]


def state_kernel(module_ref, grad_ref, decayed_ref, momentum_ref, new_params_ref, new_momentum_ref, token_ref):
    token_ref[...] = jnp.zeros_like(token_ref)
    count = new_params_ref.shape[0]
    first = pl.program_id(0) * count
    level = first // LEVEL_MODULES
    for place in range(count):
        module = first + place
        leader = module_ref[module]
        taken = jnp.where(leader < 0, 0.0, 1.0)
        grad = taken * grad_ref[level, jnp.maximum(leader, 0)]
        new_momentum_ref[place] = beta_coef * momentum_ref[module] + grad
        new_params_ref[place] = decayed_ref[module] - grad_coef * grad


def give_back_kernel(size, here_ref, *refs):
    here = here_ref[0]
    for j, k in enumerate(order_of(size)):
        for level in range(LEVELS):
            refs[-1][level, origin(here, k, size) // 2] = refs[j][1 - (here & 1), level]


def own_rows_kernel(size, here_ref, *refs):
    here = here_ref[0]
    core = here & 1
    out_ref, sems = refs[-2:]
    copies = []
    for j, k in enumerate(order_of(size)):
        chip = origin(here, k, size) // 2
        for level in range(LEVELS):
            copies.append(
                pltpu.make_async_copy(refs[j].at[core, level], out_ref.at[level, chip, core], sems.at[level, j])
            )
    for copy in copies:
        copy.start()
    for copy in copies:
        copy.wait()


def other_rows_kernel(here_ref, back_ref, held_ref, out_ref, sems):
    del held_ref
    core = here_ref[0] & 1
    copies = []
    for level in range(LEVELS):
        for chip in range(back_ref.shape[1]):
            copies.append(
                pltpu.make_async_copy(
                    back_ref.at[level, chip], out_ref.at[level, chip, 1 - core], sems.at[level, chip]
                )
            )
    for copy in copies:
        copy.start()
    for copy in copies:
        copy.wait()


def local(path_delta, assign, params, momentum):
    own_slab = path_delta[0]
    size = assign.shape[0]
    module_count, _, own_rows, width = params.shape
    entries = float(own_slab.size * lax.axis_size("shard"))
    state_in = params.reshape(module_count, own_rows, width)
    moment_in = momentum.reshape(module_count, own_rows, width)
    split_slab = own_slab.reshape(LEVELS, size // 2, 2, own_rows, width)
    here = lax.axis_index("path").astype(jnp.int32).reshape(1)
    order = order_of(size)
    rounds = len(order)
    swap = [(i, i ^ 1) for i in range(size)]
    shape = lambda *dims: jax.ShapeDtypeStruct(dims, jnp.float32)
    squares_shape = shape(-(-size // 8) * 8, 128)
    by_chip = shape(LEVELS, rounds, own_rows, width)
    message = shape(2, LEVELS, own_rows, width)

    squares, keep, give = call(pack_kernel, [squares_shape, by_chip, by_chip], [smem, vmem], [vmem] * 3)(
        here, split_slab
    )
    other = lax.ppermute(squares, "path", swap)
    gift = lax.ppermute(give, "path", swap)
    plan, leaders = call(
        plan_kernel,
        [jax.ShapeDtypeStruct((LEVELS, 3 * size), jnp.int32), jax.ShapeDtypeStruct((module_count,), jnp.int32)],
        [smem, smem],
        [smem] * 2,
    )(here, assign)
    squares, *messages = call(
        lambda *refs: merge_kernel(size, *refs),
        [squares_shape] + [message] * rounds,
        [smem, vmem, vmem, vmem, vmem, anywhere],
        [vmem] * (1 + rounds),
    )(here, squares, other, keep, gift, plan)
    received = [move(messages[j], k, size) for j, k in enumerate(order)]
    squares = call(sum_kernel, squares_shape, [vmem] * rounds, vmem)(*[move(squares, k, size) for k in order])
    squares = lax.psum(squares, "shard")
    factors = call(
        lambda *refs: factor_kernel(entries, *refs),
        shape(LEVELS, size, 8, 128),
        [smem, smem, vmem],
        vmem,
        scratch_shapes=[pltpu.VMEM(squares_shape.shape, jnp.float32)],
    )(here, assign, squares)
    decayed = state_in - moment_coef * moment_in

    *outgoing, grad = call(
        lambda *refs: outgoing_kernel(rounds, *refs),
        [message] * rounds + [shape(LEVELS, size, own_rows, width)],
        [smem] + [vmem] * (2 + rounds),
        [vmem] * (rounds + 1),
    )(plan, factors, decayed, *received)
    returned = [move(outgoing[j], k, size) for j, k in enumerate(order)]
    block = LEVEL_MODULES // 2
    state_block = pl.BlockSpec((block, own_rows, width), lambda i: (i, 0, 0))
    new_state, new_moment, done = call(
        state_kernel,
        [shape(*state_in.shape)] * 2 + [shape(8, 128)],
        [smem, vmem, vmem, vmem],
        [state_block, state_block, vmem],
        grid=(module_count // block,),
    )(leaders, grad, decayed, moment_in)
    back = call(
        lambda *refs: give_back_kernel(size, *refs), by_chip, [smem] + [vmem] * rounds + [anywhere], vmem
    )(here, *returned, done)
    back = lax.ppermute(back, "path", swap)
    sems = [pltpu.SemaphoreType.DMA((LEVELS, rounds))]
    path_params = call(
        lambda *refs: own_rows_kernel(size, *refs),
        shape(*split_slab.shape),
        [smem] + [anywhere] * rounds,
        anywhere,
        scratch_shapes=sems,
    )(here, *returned)
    path_params = call(
        other_rows_kernel,
        shape(*split_slab.shape),
        [smem, anywhere, anywhere],
        anywhere,
        scratch_shapes=sems,
        input_output_aliases={2: 0},
    )(here, back, path_params)
    return (path_params.reshape(path_delta.shape), new_state[:, None], new_moment[:, None])


def local_wide(path_delta, assign, params, momentum):
    own_slab = path_delta[0]
    path_count = assign.shape[0]
    module_count, _, own_rows, width = params.shape
    entries = float(own_slab.size * lax.axis_size("shard"))
    total_sq = lax.psum(jnp.sum(own_slab * own_slab), "shard")
    scaled = own_slab * (1.0 / jnp.sqrt(total_sq / entries + 1e-06))
    received = lax.all_to_all(
        scaled.reshape(LEVELS, path_count, own_rows, width), "path", split_axis=1, concat_axis=1, tiled=True
    )
    flat_ids = (assign + LEVEL_MODULES * jnp.arange(LEVELS, dtype=jnp.int32)[None, :]).T.reshape(-1)
    member = (jnp.arange(module_count, dtype=jnp.int32)[:, None] == flat_ids[None, :]).astype(jnp.float32)
    mean = member / jnp.maximum(jnp.sum(member, axis=1), 1.0)[:, None]
    grad = jnp.einsum(
        "mp,prd->mrd", mean, received.reshape(-1, own_rows, width), precision=lax.Precision.HIGHEST
    )
    new_moment = beta_coef * momentum[:, 0] + grad
    new_state = params[:, 0] - outer_rate * (grad + beta_coef * new_moment)
    outgoing = jnp.take(new_state, flat_ids, axis=0).reshape(LEVELS, path_count, own_rows, width)
    returned = lax.all_to_all(outgoing, "path", split_axis=1, concat_axis=1, tiled=True)
    return (returned.reshape(path_delta.shape), new_state[:, None], new_moment[:, None])


def solution(mesh):
    in_specs = (
        P("path", None, "shard", None),
        P(),
        P(None, "shard", "path", None),
        P(None, "shard", "path", None),
    )
    out_specs = (
        P("path", None, "shard", None),
        P(None, "shard", "path", None),
        P(None, "shard", "path", None),
    )
    chosen = local if 4 <= mesh.shape["path"] <= MOST_UNROLLED else local_wide
    return jax.shard_map(chosen, mesh=mesh, in_specs=in_specs, out_specs=out_specs, check_vma=False)
```

```python
import jax
import jax.numpy as jnp
from jax import lax
from jax.experimental import pallas as pl
from jax.experimental.pallas import tpu as pltpu
from jax.sharding import PartitionSpec as P

LEVEL_MODULES = 16
LEVELS = 2
MOST_UNROLLED = 16

outer_rate = 0.7
beta_coef = 0.9
moment_coef = outer_rate * beta_coef * beta_coef
grad_coef = outer_rate * (1.0 + beta_coef)

VMEM_LIMIT = 16 * 1024 * 1024

vmem = pl.BlockSpec(memory_space=pltpu.VMEM)
smem = pl.BlockSpec(memory_space=pltpu.SMEM)
anywhere = pl.BlockSpec(memory_space=pl.ANY)


def call(kernel, out_shape, in_specs, out_specs, **more):
    return pl.pallas_call(
        kernel,
        out_shape=out_shape,
        in_specs=in_specs,
        out_specs=out_specs,
        compiler_params=pltpu.CompilerParams(vmem_limit_bytes=VMEM_LIMIT),
        **more,
    )


def mirrored(k, size):
    if size < 8:
        return k
    return (k & ~6) | ((k & 2) << 1) | ((k & 4) >> 1)


def target(here, k, size):
    if isinstance(here, int):
        return here ^ (mirrored(k, size) if here & 1 else k)
    return here ^ jnp.where(here & 1 == 1, mirrored(k, size), k)


def origin(here, k, size):
    if isinstance(here, int):
        return here ^ (mirrored(k, size) if (here ^ k) & 1 else k)
    return here ^ jnp.where((here ^ k) & 1 == 1, mirrored(k, size), k)


def order_of(size):
    return sorted(range(2, size, 2), key=lambda k: (-bin(k).count("1"), k)) + [0]


def move(array, k, size):
    if k == 0:
        return array
    return lax.ppermute(array, "path", [(i, target(i, k, size)) for i in range(size)])


def tiles_of(rows, width):
    return [(slice(row, row + 8), slice(lane, lane + 128)) for row in range(0, rows, 8) for lane in range(0, width, 128)]


def pack_kernel(here_ref, delta_ref, square_ref, keep_ref, give_ref):
    levels, chips, halves, rows, width = delta_ref.shape

    def pack(core):
        totals = [jnp.zeros((8, 128), jnp.float32) for _ in range(4)]
        for level in range(levels):
            for chip in range(chips):
                for t, spot in enumerate(tiles_of(rows, width)):
                    kept = delta_ref[(level, chip, core, *spot)]
                    given = delta_ref[(level, chip, 1 - core, *spot)]
                    keep_ref[(level, chip, *spot)] = kept
                    give_ref[(level, chip, *spot)] = given
                    totals[t % 4] = totals[t % 4] + (kept * kept + given * given)
        total = jnp.sum((totals[0] + totals[1]) + (totals[2] + totals[3]), axis=0, keepdims=True)
        for first in range(0, square_ref.shape[0], 8):
            row = lax.broadcasted_iota(jnp.int32, (8, 128), 0) + first
            square_ref[first : first + 8] = jnp.where(row == here_ref[0], total, 0.0)

    for core in range(halves):
        pl.when(here_ref[0] & 1 == core)(lambda core=core: pack(core))


def merge_kernel(size, here_ref, keep_ref, gift_ref, token_ref, *outs):
    del token_ref
    here = here_ref[0]
    core = here & 1
    for k, out in zip(order_of(size), outs):
        chip = target(here, k, size) // 2
        for level in range(LEVELS):
            out[core, level] = keep_ref[level, chip]
            out[1 - core, level] = gift_ref[level, chip]


def sum_kernel(*refs):
    total = refs[0][...]
    for ref in refs[1:-1]:
        total = total + ref[...]
    refs[-1][...] = total


def plan_kernel(here_ref, ids_ref, plan_ref, module_ref, token_ref):
    size = ids_ref.shape[1]
    order = order_of(size)
    here = here_ref[0]
    token_ref[...] = jnp.zeros_like(token_ref)
    paths = [(origin(here, k, size) // 2) * 2 + half for k in order for half in range(2)]
    targets = [(target(here, k, size) // 2) * 2 + half for k in order for half in range(2)]
    for level in range(LEVELS):
        first = level * LEVEL_MODULES
        for module in range(LEVEL_MODULES):
            module_ref[first + module] = -1
        sources = [ids_ref[level, path] + first for path in paths]
        for i in reversed(range(size)):
            module_ref[sources[i]] = i
        for i in range(size):
            plan_ref[level, i] = module_ref[sources[i]]
            sharers = jnp.int32(0)
            for other in range(size):
                sharers = sharers + jnp.where(sources[other] == sources[i], 1, 0)
            plan_ref[level, size + i] = sharers
            plan_ref[level, 2 * size + i] = paths[i]
            module = ids_ref[level, targets[i]] + first
            plan_ref[level, 3 * size + i] = module
            plan_ref[level, 4 * size + i] = module_ref[module]


def outgoing_kernel(rounds, entries, plan_ref, square_ref, decayed_ref, *refs):
    received, outs, (grad_ref, rescale_ref) = refs[:rounds], refs[rounds:-2], refs[-2:]
    size = 2 * rounds
    total = jnp.sum(square_ref[...], axis=1, keepdims=True)
    rescale_ref[...] = jnp.broadcast_to(1.0 / jnp.sqrt(total / entries + 1e-06), rescale_ref.shape)
    for level in range(LEVELS):
        for i in range(size):
            rescale = jnp.broadcast_to(rescale_ref[pl.ds(plan_ref[level, 2 * size + i], 1), :], (8, 128))
            factor = rescale / jnp.full((8, 128), plan_ref[level, size + i], jnp.int32).astype(jnp.float32)
            for spot in tiles_of(*grad_ref.shape[2:]):
                grad_ref[(level, i, *spot)] = received[i // 2][(i % 2, level, *spot)] * factor
        for i in range(1, size):
            leader = plan_ref[level, i]

            @pl.when(leader != i)
            def _():
                grad_ref[level, leader] += grad_ref[level, i]

        for i in range(size):
            decayed = decayed_ref[plan_ref[level, 3 * size + i]]
            outs[i // 2][i % 2, level] = decayed - grad_coef * grad_ref[level, plan_ref[level, 4 * size + i]]


def state_kernel(module_ref, grad_ref, decayed_ref, momentum_ref, new_params_ref, new_momentum_ref, token_ref):
    token_ref[...] = jnp.zeros_like(token_ref)
    count = new_params_ref.shape[0]
    first = pl.program_id(0) * count
    level = first // LEVEL_MODULES
    for place in range(count):
        module = first + place
        leader = module_ref[module]
        taken = jnp.where(leader < 0, 0.0, 1.0)
        grad = taken * grad_ref[level, jnp.maximum(leader, 0)]
        new_momentum_ref[place] = beta_coef * momentum_ref[module] + grad
        new_params_ref[place] = decayed_ref[module] - grad_coef * grad


def give_back_kernel(size, here_ref, *refs):
    here = here_ref[0]
    for j, k in enumerate(order_of(size)):
        for level in range(LEVELS):
            refs[-1][level, origin(here, k, size) // 2] = refs[j][1 - (here & 1), level]


def own_rows_kernel(size, here_ref, *refs):
    here = here_ref[0]
    core = here & 1
    out_ref, sems = refs[-2:]
    copies = []
    for j, k in enumerate(order_of(size)):
        chip = origin(here, k, size) // 2
        for level in range(LEVELS):
            copies.append(
                pltpu.make_async_copy(refs[j].at[core, level], out_ref.at[level, chip, core], sems.at[level, j])
            )
    for copy in copies:
        copy.start()
    for copy in copies:
        copy.wait()


def other_rows_kernel(here_ref, back_ref, held_ref, out_ref, sems):
    del held_ref
    core = here_ref[0] & 1
    copies = []
    for level in range(LEVELS):
        for chip in range(back_ref.shape[1]):
            copies.append(
                pltpu.make_async_copy(
                    back_ref.at[level, chip], out_ref.at[level, chip, 1 - core], sems.at[level, chip]
                )
            )
    for copy in copies:
        copy.start()
    for copy in copies:
        copy.wait()


def local(path_delta, assign, params, momentum):
    own_slab = path_delta[0]
    size = assign.shape[0]
    module_count, _, own_rows, width = params.shape
    entries = float(own_slab.size * lax.axis_size("shard"))
    state_in = params.reshape(module_count, own_rows, width)
    moment_in = momentum.reshape(module_count, own_rows, width)
    split_slab = own_slab.reshape(LEVELS, size // 2, 2, own_rows, width)
    here = lax.axis_index("path").astype(jnp.int32).reshape(1)
    order = order_of(size)
    rounds = len(order)
    swap = [(i, i ^ 1) for i in range(size)]
    shape = lambda *dims: jax.ShapeDtypeStruct(dims, jnp.float32)
    squares_shape = shape(-(-size // 8) * 8, 128)
    by_chip = shape(LEVELS, rounds, own_rows, width)
    message = shape(2, LEVELS, own_rows, width)

    squares, keep, give = call(pack_kernel, [squares_shape, by_chip, by_chip], [smem, vmem], [vmem] * 3)(
        here, split_slab
    )
    gift = lax.ppermute(give, "path", swap)
    squares = call(sum_kernel, squares_shape, [vmem] * rounds, vmem)(*[move(squares, k, size) for k in order])
    plan, leaders, planned = call(
        plan_kernel,
        [
            jax.ShapeDtypeStruct((LEVELS, 5 * size), jnp.int32),
            jax.ShapeDtypeStruct((module_count,), jnp.int32),
            shape(8, 128),
        ],
        [smem, smem],
        [smem, smem, vmem],
    )(here, assign.T)
    messages = call(
        lambda *refs: merge_kernel(size, *refs),
        [message] * rounds,
        [smem, vmem, vmem, anywhere],
        [vmem] * rounds,
    )(here, keep, gift, planned)
    received = [move(messages[j], k, size) for j, k in enumerate(order)]
    other = lax.ppermute(squares, "path", swap)
    squares = lax.psum(call(sum_kernel, squares_shape, [vmem] * 2, vmem)(squares, other), "shard")
    decayed = state_in - moment_coef * moment_in

    *outgoing, grad = call(
        lambda *refs: outgoing_kernel(rounds, entries, *refs),
        [message] * rounds + [shape(LEVELS, size, own_rows, width)],
        [smem] + [vmem] * (2 + rounds),
        [vmem] * (rounds + 1),
        scratch_shapes=[pltpu.VMEM(squares_shape.shape, jnp.float32)],
    )(plan, squares, decayed, *received)
    returned = [move(outgoing[j], k, size) for j, k in enumerate(order)]
    block = LEVEL_MODULES // 2
    state_block = pl.BlockSpec((block, own_rows, width), lambda i: (i, 0, 0))
    new_state, new_moment, done = call(
        state_kernel,
        [shape(*state_in.shape)] * 2 + [shape(8, 128)],
        [smem, vmem, vmem, vmem],
        [state_block, state_block, vmem],
        grid=(module_count // block,),
    )(leaders, grad, decayed, moment_in)
    back = call(
        lambda *refs: give_back_kernel(size, *refs), by_chip, [smem] + [vmem] * rounds + [anywhere], vmem
    )(here, *returned, done)
    back = lax.ppermute(back, "path", swap)
    sems = [pltpu.SemaphoreType.DMA((LEVELS, rounds))]
    path_params = call(
        lambda *refs: own_rows_kernel(size, *refs),
        shape(*split_slab.shape),
        [smem] + [anywhere] * rounds,
        anywhere,
        scratch_shapes=sems,
    )(here, *returned)
    path_params = call(
        other_rows_kernel,
        shape(*split_slab.shape),
        [smem, anywhere, anywhere],
        anywhere,
        scratch_shapes=sems,
        input_output_aliases={2: 0},
    )(here, back, path_params)
    return (path_params.reshape(path_delta.shape), new_state[:, None], new_moment[:, None])


def local_wide(path_delta, assign, params, momentum):
    own_slab = path_delta[0]
    path_count = assign.shape[0]
    module_count, _, own_rows, width = params.shape
    entries = float(own_slab.size * lax.axis_size("shard"))
    total_sq = lax.psum(jnp.sum(own_slab * own_slab), "shard")
    scaled = own_slab * (1.0 / jnp.sqrt(total_sq / entries + 1e-06))
    received = lax.all_to_all(
        scaled.reshape(LEVELS, path_count, own_rows, width), "path", split_axis=1, concat_axis=1, tiled=True
    )
    flat_ids = (assign + LEVEL_MODULES * jnp.arange(LEVELS, dtype=jnp.int32)[None, :]).T.reshape(-1)
    member = (jnp.arange(module_count, dtype=jnp.int32)[:, None] == flat_ids[None, :]).astype(jnp.float32)
    mean = member / jnp.maximum(jnp.sum(member, axis=1), 1.0)[:, None]
    grad = jnp.einsum(
        "mp,prd->mrd", mean, received.reshape(-1, own_rows, width), precision=lax.Precision.HIGHEST
    )
    new_moment = beta_coef * momentum[:, 0] + grad
    new_state = params[:, 0] - outer_rate * (grad + beta_coef * new_moment)
    outgoing = jnp.take(new_state, flat_ids, axis=0).reshape(LEVELS, path_count, own_rows, width)
    returned = lax.all_to_all(outgoing, "path", split_axis=1, concat_axis=1, tiled=True)
    return (returned.reshape(path_delta.shape), new_state[:, None], new_moment[:, None])


def solution(mesh):
    in_specs = (
        P("path", None, "shard", None),
        P(),
        P(None, "shard", "path", None),
        P(None, "shard", "path", None),
    )
    out_specs = (
        P("path", None, "shard", None),
        P(None, "shard", "path", None),
        P(None, "shard", "path", None),
    )
    chosen = local if 4 <= mesh.shape["path"] <= MOST_UNROLLED else local_wide
    return jax.shard_map(chosen, mesh=mesh, in_specs=in_specs, out_specs=out_specs, check_vma=False)
```

```python
import jax
import jax.numpy as jnp
from jax import lax
from jax.experimental import pallas as pl
from jax.experimental.pallas import tpu as pltpu
from jax.sharding import PartitionSpec as P

LEVEL_MODULES = 16
LEVELS = 2
MOST_UNROLLED = 16

outer_rate = 0.7
beta_coef = 0.9
moment_coef = outer_rate * beta_coef * beta_coef
grad_coef = outer_rate * (1.0 + beta_coef)

VMEM_LIMIT = 16 * 1024 * 1024

vmem = pl.BlockSpec(memory_space=pltpu.VMEM)
smem = pl.BlockSpec(memory_space=pltpu.SMEM)
anywhere = pl.BlockSpec(memory_space=pl.ANY)


def call(kernel, out_shape, in_specs, out_specs, **more):
    return pl.pallas_call(
        kernel,
        out_shape=out_shape,
        in_specs=in_specs,
        out_specs=out_specs,
        compiler_params=pltpu.CompilerParams(vmem_limit_bytes=VMEM_LIMIT),
        **more,
    )


def mirrored(k, size):
    if size < 8:
        return k
    return (k & ~6) | ((k & 2) << 1) | ((k & 4) >> 1)


def target(here, k, size):
    if isinstance(here, int):
        return here ^ (mirrored(k, size) if here & 1 else k)
    return here ^ jnp.where(here & 1 == 1, mirrored(k, size), k)


def origin(here, k, size):
    if isinstance(here, int):
        return here ^ (mirrored(k, size) if (here ^ k) & 1 else k)
    return here ^ jnp.where((here ^ k) & 1 == 1, mirrored(k, size), k)


def order_of(size):
    return sorted(range(2, size, 2), key=lambda k: (-bin(k).count("1"), k)) + [0]


def move(array, k, size):
    if k == 0:
        return array
    return lax.ppermute(array, "path", [(i, target(i, k, size)) for i in range(size)])


def tiles_of(rows, width):
    return [(slice(row, row + 8), slice(lane, lane + 128)) for row in range(0, rows, 8) for lane in range(0, width, 128)]


def pack_kernel(here_ref, delta_ref, square_ref, keep_ref, give_ref):
    levels, chips, halves, rows, width = delta_ref.shape

    def pack(core):
        totals = [jnp.zeros((8, 128), jnp.float32) for _ in range(4)]
        for level in range(levels):
            for chip in range(chips):
                for t, spot in enumerate(tiles_of(rows, width)):
                    kept = delta_ref[(level, chip, core, *spot)]
                    given = delta_ref[(level, chip, 1 - core, *spot)]
                    keep_ref[(level, chip, *spot)] = kept
                    give_ref[(level, chip, *spot)] = given
                    totals[t % 4] = totals[t % 4] + (kept * kept + given * given)
        total = jnp.sum((totals[0] + totals[1]) + (totals[2] + totals[3]), axis=0, keepdims=True)
        for first in range(0, square_ref.shape[0], 8):
            row = lax.broadcasted_iota(jnp.int32, (8, 128), 0) + first
            square_ref[first : first + 8] = jnp.where(row == here_ref[0], total, 0.0)

    for core in range(halves):
        pl.when(here_ref[0] & 1 == core)(lambda core=core: pack(core))


def scale_kernel(entries, here_ref, plan_ref, square_ref, other_ref, keep_ref, gift_ref, *refs):
    outs, rescale_ref = refs[:-1], refs[-1]
    here = here_ref[0]
    core = here & 1
    rounds = len(outs) // LEVELS
    size = 2 * rounds
    total = jnp.sum(square_ref[...] + other_ref[...], axis=1, keepdims=True)
    rescale_ref[...] = jnp.broadcast_to(1.0 / jnp.sqrt(total / entries + 1e-06), rescale_ref.shape)
    for half, (rows_ref, source) in enumerate(((keep_ref, core), (gift_ref, 1 - core))):
        rescale = jnp.broadcast_to(rescale_ref[pl.ds((here // 2) * 2 + source, 1), :], (8, 128))
        for level in range(LEVELS):
            sharers = plan_ref[level, 2 * size - 2 + source]
            factor = rescale / jnp.full((8, 128), sharers, jnp.int32).astype(jnp.float32)
            for j, k in enumerate(order_of(size)):
                out = outs[level * rounds + j]
                chip = target(here, k, size) // 2
                for spot in tiles_of(*out.shape[1:]):
                    out[(source, *spot)] = rows_ref[(level, chip, *spot)] * factor


def sum_kernel(*refs):
    total = refs[0][...]
    for ref in refs[1:-1]:
        total = total + ref[...]
    refs[-1][...] = total


def plan_kernel(here_ref, ids_ref, plan_ref, module_ref, token_ref):
    size = ids_ref.shape[1]
    order = order_of(size)
    here = here_ref[0]
    token_ref[...] = jnp.zeros_like(token_ref)
    paths = [(origin(here, k, size) // 2) * 2 + half for k in order for half in range(2)]
    targets = [(target(here, k, size) // 2) * 2 + half for k in order for half in range(2)]
    for level in range(LEVELS):
        first = level * LEVEL_MODULES
        for module in range(LEVEL_MODULES):
            module_ref[first + module] = -1
        sources = [ids_ref[level, path] + first for path in paths]
        for i in reversed(range(size)):
            module_ref[sources[i]] = i
        for i in range(size):
            plan_ref[level, i] = module_ref[sources[i]]
            sharers = jnp.int32(0)
            for other in range(size):
                sharers = sharers + jnp.where(sources[other] == sources[i], 1, 0)
            plan_ref[level, size + i] = sharers
            plan_ref[level, 2 * size + i] = paths[i]
            module = ids_ref[level, targets[i]] + first
            plan_ref[level, 3 * size + i] = module
            plan_ref[level, 4 * size + i] = module_ref[module]


def outgoing_kernel(level, rounds, plan_ref, decayed_ref, *refs):
    received, outs, grad_ref = refs[:rounds], refs[rounds:-1], refs[-1]
    size = 2 * rounds
    for i in range(size):
        grad_ref[i] = received[i // 2][i % 2]
    for i in range(1, size):
        leader = plan_ref[level, i]

        @pl.when(leader != i)
        def _():
            grad_ref[leader] += grad_ref[i]

    for i in range(size):
        decayed = decayed_ref[plan_ref[level, 3 * size + i]]
        outs[i // 2][i % 2] = decayed - grad_coef * grad_ref[plan_ref[level, 4 * size + i]]


def state_kernel(module_ref, *refs):
    grads, (decayed_ref, momentum_ref, new_params_ref, new_momentum_ref, token_ref) = refs[:LEVELS], refs[LEVELS:]
    token_ref[...] = jnp.zeros_like(token_ref)
    count = new_params_ref.shape[0]
    first = pl.program_id(0) * count

    def update(grad_ref):
        for place in range(count):
            module = first + place
            leader = module_ref[module]
            taken = jnp.where(leader < 0, 0.0, 1.0)
            grad = taken * grad_ref[jnp.maximum(leader, 0)]
            new_momentum_ref[place] = beta_coef * momentum_ref[module] + grad
            new_params_ref[place] = decayed_ref[module] - grad_coef * grad

    for level, grad_ref in enumerate(grads):
        pl.when(first // LEVEL_MODULES == level)(lambda grad_ref=grad_ref: update(grad_ref))


def give_back_kernel(size, here_ref, *refs):
    here = here_ref[0]
    for j, k in enumerate(order_of(size)):
        refs[-1][origin(here, k, size) // 2] = refs[j][1 - (here & 1)]


def own_rows_kernel(size, here_ref, *refs):
    order = order_of(size)
    here = here_ref[0]
    core = here & 1
    out_ref, sems = refs[-2:]
    copies = []
    for level in range(LEVELS):
        for j, k in enumerate(order):
            chip = origin(here, k, size) // 2
            block = refs[level * len(order) + j]
            copies.append(pltpu.make_async_copy(block.at[core], out_ref.at[level, chip, core], sems.at[level, j]))
    for copy in copies:
        copy.start()
    for copy in copies:
        copy.wait()


def other_rows_kernel(here_ref, *refs):
    out_ref, sems = refs[-2:]
    core = here_ref[0] & 1
    copies = []
    for level in range(LEVELS):
        for chip in range(refs[level].shape[0]):
            copies.append(
                pltpu.make_async_copy(
                    refs[level].at[chip], out_ref.at[level, chip, 1 - core], sems.at[level, chip]
                )
            )
    for copy in copies:
        copy.start()
    for copy in copies:
        copy.wait()


def local(path_delta, assign, params, momentum):
    own_slab = path_delta[0]
    size = assign.shape[0]
    module_count, _, own_rows, width = params.shape
    shards = lax.axis_size("shard")
    entries = float(own_slab.size * shards)
    state_in = params.reshape(module_count, own_rows, width)
    moment_in = momentum.reshape(module_count, own_rows, width)
    split_slab = own_slab.reshape(LEVELS, size // 2, 2, own_rows, width)
    here = lax.axis_index("path").astype(jnp.int32).reshape(1)
    order = order_of(size)
    rounds = len(order)
    swap = [(i, i ^ 1) for i in range(size)]
    shape = lambda *dims: jax.ShapeDtypeStruct(dims, jnp.float32)
    squares_shape = shape(-(-size // 8) * 8, 128)
    by_chip = shape(LEVELS, rounds, own_rows, width)
    message = shape(2, own_rows, width)

    squares, keep, give = call(pack_kernel, [squares_shape, by_chip, by_chip], [smem, vmem], [vmem] * 3)(
        here, split_slab
    )
    gift = lax.ppermute(give, "path", swap)
    tiles = [squares] + [
        lax.ppermute(squares, "shard", [(i, i ^ step) for i in range(shards)]) for step in range(shards - 1, 0, -1)
    ]
    squares = call(sum_kernel, squares_shape, [vmem] * shards, vmem)(*tiles)
    other = lax.ppermute(squares, "path", swap)
    plan, leaders, planned = call(
        plan_kernel,
        [
            jax.ShapeDtypeStruct((LEVELS, 5 * size), jnp.int32),
            jax.ShapeDtypeStruct((module_count,), jnp.int32),
            shape(8, 128),
        ],
        [smem, smem],
        [smem, smem, vmem],
    )(here, assign.T)
    messages = call(
        lambda *refs: scale_kernel(entries, *refs),
        [message] * (LEVELS * rounds),
        [smem, smem, vmem, vmem, vmem, vmem],
        [vmem] * (LEVELS * rounds),
        scratch_shapes=[pltpu.VMEM(squares_shape.shape, jnp.float32)],
    )(here, plan, squares, other, keep, gift)
    decayed = state_in - moment_coef * moment_in

    returned, grads = [], []
    for level in range(LEVELS):
        received = [move(messages[level * rounds + j], k, size) for j, k in enumerate(order)]
        *outgoing, grad = call(
            lambda *refs, level=level: outgoing_kernel(level, rounds, *refs),
            [message] * rounds + [shape(size, own_rows, width)],
            [smem] + [vmem] * (1 + rounds),
            [vmem] * (rounds + 1),
        )(plan, decayed, *received)
        returned.append([move(outgoing[j], k, size) for j, k in enumerate(order)])
        grads.append(grad)

    block = LEVEL_MODULES // 2
    state_block = pl.BlockSpec((block, own_rows, width), lambda i: (i, 0, 0))
    new_state, new_moment, done = call(
        state_kernel,
        [shape(*state_in.shape)] * 2 + [shape(8, 128)],
        [smem] + [vmem] * (LEVELS + 2),
        [state_block, state_block, vmem],
        grid=(module_count // block,),
    )(leaders, *grads, decayed, moment_in)

    backs = []
    for level in range(LEVELS):
        before = [done] if level == LEVELS - 1 else []
        back = call(
            lambda *refs: give_back_kernel(size, *refs),
            shape(rounds, own_rows, width),
            [smem] + [vmem] * rounds + [anywhere] * len(before),
            vmem,
        )(here, *returned[level], *before)
        backs.append(lax.ppermute(back, "path", swap))
    sems = [pltpu.SemaphoreType.DMA((LEVELS, rounds))]
    path_params = call(
        lambda *refs: own_rows_kernel(size, *refs),
        shape(*split_slab.shape),
        [smem] + [anywhere] * (LEVELS * rounds),
        anywhere,
        scratch_shapes=sems,
    )(here, *returned[0], *returned[1])
    path_params = call(
        other_rows_kernel,
        shape(*split_slab.shape),
        [smem] + [anywhere] * (LEVELS + 1),
        anywhere,
        scratch_shapes=sems,
        input_output_aliases={LEVELS + 1: 0},
    )(here, *backs, path_params)
    return (path_params.reshape(path_delta.shape), new_state[:, None], new_moment[:, None])


def local_wide(path_delta, assign, params, momentum):
    own_slab = path_delta[0]
    path_count = assign.shape[0]
    module_count, _, own_rows, width = params.shape
    entries = float(own_slab.size * lax.axis_size("shard"))
    total_sq = lax.psum(jnp.sum(own_slab * own_slab), "shard")
    scaled = own_slab * (1.0 / jnp.sqrt(total_sq / entries + 1e-06))
    received = lax.all_to_all(
        scaled.reshape(LEVELS, path_count, own_rows, width), "path", split_axis=1, concat_axis=1, tiled=True
    )
    flat_ids = (assign + LEVEL_MODULES * jnp.arange(LEVELS, dtype=jnp.int32)[None, :]).T.reshape(-1)
    member = (jnp.arange(module_count, dtype=jnp.int32)[:, None] == flat_ids[None, :]).astype(jnp.float32)
    mean = member / jnp.maximum(jnp.sum(member, axis=1), 1.0)[:, None]
    grad = jnp.einsum(
        "mp,prd->mrd", mean, received.reshape(-1, own_rows, width), precision=lax.Precision.HIGHEST
    )
    new_moment = beta_coef * momentum[:, 0] + grad
    new_state = params[:, 0] - outer_rate * (grad + beta_coef * new_moment)
    outgoing = jnp.take(new_state, flat_ids, axis=0).reshape(LEVELS, path_count, own_rows, width)
    returned = lax.all_to_all(outgoing, "path", split_axis=1, concat_axis=1, tiled=True)
    return (returned.reshape(path_delta.shape), new_state[:, None], new_moment[:, None])


def solution(mesh):
    in_specs = (
        P("path", None, "shard", None),
        P(),
        P(None, "shard", "path", None),
        P(None, "shard", "path", None),
    )
    out_specs = (
        P("path", None, "shard", None),
        P(None, "shard", "path", None),
        P(None, "shard", "path", None),
    )
    chosen = local if 4 <= mesh.shape["path"] <= MOST_UNROLLED else local_wide
    return jax.shard_map(chosen, mesh=mesh, in_specs=in_specs, out_specs=out_specs, check_vma=False)
```

```python
import jax
import jax.numpy as jnp
from jax import lax
from jax.experimental import pallas as pl
from jax.experimental.pallas import tpu as pltpu
from jax.sharding import PartitionSpec as P

LEVEL_MODULES = 16
LEVELS = 2
MOST_UNROLLED = 8

outer_rate = 0.7
beta_coef = 0.9
moment_coef = outer_rate * beta_coef * beta_coef
grad_coef = outer_rate * (1.0 + beta_coef)

VMEM_LIMIT = 16 * 1024 * 1024

vmem = pl.BlockSpec(memory_space=pltpu.VMEM)
smem = pl.BlockSpec(memory_space=pltpu.SMEM)
anywhere = pl.BlockSpec(memory_space=pl.ANY)


def call(kernel, out_shape, in_specs, out_specs, **more):
    return pl.pallas_call(
        kernel,
        out_shape=out_shape,
        in_specs=in_specs,
        out_specs=out_specs,
        compiler_params=pltpu.CompilerParams(vmem_limit_bytes=VMEM_LIMIT),
        **more,
    )


def mirrored(k, size):
    if size < 8:
        return k
    return (k & ~6) | ((k & 2) << 1) | ((k & 4) >> 1)


def target(here, k, size):
    if isinstance(here, int):
        return here ^ (mirrored(k, size) if here & 1 else k)
    return here ^ jnp.where(here & 1 == 1, mirrored(k, size), k)


def origin(here, k, size):
    if isinstance(here, int):
        return here ^ (mirrored(k, size) if (here ^ k) & 1 else k)
    return here ^ jnp.where((here ^ k) & 1 == 1, mirrored(k, size), k)


def order_of(size):
    return sorted(range(2, size, 2), key=lambda k: (-bin(k).count("1"), k)) + [0]


def move(array, k, size):
    if k == 0:
        return array
    return lax.ppermute(array, "path", [(i, target(i, k, size)) for i in range(size)])


def tiles_of(rows, width):
    return [(slice(row, row + 8), slice(lane, lane + 128)) for row in range(0, rows, 8) for lane in range(0, width, 128)]


def pack_kernel(size, here_ref, delta_ref, square_ref, *outs):
    order = order_of(size)
    totals = [jnp.zeros((8, 128), jnp.float32) for _ in range(4)]
    for level in range(LEVELS):
        for j, k in enumerate(order):
            out = outs[level * len(order) + j]
            chip = target(here_ref[0], k, size) // 2
            for half in range(2):
                for t, spot in enumerate(tiles_of(*out.shape[1:])):
                    block = delta_ref[(level, chip, half, *spot)]
                    out[(half, *spot)] = block
                    totals[t % 4] = totals[t % 4] + block * block
    square_ref[...] = (totals[0] + totals[1]) + (totals[2] + totals[3])


def scale_kernel(entries, here_ref, plan_ref, square_ref, *refs):
    count = len(refs) // 2
    rounds = count // LEVELS
    give_ref = refs[-1]
    core = here_ref[0] & 1
    total = jnp.broadcast_to(jnp.sum(square_ref[...], keepdims=True), (8, 128))
    rescale = 1.0 / jnp.sqrt(total / entries + 1e-06)
    for level in range(LEVELS):
        sharers = plan_ref[level, 2 * rounds + rounds - 1]
        factor = rescale / jnp.full((8, 128), sharers, jnp.int32).astype(jnp.float32)
        for j in range(level * rounds, (level + 1) * rounds):
            for half in range(2):
                for spot in tiles_of(*refs[j].shape[1:]):
                    refs[count + j][(half, *spot)] = refs[j][(half, *spot)] * factor
        give_ref[level] = refs[count + (level + 1) * rounds - 1][1 - core]


def sum_kernel(count, *refs):
    total = refs[0][...]
    for ref in refs[1:count]:
        total = total + ref[...]
    refs[-1][...] = total


def plan_kernel(here_ref, ids_ref, plan_ref, module_ref, token_ref):
    size = ids_ref.shape[1]
    order = order_of(size)
    here = here_ref[0]
    token_ref[...] = jnp.zeros_like(token_ref)
    paths = [origin(core, k, size) for core in (here, here ^ 1) for k in order]
    targets = [(target(here, k, size) // 2) * 2 + half for k in order for half in range(2)]
    for level in range(LEVELS):
        first = level * LEVEL_MODULES
        for module in range(LEVEL_MODULES):
            module_ref[first + module] = -1
        sources = [ids_ref[level, path] + first for path in paths]
        for i in reversed(range(size)):
            module_ref[sources[i]] = i
        for i in range(size):
            plan_ref[level, i] = module_ref[sources[i]]
            sharers = jnp.int32(0)
            for other in range(size):
                sharers = sharers + jnp.where(sources[other] == sources[i], 1, 0)
            plan_ref[level, size + i] = sharers
            plan_ref[level, 2 * size + i] = paths[i]
            module = ids_ref[level, targets[i]] + first
            plan_ref[level, 3 * size + i] = module
            plan_ref[level, 4 * size + i] = module_ref[module]


def give_kernel(here_ref, *refs):
    outs = refs[-2:]
    for j, block in enumerate(refs[:-2]):
        for part, out in enumerate(outs):
            out[j] = block[1 - (here_ref[0] & 1), part * out.shape[1] : (part + 1) * out.shape[1]]


def outgoing_kernel(level, rounds, here_ref, plan_ref, decayed_ref, own_ref, *refs):
    received, parts, outs, grad_ref = refs[:rounds], refs[rounds : rounds + 2], refs[rounds + 2 : -1], refs[-1]
    size = 2 * rounds
    core = here_ref[0] & 1
    for j in range(rounds):
        grad_ref[j] = received[j][core]
    for j in range(rounds - 1):
        for part, ref in enumerate(parts):
            grad_ref[rounds + j, part * ref.shape[1] : (part + 1) * ref.shape[1]] = ref[j]
    grad_ref[size - 1] = own_ref[level]
    for i in range(1, size):
        leader = plan_ref[level, i]

        @pl.when(leader != i)
        def _():
            grad_ref[leader] += grad_ref[i]

    for i in range(size):
        decayed = decayed_ref[plan_ref[level, 3 * size + i]]
        outs[i // 2][i % 2] = decayed - grad_coef * grad_ref[plan_ref[level, 4 * size + i]]


def state_kernel(module_ref, *refs):
    grads, (decayed_ref, momentum_ref, new_params_ref, new_momentum_ref, token_ref) = refs[:LEVELS], refs[LEVELS:]
    token_ref[...] = jnp.zeros_like(token_ref)
    count = new_params_ref.shape[0]
    first = pl.program_id(0) * count

    def update(grad_ref):
        for place in range(count):
            module = first + place
            leader = module_ref[module]
            taken = jnp.where(leader < 0, 0.0, 1.0)
            grad = taken * grad_ref[jnp.maximum(leader, 0)]
            new_momentum_ref[place] = beta_coef * momentum_ref[module] + grad
            new_params_ref[place] = decayed_ref[module] - grad_coef * grad

    for level, grad_ref in enumerate(grads):
        pl.when(first // LEVEL_MODULES == level)(lambda grad_ref=grad_ref: update(grad_ref))


def give_back_kernel(size, here_ref, *refs):
    here = here_ref[0]
    for j, k in enumerate(order_of(size)):
        refs[-1][origin(here, k, size) // 2] = refs[j][1 - (here & 1)]


def own_rows_kernel(size, here_ref, *refs):
    order = order_of(size)
    here = here_ref[0]
    core = here & 1
    out_ref, sems = refs[-2:]
    copies = []
    for level in range(LEVELS):
        for j, k in enumerate(order):
            chip = origin(here, k, size) // 2
            block = refs[level * len(order) + j]
            copies.append(pltpu.make_async_copy(block.at[core], out_ref.at[level, chip, core], sems.at[level, j]))
    for copy in copies:
        copy.start()
    for copy in copies:
        copy.wait()


def other_rows_kernel(here_ref, *refs):
    out_ref, sems = refs[-2:]
    core = here_ref[0] & 1
    copies = []
    for level in range(LEVELS):
        for chip in range(refs[level].shape[0]):
            copies.append(
                pltpu.make_async_copy(
                    refs[level].at[chip], out_ref.at[level, chip, 1 - core], sems.at[level, chip]
                )
            )
    for copy in copies:
        copy.start()
    for copy in copies:
        copy.wait()


def local(path_delta, assign, params, momentum):
    own_slab = path_delta[0]
    size = assign.shape[0]
    module_count, _, own_rows, width = params.shape
    shards = lax.axis_size("shard")
    entries = float(own_slab.size * shards)
    state_in = params.reshape(module_count, own_rows, width)
    moment_in = momentum.reshape(module_count, own_rows, width)
    split_slab = own_slab.reshape(LEVELS, size // 2, 2, own_rows, width)
    here = lax.axis_index("path").astype(jnp.int32).reshape(1)
    order = order_of(size)
    rounds = len(order)
    swap = [(i, i ^ 1) for i in range(size)]
    shape = lambda *dims: jax.ShapeDtypeStruct(dims, jnp.float32)
    squares_shape = shape(8, 128)
    message = shape(2, own_rows, width)

    squares, *raw = call(
        lambda *refs: pack_kernel(size, *refs),
        [squares_shape] + [message] * (LEVELS * rounds),
        [smem, vmem],
        [vmem] * (1 + LEVELS * rounds),
    )(here, split_slab)
    plan, leaders, planned = call(
        plan_kernel,
        [
            jax.ShapeDtypeStruct((LEVELS, 5 * size), jnp.int32),
            jax.ShapeDtypeStruct((module_count,), jnp.int32),
            shape(8, 128),
        ],
        [smem, smem],
        [smem, smem, vmem],
    )(here, assign.T)
    tiles = [squares] + [
        lax.ppermute(squares, "shard", [(i, i ^ step) for i in range(shards)]) for step in range(shards - 1, 0, -1)
    ]
    squares = call(
        lambda *refs: sum_kernel(shards, *refs), squares_shape, [vmem] * shards + [anywhere], vmem
    )(*tiles, planned)
    *messages, give = call(
        lambda *refs: scale_kernel(entries, *refs),
        [message] * (LEVELS * rounds) + [shape(LEVELS, own_rows, width)],
        [smem, smem] + [vmem] * (1 + LEVELS * rounds),
        [vmem] * (LEVELS * rounds + 1),
    )(here, plan, squares, *raw)
    own = lax.ppermute(give, "path", swap)
    decayed = state_in - moment_coef * moment_in

    returned, grads = [], []
    for level in range(LEVELS):
        received = [move(messages[level * rounds + j], k, size) for j, k in enumerate(order)]
        parts = call(
            give_kernel, [shape(rounds - 1, own_rows // 2, width)] * 2, [smem] + [vmem] * (rounds - 1), [vmem] * 2
        )(here, *received[:-1])
        parts = [lax.ppermute(part, "path", swap) for part in parts]
        *outgoing, grad = call(
            lambda *refs, level=level: outgoing_kernel(level, rounds, *refs),
            [message] * rounds + [shape(size, own_rows, width)],
            [smem, smem] + [vmem] * (4 + rounds),
            [vmem] * (rounds + 1),
        )(here, plan, decayed, own, *received, *parts)
        returned.append([move(outgoing[j], k, size) for j, k in enumerate(order)])
        grads.append(grad)

    block = LEVEL_MODULES // 2
    state_block = pl.BlockSpec((block, own_rows, width), lambda i: (i, 0, 0))
    new_state, new_moment, done = call(
        state_kernel,
        [shape(*state_in.shape)] * 2 + [shape(8, 128)],
        [smem] + [vmem] * (LEVELS + 2),
        [state_block, state_block, vmem],
        grid=(module_count // block,),
    )(leaders, *grads, decayed, moment_in)

    backs = []
    for level in range(LEVELS):
        before = [done] if level == LEVELS - 1 else []
        back = call(
            lambda *refs: give_back_kernel(size, *refs),
            shape(rounds, own_rows, width),
            [smem] + [vmem] * rounds + [anywhere] * len(before),
            vmem,
        )(here, *returned[level], *before)
        backs.append(lax.ppermute(back, "path", swap))
    sems = [pltpu.SemaphoreType.DMA((LEVELS, rounds))]
    path_params = call(
        lambda *refs: own_rows_kernel(size, *refs),
        shape(*split_slab.shape),
        [smem] + [anywhere] * (LEVELS * rounds),
        anywhere,
        scratch_shapes=sems,
    )(here, *returned[0], *returned[1])
    path_params = call(
        other_rows_kernel,
        shape(*split_slab.shape),
        [smem] + [anywhere] * (LEVELS + 1),
        anywhere,
        scratch_shapes=sems,
        input_output_aliases={LEVELS + 1: 0},
    )(here, *backs, path_params)
    return (path_params.reshape(path_delta.shape), new_state[:, None], new_moment[:, None])


def local_wide(path_delta, assign, params, momentum):
    own_slab = path_delta[0]
    path_count = assign.shape[0]
    module_count, _, own_rows, width = params.shape
    entries = float(own_slab.size * lax.axis_size("shard"))
    total_sq = lax.psum(jnp.sum(own_slab * own_slab), "shard")
    scaled = own_slab * (1.0 / jnp.sqrt(total_sq / entries + 1e-06))
    received = lax.all_to_all(
        scaled.reshape(LEVELS, path_count, own_rows, width), "path", split_axis=1, concat_axis=1, tiled=True
    )
    flat_ids = (assign + LEVEL_MODULES * jnp.arange(LEVELS, dtype=jnp.int32)[None, :]).T.reshape(-1)
    member = (jnp.arange(module_count, dtype=jnp.int32)[:, None] == flat_ids[None, :]).astype(jnp.float32)
    mean = member / jnp.maximum(jnp.sum(member, axis=1), 1.0)[:, None]
    grad = jnp.einsum(
        "mp,prd->mrd", mean, received.reshape(-1, own_rows, width), precision=lax.Precision.HIGHEST
    )
    new_moment = beta_coef * momentum[:, 0] + grad
    new_state = params[:, 0] - outer_rate * (grad + beta_coef * new_moment)
    outgoing = jnp.take(new_state, flat_ids, axis=0).reshape(LEVELS, path_count, own_rows, width)
    returned = lax.all_to_all(outgoing, "path", split_axis=1, concat_axis=1, tiled=True)
    return (returned.reshape(path_delta.shape), new_state[:, None], new_moment[:, None])


def solution(mesh):
    in_specs = (
        P("path", None, "shard", None),
        P(),
        P(None, "shard", "path", None),
        P(None, "shard", "path", None),
    )
    out_specs = (
        P("path", None, "shard", None),
        P(None, "shard", "path", None),
        P(None, "shard", "path", None),
    )
    chosen = local if 4 <= mesh.shape["path"] <= MOST_UNROLLED else local_wide
    return jax.shard_map(chosen, mesh=mesh, in_specs=in_specs, out_specs=out_specs, check_vma=False)
```

```python
import jax
import jax.numpy as jnp
from jax import lax
from jax.experimental import pallas as pl
from jax.experimental.pallas import tpu as pltpu
from jax.sharding import PartitionSpec as P

LEVEL_MODULES = 16
LEVELS = 2
MOST_UNROLLED = 8

outer_rate = 0.7
beta_coef = 0.9
moment_coef = outer_rate * beta_coef * beta_coef
grad_coef = outer_rate * (1.0 + beta_coef)

VMEM_LIMIT = 16 * 1024 * 1024

vmem = pl.BlockSpec(memory_space=pltpu.VMEM)
smem = pl.BlockSpec(memory_space=pltpu.SMEM)
anywhere = pl.BlockSpec(memory_space=pl.ANY)


def call(kernel, out_shape, in_specs, out_specs, **more):
    return pl.pallas_call(
        kernel,
        out_shape=out_shape,
        in_specs=in_specs,
        out_specs=out_specs,
        compiler_params=pltpu.CompilerParams(vmem_limit_bytes=VMEM_LIMIT),
        **more,
    )


def mirrored(k, size):
    if size < 8:
        return k
    return (k & ~6) | ((k & 2) << 1) | ((k & 4) >> 1)


def target(here, k, size):
    if isinstance(here, int):
        return here ^ (mirrored(k, size) if here & 1 else k)
    return here ^ jnp.where(here & 1 == 1, mirrored(k, size), k)


def origin(here, k, size):
    if isinstance(here, int):
        return here ^ (mirrored(k, size) if (here ^ k) & 1 else k)
    return here ^ jnp.where((here ^ k) & 1 == 1, mirrored(k, size), k)


def order_of(size):
    return sorted(range(2, size, 2), key=lambda k: (-bin(k).count("1"), k)) + [0]


def move(array, k, size):
    if k == 0:
        return array
    return lax.ppermute(array, "path", [(i, target(i, k, size)) for i in range(size)])


def tiles_of(rows, width):
    return [(slice(row, row + 8), slice(lane, lane + 128)) for row in range(0, rows, 8) for lane in range(0, width, 128)]


def pack_kernel(here_ref, delta_ref, square_ref, keep_ref, give_ref):
    levels, chips, halves, rows, width = delta_ref.shape

    def pack(core):
        totals = [jnp.zeros((8, 128), jnp.float32) for _ in range(4)]
        for level in range(levels):
            for chip in range(chips):
                for t, spot in enumerate(tiles_of(rows, width)):
                    kept = delta_ref[(level, chip, core, *spot)]
                    given = delta_ref[(level, chip, 1 - core, *spot)]
                    keep_ref[(level, chip, *spot)] = kept
                    give_ref[(level, chip, *spot)] = given
                    totals[t % 4] = totals[t % 4] + (kept * kept + given * given)
        total = jnp.sum((totals[0] + totals[1]) + (totals[2] + totals[3]), axis=0, keepdims=True)
        for first in range(0, square_ref.shape[0], 8):
            row = lax.broadcasted_iota(jnp.int32, (8, 128), 0) + first
            square_ref[first : first + 8] = jnp.where(row == here_ref[0], total, 0.0)

    for core in range(halves):
        pl.when(here_ref[0] & 1 == core)(lambda core=core: pack(core))


def first_merge_kernel(size, here_ref, keep_ref, gift_ref, *outs):
    here = here_ref[0]
    core = here & 1
    for k, out in zip(order_of(size), outs):
        chip = target(here, k, size) // 2
        rows = keep_ref.shape[2]
        for source, ref in ((core, keep_ref), (1 - core, gift_ref)):
            out[source, :rows] = ref[0, chip]
            out[source, rows:] = ref[1, chip, : rows // 2]


def second_merge_kernel(size, here_ref, square_ref, other_ref, keep_ref, gift_ref, *outs):
    here = here_ref[0]
    core = here & 1
    squares = square_ref[...] + other_ref[...]
    _, _, rows, width = keep_ref.shape
    spots = tiles_of(rows, width)[-(rows * width // 2048) :]
    for k, out in zip(order_of(size), outs):
        chip = target(here, k, size) // 2
        for source, ref in ((core, keep_ref), (1 - core, gift_ref)):
            for t, spot in enumerate(spots):
                out[source * len(spots) + t] = ref[(1, chip, *spot)]
        out[2 * len(spots)] = squares


def sum_kernel(count, *refs):
    total = refs[0][...]
    for ref in refs[1:count]:
        total = total + ref[...]
    refs[-1][...] = total


def plan_kernel(here_ref, ids_ref, plan_ref, module_ref, token_ref):
    size = ids_ref.shape[1]
    order = order_of(size)
    here = here_ref[0]
    token_ref[...] = jnp.zeros_like(token_ref)
    paths = [(origin(here, k, size) // 2) * 2 + half for k in order for half in range(2)]
    targets = [(target(here, k, size) // 2) * 2 + half for k in order for half in range(2)]
    for level in range(LEVELS):
        first = level * LEVEL_MODULES
        for module in range(LEVEL_MODULES):
            module_ref[first + module] = -1
        sources = [ids_ref[level, path] + first for path in paths]
        for i in reversed(range(size)):
            module_ref[sources[i]] = i
        for i in range(size):
            plan_ref[level, i] = module_ref[sources[i]]
            sharers = jnp.int32(0)
            for other in range(size):
                sharers = sharers + jnp.where(sources[other] == sources[i], 1, 0)
            plan_ref[level, size + i] = sharers
            plan_ref[level, 2 * size + i] = paths[i]
            module = ids_ref[level, targets[i]] + first
            plan_ref[level, 3 * size + i] = module
            plan_ref[level, 4 * size + i] = module_ref[module]


def outgoing_kernel(rounds, entries, plan_ref, decayed_ref, *refs):
    firsts, seconds = refs[:rounds], refs[rounds : 2 * rounds]
    outs, (grad_ref, rescale_ref) = refs[2 * rounds : -2], refs[-2:]
    size = 2 * rounds
    rows, width = grad_ref.shape[2:]
    spots = tiles_of(rows, width)
    half = len(spots) // 2
    squares = seconds[0][2 * half]
    for second in seconds[1:]:
        squares = squares + second[2 * half]
    total = jnp.sum(squares, axis=1, keepdims=True)
    rescale_ref[...] = jnp.broadcast_to(1.0 / jnp.sqrt(total / entries + 1e-06), rescale_ref.shape)
    for level in range(LEVELS):
        for i in range(size):
            rescale = jnp.broadcast_to(rescale_ref[pl.ds(plan_ref[level, 2 * size + i], 1), :], (8, 128))
            factor = rescale / jnp.full((8, 128), plan_ref[level, size + i], jnp.int32).astype(jnp.float32)
            for t, spot in enumerate(spots):
                if level == 0 or t < half:
                    place = slice(level * rows + spot[0].start, level * rows + spot[0].stop)
                    block = firsts[i // 2][i % 2, place, spot[1]]
                else:
                    block = seconds[i // 2][(i % 2) * half + t - half]
                grad_ref[(level, i, *spot)] = block * factor
        for i in range(1, size):
            leader = plan_ref[level, i]

            @pl.when(leader != i)
            def _():
                grad_ref[level, leader] += grad_ref[level, i]

        for i in range(size):
            decayed = decayed_ref[plan_ref[level, 3 * size + i]]
            outs[i // 2][i % 2, level] = decayed - grad_coef * grad_ref[level, plan_ref[level, 4 * size + i]]


def state_kernel(module_ref, grad_ref, decayed_ref, momentum_ref, new_params_ref, new_momentum_ref, token_ref):
    token_ref[...] = jnp.zeros_like(token_ref)
    count = new_params_ref.shape[0]
    first = pl.program_id(0) * count
    level = first // LEVEL_MODULES
    for place in range(count):
        module = first + place
        leader = module_ref[module]
        taken = jnp.where(leader < 0, 0.0, 1.0)
        grad = taken * grad_ref[level, jnp.maximum(leader, 0)]
        new_momentum_ref[place] = beta_coef * momentum_ref[module] + grad
        new_params_ref[place] = decayed_ref[module] - grad_coef * grad


def give_back_kernel(size, here_ref, *refs):
    here = here_ref[0]
    for j, k in enumerate(order_of(size)):
        for level in range(LEVELS):
            refs[-1][level, origin(here, k, size) // 2] = refs[j][1 - (here & 1), level]


def own_rows_kernel(size, here_ref, *refs):
    here = here_ref[0]
    core = here & 1
    out_ref, sems = refs[-2:]
    copies = []
    for j, k in enumerate(order_of(size)):
        chip = origin(here, k, size) // 2
        for level in range(LEVELS):
            copies.append(
                pltpu.make_async_copy(refs[j].at[core, level], out_ref.at[level, chip, core], sems.at[level, j])
            )
    for copy in copies:
        copy.start()
    for copy in copies:
        copy.wait()


def other_rows_kernel(here_ref, back_ref, held_ref, out_ref, sems):
    del held_ref
    core = here_ref[0] & 1
    copies = []
    for level in range(LEVELS):
        for chip in range(back_ref.shape[1]):
            copies.append(
                pltpu.make_async_copy(
                    back_ref.at[level, chip], out_ref.at[level, chip, 1 - core], sems.at[level, chip]
                )
            )
    for copy in copies:
        copy.start()
    for copy in copies:
        copy.wait()


def local(path_delta, assign, params, momentum):
    own_slab = path_delta[0]
    size = assign.shape[0]
    module_count, _, own_rows, width = params.shape
    shards = lax.axis_size("shard")
    entries = float(own_slab.size * shards)
    state_in = params.reshape(module_count, own_rows, width)
    moment_in = momentum.reshape(module_count, own_rows, width)
    split_slab = own_slab.reshape(LEVELS, size // 2, 2, own_rows, width)
    here = lax.axis_index("path").astype(jnp.int32).reshape(1)
    order = order_of(size)
    rounds = len(order)
    swap = [(i, i ^ 1) for i in range(size)]
    shape = lambda *dims: jax.ShapeDtypeStruct(dims, jnp.float32)
    squares_shape = shape(-(-size // 8) * 8, 128)
    by_chip = shape(LEVELS, rounds, own_rows, width)
    message = shape(2, LEVELS, own_rows, width)

    squares, keep, give = call(pack_kernel, [squares_shape, by_chip, by_chip], [smem, vmem], [vmem] * 3)(
        here, split_slab
    )
    gift = lax.ppermute(give, "path", swap)
    tiles = [squares] + [
        lax.ppermute(squares, "shard", [(i, i ^ step) for i in range(shards)]) for step in range(shards - 1, 0, -1)
    ]
    firsts = call(
        lambda *refs: first_merge_kernel(size, *refs),
        [shape(2, own_rows + own_rows // 2, width)] * rounds,
        [smem, vmem, vmem],
        [vmem] * rounds,
    )(here, keep, gift)
    firsts = [move(firsts[j], k, size) for j, k in enumerate(order)]
    decayed = state_in - moment_coef * moment_in
    plan, leaders, planned = call(
        plan_kernel,
        [
            jax.ShapeDtypeStruct((LEVELS, 5 * size), jnp.int32),
            jax.ShapeDtypeStruct((module_count,), jnp.int32),
            shape(8, 128),
        ],
        [smem, smem],
        [smem, smem, vmem],
    )(here, assign.T)
    squares = call(
        lambda *refs: sum_kernel(shards, *refs), squares_shape, [vmem] * shards + [anywhere] * 2, vmem
    )(*tiles, planned, decayed)
    other = lax.ppermute(squares, "path", swap)
    seconds = call(
        lambda *refs: second_merge_kernel(size, *refs),
        [shape(own_rows * width // 1024 + 1, 8, 128)] * rounds,
        [smem] + [vmem] * 4,
        [vmem] * rounds,
    )(here, squares, other, keep, gift)
    seconds = [move(seconds[j], k, size) for j, k in enumerate(order)]

    *outgoing, grad = call(
        lambda *refs: outgoing_kernel(rounds, entries, *refs),
        [message] * rounds + [shape(LEVELS, size, own_rows, width)],
        [smem] + [vmem] * (1 + 2 * rounds),
        [vmem] * (rounds + 1),
        scratch_shapes=[pltpu.VMEM(squares_shape.shape, jnp.float32)],
    )(plan, decayed, *firsts, *seconds)
    returned = [move(outgoing[j], k, size) for j, k in enumerate(order)]
    block = LEVEL_MODULES // 2
    state_block = pl.BlockSpec((block, own_rows, width), lambda i: (i, 0, 0))
    new_state, new_moment, done = call(
        state_kernel,
        [shape(*state_in.shape)] * 2 + [shape(8, 128)],
        [smem, vmem, vmem, vmem],
        [state_block, state_block, vmem],
        grid=(module_count // block,),
    )(leaders, grad, decayed, moment_in)
    back = call(
        lambda *refs: give_back_kernel(size, *refs), by_chip, [smem] + [vmem] * rounds + [anywhere], vmem
    )(here, *returned, done)
    back = lax.ppermute(back, "path", swap)
    sems = [pltpu.SemaphoreType.DMA((LEVELS, rounds))]
    path_params = call(
        lambda *refs: own_rows_kernel(size, *refs),
        shape(*split_slab.shape),
        [smem] + [anywhere] * rounds,
        anywhere,
        scratch_shapes=sems,
    )(here, *returned)
    path_params = call(
        other_rows_kernel,
        shape(*split_slab.shape),
        [smem, anywhere, anywhere],
        anywhere,
        scratch_shapes=sems,
        input_output_aliases={2: 0},
    )(here, back, path_params)
    return (path_params.reshape(path_delta.shape), new_state[:, None], new_moment[:, None])


def local_wide(path_delta, assign, params, momentum):
    own_slab = path_delta[0]
    path_count = assign.shape[0]
    module_count, _, own_rows, width = params.shape
    entries = float(own_slab.size * lax.axis_size("shard"))
    total_sq = lax.psum(jnp.sum(own_slab * own_slab), "shard")
    scaled = own_slab * (1.0 / jnp.sqrt(total_sq / entries + 1e-06))
    received = lax.all_to_all(
        scaled.reshape(LEVELS, path_count, own_rows, width), "path", split_axis=1, concat_axis=1, tiled=True
    )
    flat_ids = (assign + LEVEL_MODULES * jnp.arange(LEVELS, dtype=jnp.int32)[None, :]).T.reshape(-1)
    member = (jnp.arange(module_count, dtype=jnp.int32)[:, None] == flat_ids[None, :]).astype(jnp.float32)
    mean = member / jnp.maximum(jnp.sum(member, axis=1), 1.0)[:, None]
    grad = jnp.einsum(
        "mp,prd->mrd", mean, received.reshape(-1, own_rows, width), precision=lax.Precision.HIGHEST
    )
    new_moment = beta_coef * momentum[:, 0] + grad
    new_state = params[:, 0] - outer_rate * (grad + beta_coef * new_moment)
    outgoing = jnp.take(new_state, flat_ids, axis=0).reshape(LEVELS, path_count, own_rows, width)
    returned = lax.all_to_all(outgoing, "path", split_axis=1, concat_axis=1, tiled=True)
    return (returned.reshape(path_delta.shape), new_state[:, None], new_moment[:, None])


def solution(mesh):
    in_specs = (
        P("path", None, "shard", None),
        P(),
        P(None, "shard", "path", None),
        P(None, "shard", "path", None),
    )
    out_specs = (
        P("path", None, "shard", None),
        P(None, "shard", "path", None),
        P(None, "shard", "path", None),
    )
    chosen = local if 4 <= mesh.shape["path"] <= MOST_UNROLLED else local_wide
    return jax.shard_map(chosen, mesh=mesh, in_specs=in_specs, out_specs=out_specs, check_vma=False)
```

```python
import jax
import jax.numpy as jnp
from jax import lax
from jax.experimental import pallas as pl
from jax.experimental.pallas import tpu as pltpu
from jax.sharding import PartitionSpec as P

LEVEL_MODULES = 16
LEVELS = 2
MOST_UNROLLED = 8

outer_rate = 0.7
beta_coef = 0.9
moment_coef = outer_rate * beta_coef * beta_coef
grad_coef = outer_rate * (1.0 + beta_coef)

VMEM_LIMIT = 16 * 1024 * 1024

vmem = pl.BlockSpec(memory_space=pltpu.VMEM)
smem = pl.BlockSpec(memory_space=pltpu.SMEM)
anywhere = pl.BlockSpec(memory_space=pl.ANY)


def call(kernel, out_shape, in_specs, out_specs, **more):
    return pl.pallas_call(
        kernel,
        out_shape=out_shape,
        in_specs=in_specs,
        out_specs=out_specs,
        compiler_params=pltpu.CompilerParams(vmem_limit_bytes=VMEM_LIMIT),
        **more,
    )


def mirrored(k, size):
    if size < 8:
        return k
    return (k & ~6) | ((k & 2) << 1) | ((k & 4) >> 1)


def target(here, k, size):
    if isinstance(here, int):
        return here ^ (mirrored(k, size) if here & 1 else k)
    return here ^ jnp.where(here & 1 == 1, mirrored(k, size), k)


def origin(here, k, size):
    if isinstance(here, int):
        return here ^ (mirrored(k, size) if (here ^ k) & 1 else k)
    return here ^ jnp.where((here ^ k) & 1 == 1, mirrored(k, size), k)


def order_of(size):
    return sorted(range(2, size, 2), key=lambda k: (-bin(k).count("1"), k)) + [0]


def move(array, k, size):
    if k == 0:
        return array
    return lax.ppermute(array, "path", [(i, target(i, k, size)) for i in range(size)])


def tiles_of(rows, width):
    return [(slice(row, row + 8), slice(lane, lane + 128)) for row in range(0, rows, 8) for lane in range(0, width, 128)]


def pack_kernel(here_ref, delta_ref, square_ref, keep_ref, give_ref):
    levels, chips, halves, rows, width = delta_ref.shape

    def pack(core):
        totals = [jnp.zeros((8, 128), jnp.float32) for _ in range(4)]
        for level in range(levels):
            for chip in range(chips):
                for t, spot in enumerate(tiles_of(rows, width)):
                    kept = delta_ref[(level, chip, core, *spot)]
                    given = delta_ref[(level, chip, 1 - core, *spot)]
                    keep_ref[(level, chip, *spot)] = kept
                    give_ref[(level, chip, *spot)] = given
                    totals[t % 4] = totals[t % 4] + (kept * kept + given * given)
        total = jnp.sum((totals[0] + totals[1]) + (totals[2] + totals[3]), axis=0, keepdims=True)
        for first in range(0, square_ref.shape[0], 8):
            row = lax.broadcasted_iota(jnp.int32, (8, 128), 0) + first
            square_ref[first : first + 8] = jnp.where(row == here_ref[0], total, 0.0)

    for core in range(halves):
        pl.when(here_ref[0] & 1 == core)(lambda core=core: pack(core))


def first_merge_kernel(size, here_ref, keep_ref, gift_ref, *outs):
    here = here_ref[0]
    core = here & 1
    for k, out in zip(order_of(size), outs):
        chip = target(here, k, size) // 2
        rows = keep_ref.shape[2]
        for source, ref in ((core, keep_ref), (1 - core, gift_ref)):
            out[source, :rows] = ref[0, chip]
            out[source, rows:] = ref[1, chip, : rows // 2]


def second_merge_kernel(size, here_ref, square_ref, other_ref, keep_ref, gift_ref, *outs):
    here = here_ref[0]
    core = here & 1
    squares = square_ref[...] + other_ref[...]
    _, _, rows, width = keep_ref.shape
    spots = tiles_of(rows, width)[-(rows * width // 2048) :]
    for k, out in zip(order_of(size), outs):
        chip = target(here, k, size) // 2
        for source, ref in ((core, keep_ref), (1 - core, gift_ref)):
            for t, spot in enumerate(spots):
                out[source * len(spots) + t] = ref[(1, chip, *spot)]
        out[2 * len(spots)] = squares


def sum_kernel(*refs):
    total = refs[0][...]
    for ref in refs[1:-1]:
        total = total + ref[...]
    refs[-1][...] = total


def decay_kernel(params_ref, momentum_ref, out_ref):
    def decay(module, carry):
        out_ref[module] = params_ref[module] - moment_coef * momentum_ref[module]
        return carry

    lax.fori_loop(0, out_ref.shape[0], decay, 0)


def plan_kernel(here_ref, ids_ref, plan_ref, module_ref):
    size = ids_ref.shape[1]
    order = order_of(size)
    here = here_ref[0]
    paths = [(origin(here, k, size) // 2) * 2 + half for k in order for half in range(2)]
    targets = [(target(here, k, size) // 2) * 2 + half for k in order for half in range(2)]
    for level in range(LEVELS):
        first = level * LEVEL_MODULES
        for module in range(LEVEL_MODULES):
            module_ref[first + module] = -1
        sources = [ids_ref[level, path] + first for path in paths]
        for i in reversed(range(size)):
            module_ref[sources[i]] = i
        for i in range(size):
            plan_ref[level, i] = module_ref[sources[i]]
            sharers = jnp.int32(0)
            for other in range(size):
                sharers = sharers + jnp.where(sources[other] == sources[i], 1, 0)
            plan_ref[level, size + i] = sharers
            plan_ref[level, 2 * size + i] = paths[i]
            module = ids_ref[level, targets[i]] + first
            plan_ref[level, 3 * size + i] = module
            plan_ref[level, 4 * size + i] = module_ref[module]


def outgoing_kernel(rounds, entries, plan_ref, decayed_ref, *refs):
    firsts, seconds = refs[:rounds], refs[rounds : 2 * rounds]
    outs, (grad_ref, rescale_ref) = refs[2 * rounds : -2], refs[-2:]
    size = 2 * rounds
    rows, width = grad_ref.shape[2:]
    spots = tiles_of(rows, width)
    half = len(spots) // 2
    squares = seconds[0][2 * half]
    for second in seconds[1:]:
        squares = squares + second[2 * half]
    total = jnp.sum(squares, axis=1, keepdims=True)
    rescale_ref[...] = jnp.broadcast_to(1.0 / jnp.sqrt(total / entries + 1e-06), rescale_ref.shape)
    for level in range(LEVELS):
        for i in range(size):
            rescale = jnp.broadcast_to(rescale_ref[pl.ds(plan_ref[level, 2 * size + i], 1), :], (8, 128))
            factor = rescale / jnp.full((8, 128), plan_ref[level, size + i], jnp.int32).astype(jnp.float32)
            for t, spot in enumerate(spots):
                if level == 0 or t < half:
                    place = slice(level * rows + spot[0].start, level * rows + spot[0].stop)
                    block = firsts[i // 2][i % 2, place, spot[1]]
                else:
                    block = seconds[i // 2][(i % 2) * half + t - half]
                grad_ref[(level, i, *spot)] = block * factor
        for i in range(1, size):
            leader = plan_ref[level, i]

            @pl.when(leader != i)
            def _():
                grad_ref[level, leader] += grad_ref[level, i]

        for i in range(size):
            decayed = decayed_ref[plan_ref[level, 3 * size + i]]
            outs[i // 2][i % 2, level] = decayed - grad_coef * grad_ref[level, plan_ref[level, 4 * size + i]]


def state_kernel(module_ref, grad_ref, decayed_ref, momentum_ref, new_params_ref, new_momentum_ref, token_ref):
    token_ref[...] = jnp.zeros_like(token_ref)
    count = new_params_ref.shape[0]
    first = pl.program_id(0) * count
    level = first // LEVEL_MODULES
    for place in range(count):
        module = first + place
        leader = module_ref[module]
        taken = jnp.where(leader < 0, 0.0, 1.0)
        grad = taken * grad_ref[level, jnp.maximum(leader, 0)]
        new_momentum_ref[place] = beta_coef * momentum_ref[module] + grad
        new_params_ref[place] = decayed_ref[module] - grad_coef * grad


def give_back_kernel(size, here_ref, *refs):
    here = here_ref[0]
    for j, k in enumerate(order_of(size)):
        for level in range(LEVELS):
            refs[-1][level, origin(here, k, size) // 2] = refs[j][1 - (here & 1), level]


def own_rows_kernel(size, here_ref, *refs):
    here = here_ref[0]
    core = here & 1
    out_ref, sems = refs[-2:]
    copies = []
    for j, k in enumerate(order_of(size)):
        chip = origin(here, k, size) // 2
        for level in range(LEVELS):
            copies.append(
                pltpu.make_async_copy(refs[j].at[core, level], out_ref.at[level, chip, core], sems.at[level, j])
            )
    for copy in copies:
        copy.start()
    for copy in copies:
        copy.wait()


def other_rows_kernel(here_ref, back_ref, held_ref, out_ref, sems):
    del held_ref
    core = here_ref[0] & 1
    copies = []
    for level in range(LEVELS):
        for chip in range(back_ref.shape[1]):
            copies.append(
                pltpu.make_async_copy(
                    back_ref.at[level, chip], out_ref.at[level, chip, 1 - core], sems.at[level, chip]
                )
            )
    for copy in copies:
        copy.start()
    for copy in copies:
        copy.wait()


def local(path_delta, assign, params, momentum):
    own_slab = path_delta[0]
    size = assign.shape[0]
    module_count, _, own_rows, width = params.shape
    shards = lax.axis_size("shard")
    entries = float(own_slab.size * shards)
    state_in = params.reshape(module_count, own_rows, width)
    moment_in = momentum.reshape(module_count, own_rows, width)
    split_slab = own_slab.reshape(LEVELS, size // 2, 2, own_rows, width)
    here = lax.axis_index("path").astype(jnp.int32).reshape(1)
    order = order_of(size)
    rounds = len(order)
    swap = [(i, i ^ 1) for i in range(size)]
    shape = lambda *dims: jax.ShapeDtypeStruct(dims, jnp.float32)
    squares_shape = shape(-(-size // 8) * 8, 128)
    by_chip = shape(LEVELS, rounds, own_rows, width)
    message = shape(2, LEVELS, own_rows, width)

    squares, keep, give = call(pack_kernel, [squares_shape, by_chip, by_chip], [smem, vmem], [vmem] * 3)(
        here, split_slab
    )
    gift = lax.ppermute(give, "path", swap)
    tiles = [squares] + [
        lax.ppermute(squares, "shard", [(i, i ^ step) for i in range(shards)]) for step in range(shards - 1, 0, -1)
    ]
    firsts = call(
        lambda *refs: first_merge_kernel(size, *refs),
        [shape(2, own_rows + own_rows // 2, width)] * rounds,
        [smem, vmem, vmem],
        [vmem] * rounds,
    )(here, keep, gift)
    firsts = [move(firsts[j], k, size) for j, k in enumerate(order)]
    decayed = call(decay_kernel, shape(*state_in.shape), [vmem, vmem], vmem)(state_in, moment_in)
    plan, leaders = call(
        plan_kernel,
        [
            jax.ShapeDtypeStruct((LEVELS, 5 * size), jnp.int32),
            jax.ShapeDtypeStruct((module_count,), jnp.int32),
        ],
        [smem, smem],
        [smem, smem],
    )(here, assign.T)
    squares = call(sum_kernel, squares_shape, [vmem] * shards, vmem)(*tiles)
    other = lax.ppermute(squares, "path", swap)
    seconds = call(
        lambda *refs: second_merge_kernel(size, *refs),
        [shape(own_rows * width // 1024 + 1, 8, 128)] * rounds,
        [smem] + [vmem] * 4,
        [vmem] * rounds,
    )(here, squares, other, keep, gift)
    seconds = [move(seconds[j], k, size) for j, k in enumerate(order)]

    *outgoing, grad = call(
        lambda *refs: outgoing_kernel(rounds, entries, *refs),
        [message] * rounds + [shape(LEVELS, size, own_rows, width)],
        [smem] + [vmem] * (1 + 2 * rounds),
        [vmem] * (rounds + 1),
        scratch_shapes=[pltpu.VMEM(squares_shape.shape, jnp.float32)],
    )(plan, decayed, *firsts, *seconds)
    returned = [move(outgoing[j], k, size) for j, k in enumerate(order)]
    block = LEVEL_MODULES // 2
    state_block = pl.BlockSpec((block, own_rows, width), lambda i: (i, 0, 0))
    new_state, new_moment, done = call(
        state_kernel,
        [shape(*state_in.shape)] * 2 + [shape(8, 128)],
        [smem, vmem, vmem, vmem],
        [state_block, state_block, vmem],
        grid=(module_count // block,),
    )(leaders, grad, decayed, moment_in)
    back = call(
        lambda *refs: give_back_kernel(size, *refs), by_chip, [smem] + [vmem] * rounds + [anywhere], vmem
    )(here, *returned, done)
    back = lax.ppermute(back, "path", swap)
    sems = [pltpu.SemaphoreType.DMA((LEVELS, rounds))]
    path_params = call(
        lambda *refs: own_rows_kernel(size, *refs),
        shape(*split_slab.shape),
        [smem] + [anywhere] * rounds,
        anywhere,
        scratch_shapes=sems,
    )(here, *returned)
    path_params = call(
        other_rows_kernel,
        shape(*split_slab.shape),
        [smem, anywhere, anywhere],
        anywhere,
        scratch_shapes=sems,
        input_output_aliases={2: 0},
    )(here, back, path_params)
    return (path_params.reshape(path_delta.shape), new_state[:, None], new_moment[:, None])


def local_wide(path_delta, assign, params, momentum):
    own_slab = path_delta[0]
    path_count = assign.shape[0]
    module_count, _, own_rows, width = params.shape
    entries = float(own_slab.size * lax.axis_size("shard"))
    total_sq = lax.psum(jnp.sum(own_slab * own_slab), "shard")
    scaled = own_slab * (1.0 / jnp.sqrt(total_sq / entries + 1e-06))
    received = lax.all_to_all(
        scaled.reshape(LEVELS, path_count, own_rows, width), "path", split_axis=1, concat_axis=1, tiled=True
    )
    flat_ids = (assign + LEVEL_MODULES * jnp.arange(LEVELS, dtype=jnp.int32)[None, :]).T.reshape(-1)
    member = (jnp.arange(module_count, dtype=jnp.int32)[:, None] == flat_ids[None, :]).astype(jnp.float32)
    mean = member / jnp.maximum(jnp.sum(member, axis=1), 1.0)[:, None]
    grad = jnp.einsum(
        "mp,prd->mrd", mean, received.reshape(-1, own_rows, width), precision=lax.Precision.HIGHEST
    )
    new_moment = beta_coef * momentum[:, 0] + grad
    new_state = params[:, 0] - outer_rate * (grad + beta_coef * new_moment)
    outgoing = jnp.take(new_state, flat_ids, axis=0).reshape(LEVELS, path_count, own_rows, width)
    returned = lax.all_to_all(outgoing, "path", split_axis=1, concat_axis=1, tiled=True)
    return (returned.reshape(path_delta.shape), new_state[:, None], new_moment[:, None])


def solution(mesh):
    in_specs = (
        P("path", None, "shard", None),
        P(),
        P(None, "shard", "path", None),
        P(None, "shard", "path", None),
    )
    out_specs = (
        P("path", None, "shard", None),
        P(None, "shard", "path", None),
        P(None, "shard", "path", None),
    )
    chosen = local if 4 <= mesh.shape["path"] <= MOST_UNROLLED else local_wide
    return jax.shard_map(chosen, mesh=mesh, in_specs=in_specs, out_specs=out_specs, check_vma=False)
```

```python
import jax
import jax.numpy as jnp
from jax import lax
from jax.experimental import pallas as pl
from jax.experimental.pallas import tpu as pltpu
from jax.sharding import PartitionSpec as P

LEVEL_MODULES = 16
LEVELS = 2
MOST_UNROLLED = 8

outer_rate = 0.7
beta_coef = 0.9
moment_coef = outer_rate * beta_coef * beta_coef
grad_coef = outer_rate * (1.0 + beta_coef)

VMEM_LIMIT = 16 * 1024 * 1024

vmem = pl.BlockSpec(memory_space=pltpu.VMEM)
smem = pl.BlockSpec(memory_space=pltpu.SMEM)
anywhere = pl.BlockSpec(memory_space=pl.ANY)


def call(kernel, out_shape, in_specs, out_specs, **more):
    return pl.pallas_call(
        kernel,
        out_shape=out_shape,
        in_specs=in_specs,
        out_specs=out_specs,
        compiler_params=pltpu.CompilerParams(vmem_limit_bytes=VMEM_LIMIT),
        **more,
    )


def mirrored(k, size):
    if size < 8:
        return k
    return (k & ~6) | ((k & 2) << 1) | ((k & 4) >> 1)


def target(here, k, size):
    if isinstance(here, int):
        return here ^ (mirrored(k, size) if here & 1 else k)
    return here ^ jnp.where(here & 1 == 1, mirrored(k, size), k)


def origin(here, k, size):
    if isinstance(here, int):
        return here ^ (mirrored(k, size) if (here ^ k) & 1 else k)
    return here ^ jnp.where((here ^ k) & 1 == 1, mirrored(k, size), k)


def order_of(size):
    return sorted(range(2, size, 2), key=lambda k: (-bin(k).count("1"), k)) + [0]


def move(array, k, size):
    if k == 0:
        return array
    return lax.ppermute(array, "path", [(i, target(i, k, size)) for i in range(size)])


def tiles_of(rows, width):
    return [(slice(row, row + 8), slice(lane, lane + 128)) for row in range(0, rows, 8) for lane in range(0, width, 128)]


def pack_kernel(here_ref, delta_ref, square_ref, keep_ref, give_ref):
    levels, chips, halves, rows, width = delta_ref.shape

    def pack(core):
        totals = [jnp.zeros((8, 128), jnp.float32) for _ in range(4)]
        for level in range(levels):
            for chip in range(chips):
                for t, spot in enumerate(tiles_of(rows, width)):
                    kept = delta_ref[(level, chip, core, *spot)]
                    given = delta_ref[(level, chip, 1 - core, *spot)]
                    keep_ref[(level, chip, *spot)] = kept
                    give_ref[(level, chip, *spot)] = given
                    totals[t % 4] = totals[t % 4] + (kept * kept + given * given)
        total = jnp.sum((totals[0] + totals[1]) + (totals[2] + totals[3]), axis=0, keepdims=True)
        for first in range(0, square_ref.shape[0], 8):
            row = lax.broadcasted_iota(jnp.int32, (8, 128), 0) + first
            square_ref[first : first + 8] = jnp.where(row == here_ref[0], total, 0.0)

    for core in range(halves):
        pl.when(here_ref[0] & 1 == core)(lambda core=core: pack(core))


def first_merge_kernel(size, here_ref, keep_ref, gift_ref, *outs):
    here = here_ref[0]
    core = here & 1
    for k, out in zip(order_of(size), outs):
        chip = target(here, k, size) // 2
        rows = keep_ref.shape[2]
        for source, ref in ((core, keep_ref), (1 - core, gift_ref)):
            out[source, :rows] = ref[0, chip]
            out[source, rows:] = ref[1, chip, : rows // 2]


def second_merge_kernel(size, here_ref, square_ref, other_ref, keep_ref, gift_ref, *outs):
    here = here_ref[0]
    core = here & 1
    squares = square_ref[...] + other_ref[...]
    _, _, rows, width = keep_ref.shape
    spots = tiles_of(rows, width)[-(rows * width // 2048) :]
    for k, out in zip(order_of(size), outs):
        chip = target(here, k, size) // 2
        for source, ref in ((core, keep_ref), (1 - core, gift_ref)):
            for t, spot in enumerate(spots):
                out[source * len(spots) + t] = ref[(1, chip, *spot)]
        out[2 * len(spots)] = squares


def sum_kernel(count, *refs):
    total = refs[0][...]
    for ref in refs[1:count]:
        total = total + ref[...]
    refs[-1][...] = total


def decay_kernel(params_ref, decay_ref, out_ref):
    def decay(module, carry):
        out_ref[module] = params_ref[module] - decay_ref[module]
        return carry

    lax.fori_loop(0, out_ref.shape[0], decay, 0)


def plan_kernel(here_ref, ids_ref, plan_ref, module_ref):
    size = ids_ref.shape[1]
    order = order_of(size)
    here = here_ref[0]
    paths = [(origin(here, k, size) // 2) * 2 + half for k in order for half in range(2)]
    targets = [(target(here, k, size) // 2) * 2 + half for k in order for half in range(2)]
    for level in range(LEVELS):
        first = level * LEVEL_MODULES
        for module in range(LEVEL_MODULES):
            module_ref[first + module] = -1
        sources = [ids_ref[level, path] + first for path in paths]
        for i in reversed(range(size)):
            module_ref[sources[i]] = i
        for i in range(size):
            plan_ref[level, i] = module_ref[sources[i]]
            sharers = jnp.int32(0)
            for other in range(size):
                sharers = sharers + jnp.where(sources[other] == sources[i], 1, 0)
            plan_ref[level, size + i] = sharers
            plan_ref[level, 2 * size + i] = paths[i]
            module = ids_ref[level, targets[i]] + first
            plan_ref[level, 3 * size + i] = module
            plan_ref[level, 4 * size + i] = module_ref[module]


def outgoing_kernel(rounds, entries, plan_ref, decayed_ref, *refs):
    firsts, seconds = refs[:rounds], refs[rounds : 2 * rounds]
    outs, (grad_ref, rescale_ref) = refs[2 * rounds : -2], refs[-2:]
    size = 2 * rounds
    rows, width = grad_ref.shape[2:]
    spots = tiles_of(rows, width)
    half = len(spots) // 2
    squares = seconds[0][2 * half]
    for second in seconds[1:]:
        squares = squares + second[2 * half]
    total = jnp.sum(squares, axis=1, keepdims=True)
    rescale_ref[...] = jnp.broadcast_to(1.0 / jnp.sqrt(total / entries + 1e-06), rescale_ref.shape)
    for level in range(LEVELS):
        for i in range(size):
            rescale = jnp.broadcast_to(rescale_ref[pl.ds(plan_ref[level, 2 * size + i], 1), :], (8, 128))
            factor = rescale / jnp.full((8, 128), plan_ref[level, size + i], jnp.int32).astype(jnp.float32)
            for t, spot in enumerate(spots):
                if level == 0 or t < half:
                    place = slice(level * rows + spot[0].start, level * rows + spot[0].stop)
                    block = firsts[i // 2][i % 2, place, spot[1]]
                else:
                    block = seconds[i // 2][(i % 2) * half + t - half]
                grad_ref[(level, i, *spot)] = block * factor
        for i in range(1, size):
            leader = plan_ref[level, i]

            @pl.when(leader != i)
            def _():
                grad_ref[level, leader] += grad_ref[level, i]

        for i in range(size):
            decayed = decayed_ref[plan_ref[level, 3 * size + i]]
            outs[i // 2][i % 2, level] = decayed - grad_coef * grad_ref[level, plan_ref[level, 4 * size + i]]


def state_kernel(module_ref, grad_ref, decayed_ref, momentum_ref, new_params_ref, new_momentum_ref, token_ref):
    token_ref[...] = jnp.zeros_like(token_ref)
    count = new_params_ref.shape[0]
    first = pl.program_id(0) * count
    level = first // LEVEL_MODULES
    for place in range(count):
        module = first + place
        leader = module_ref[module]
        taken = jnp.where(leader < 0, 0.0, 1.0)
        grad = taken * grad_ref[level, jnp.maximum(leader, 0)]
        new_momentum_ref[place] = beta_coef * momentum_ref[module] + grad
        new_params_ref[place] = decayed_ref[module] - grad_coef * grad


def give_back_kernel(size, here_ref, *refs):
    here = here_ref[0]
    for j, k in enumerate(order_of(size)):
        for level in range(LEVELS):
            refs[-1][level, origin(here, k, size) // 2] = refs[j][1 - (here & 1), level]


def own_rows_kernel(size, here_ref, *refs):
    here = here_ref[0]
    core = here & 1
    out_ref, sems = refs[-2:]
    copies = []
    for j, k in enumerate(order_of(size)):
        chip = origin(here, k, size) // 2
        for level in range(LEVELS):
            copies.append(
                pltpu.make_async_copy(refs[j].at[core, level], out_ref.at[level, chip, core], sems.at[level, j])
            )
    for copy in copies:
        copy.start()
    for copy in copies:
        copy.wait()


def other_rows_kernel(here_ref, back_ref, held_ref, out_ref, sems):
    del held_ref
    core = here_ref[0] & 1
    copies = []
    for level in range(LEVELS):
        for chip in range(back_ref.shape[1]):
            copies.append(
                pltpu.make_async_copy(
                    back_ref.at[level, chip], out_ref.at[level, chip, 1 - core], sems.at[level, chip]
                )
            )
    for copy in copies:
        copy.start()
    for copy in copies:
        copy.wait()


def local(path_delta, assign, params, momentum):
    own_slab = path_delta[0]
    size = assign.shape[0]
    module_count, _, own_rows, width = params.shape
    shards = lax.axis_size("shard")
    entries = float(own_slab.size * shards)
    state_in = params.reshape(module_count, own_rows, width)
    moment_in = momentum.reshape(module_count, own_rows, width)
    split_slab = own_slab.reshape(LEVELS, size // 2, 2, own_rows, width)
    here = lax.axis_index("path").astype(jnp.int32).reshape(1)
    order = order_of(size)
    rounds = len(order)
    swap = [(i, i ^ 1) for i in range(size)]
    shape = lambda *dims: jax.ShapeDtypeStruct(dims, jnp.float32)
    squares_shape = shape(-(-size // 8) * 8, 128)
    by_chip = shape(LEVELS, rounds, own_rows, width)
    message = shape(2, LEVELS, own_rows, width)

    squares, keep, give = call(pack_kernel, [squares_shape, by_chip, by_chip], [smem, vmem], [vmem] * 3)(
        here, split_slab
    )
    gift = lax.ppermute(give, "path", swap)
    tiles = [squares] + [
        lax.ppermute(squares, "shard", [(i, i ^ step) for i in range(shards)]) for step in range(shards - 1, 0, -1)
    ]
    firsts = call(
        lambda *refs: first_merge_kernel(size, *refs),
        [shape(2, own_rows + own_rows // 2, width)] * rounds,
        [smem, vmem, vmem],
        [vmem] * rounds,
    )(here, keep, gift)
    firsts = [move(firsts[j], k, size) for j, k in enumerate(order)]
    decay = moment_coef * moment_in
    decayed = call(decay_kernel, shape(*state_in.shape), [vmem, vmem], vmem)(state_in, decay)
    plan, leaders = call(
        plan_kernel,
        [
            jax.ShapeDtypeStruct((LEVELS, 5 * size), jnp.int32),
            jax.ShapeDtypeStruct((module_count,), jnp.int32),
        ],
        [smem, smem],
        [smem, smem],
    )(here, assign.T)
    squares = call(
        lambda *refs: sum_kernel(shards, *refs), squares_shape, [vmem] * shards + [anywhere], vmem
    )(*tiles, decay)
    other = lax.ppermute(squares, "path", swap)
    seconds = call(
        lambda *refs: second_merge_kernel(size, *refs),
        [shape(own_rows * width // 1024 + 1, 8, 128)] * rounds,
        [smem] + [vmem] * 4,
        [vmem] * rounds,
    )(here, squares, other, keep, gift)
    seconds = [move(seconds[j], k, size) for j, k in enumerate(order)]

    *outgoing, grad = call(
        lambda *refs: outgoing_kernel(rounds, entries, *refs),
        [message] * rounds + [shape(LEVELS, size, own_rows, width)],
        [smem] + [vmem] * (1 + 2 * rounds),
        [vmem] * (rounds + 1),
        scratch_shapes=[pltpu.VMEM(squares_shape.shape, jnp.float32)],
    )(plan, decayed, *firsts, *seconds)
    returned = [move(outgoing[j], k, size) for j, k in enumerate(order)]
    block = LEVEL_MODULES // 2
    state_block = pl.BlockSpec((block, own_rows, width), lambda i: (i, 0, 0))
    new_state, new_moment, done = call(
        state_kernel,
        [shape(*state_in.shape)] * 2 + [shape(8, 128)],
        [smem, vmem, vmem, vmem],
        [state_block, state_block, vmem],
        grid=(module_count // block,),
    )(leaders, grad, decayed, moment_in)
    back = call(
        lambda *refs: give_back_kernel(size, *refs), by_chip, [smem] + [vmem] * rounds + [anywhere], vmem
    )(here, *returned, done)
    back = lax.ppermute(back, "path", swap)
    sems = [pltpu.SemaphoreType.DMA((LEVELS, rounds))]
    path_params = call(
        lambda *refs: own_rows_kernel(size, *refs),
        shape(*split_slab.shape),
        [smem] + [anywhere] * rounds,
        anywhere,
        scratch_shapes=sems,
    )(here, *returned)
    path_params = call(
        other_rows_kernel,
        shape(*split_slab.shape),
        [smem, anywhere, anywhere],
        anywhere,
        scratch_shapes=sems,
        input_output_aliases={2: 0},
    )(here, back, path_params)
    return (path_params.reshape(path_delta.shape), new_state[:, None], new_moment[:, None])


def local_wide(path_delta, assign, params, momentum):
    own_slab = path_delta[0]
    path_count = assign.shape[0]
    module_count, _, own_rows, width = params.shape
    entries = float(own_slab.size * lax.axis_size("shard"))
    total_sq = lax.psum(jnp.sum(own_slab * own_slab), "shard")
    scaled = own_slab * (1.0 / jnp.sqrt(total_sq / entries + 1e-06))
    received = lax.all_to_all(
        scaled.reshape(LEVELS, path_count, own_rows, width), "path", split_axis=1, concat_axis=1, tiled=True
    )
    flat_ids = (assign + LEVEL_MODULES * jnp.arange(LEVELS, dtype=jnp.int32)[None, :]).T.reshape(-1)
    member = (jnp.arange(module_count, dtype=jnp.int32)[:, None] == flat_ids[None, :]).astype(jnp.float32)
    mean = member / jnp.maximum(jnp.sum(member, axis=1), 1.0)[:, None]
    grad = jnp.einsum(
        "mp,prd->mrd", mean, received.reshape(-1, own_rows, width), precision=lax.Precision.HIGHEST
    )
    new_moment = beta_coef * momentum[:, 0] + grad
    new_state = params[:, 0] - outer_rate * (grad + beta_coef * new_moment)
    outgoing = jnp.take(new_state, flat_ids, axis=0).reshape(LEVELS, path_count, own_rows, width)
    returned = lax.all_to_all(outgoing, "path", split_axis=1, concat_axis=1, tiled=True)
    return (returned.reshape(path_delta.shape), new_state[:, None], new_moment[:, None])


def solution(mesh):
    in_specs = (
        P("path", None, "shard", None),
        P(),
        P(None, "shard", "path", None),
        P(None, "shard", "path", None),
    )
    out_specs = (
        P("path", None, "shard", None),
        P(None, "shard", "path", None),
        P(None, "shard", "path", None),
    )
    chosen = local if 4 <= mesh.shape["path"] <= MOST_UNROLLED else local_wide
    return jax.shard_map(chosen, mesh=mesh, in_specs=in_specs, out_specs=out_specs, check_vma=False)
```

```python
import jax
import jax.numpy as jnp
from jax import lax
from jax.experimental import pallas as pl
from jax.experimental.pallas import tpu as pltpu
from jax.sharding import PartitionSpec as P

LEVEL_MODULES = 16
LEVELS = 2
MOST_UNROLLED = 8

outer_rate = 0.7
beta_coef = 0.9
moment_coef = outer_rate * beta_coef * beta_coef
grad_coef = outer_rate * (1.0 + beta_coef)

VMEM_LIMIT = 16 * 1024 * 1024

vmem = pl.BlockSpec(memory_space=pltpu.VMEM)
smem = pl.BlockSpec(memory_space=pltpu.SMEM)
anywhere = pl.BlockSpec(memory_space=pl.ANY)


def call(kernel, out_shape, in_specs, out_specs, **more):
    return pl.pallas_call(
        kernel,
        out_shape=out_shape,
        in_specs=in_specs,
        out_specs=out_specs,
        compiler_params=pltpu.CompilerParams(vmem_limit_bytes=VMEM_LIMIT),
        **more,
    )


def mirrored(k, size):
    if size < 8:
        return k
    return (k & ~6) | ((k & 2) << 1) | ((k & 4) >> 1)


def target(here, k, size):
    if isinstance(here, int):
        return here ^ (mirrored(k, size) if here & 1 else k)
    return here ^ jnp.where(here & 1 == 1, mirrored(k, size), k)


def origin(here, k, size):
    if isinstance(here, int):
        return here ^ (mirrored(k, size) if (here ^ k) & 1 else k)
    return here ^ jnp.where((here ^ k) & 1 == 1, mirrored(k, size), k)


def order_of(size):
    return sorted(range(2, size, 2), key=lambda k: (-bin(k).count("1"), k)) + [0]


def whole_in_first(k):
    return bin(k).count("1") > 1


def move(array, k, size):
    if k == 0:
        return array
    return lax.ppermute(array, "path", [(i, target(i, k, size)) for i in range(size)])


def tiles_of(rows, width):
    return [(slice(row, row + 8), slice(lane, lane + 128)) for row in range(0, rows, 8) for lane in range(0, width, 128)]


def pack_kernel(here_ref, delta_ref, square_ref, keep_ref, give_ref):
    levels, chips, halves, rows, width = delta_ref.shape

    def pack(core):
        totals = [jnp.zeros((8, 128), jnp.float32) for _ in range(4)]
        for level in range(levels):
            for chip in range(chips):
                for t, spot in enumerate(tiles_of(rows, width)):
                    kept = delta_ref[(level, chip, core, *spot)]
                    given = delta_ref[(level, chip, 1 - core, *spot)]
                    keep_ref[(level, chip, *spot)] = kept
                    give_ref[(level, chip, *spot)] = given
                    totals[t % 4] = totals[t % 4] + (kept * kept + given * given)
        total = jnp.sum((totals[0] + totals[1]) + (totals[2] + totals[3]), axis=0, keepdims=True)
        for first in range(0, square_ref.shape[0], 8):
            row = lax.broadcasted_iota(jnp.int32, (8, 128), 0) + first
            square_ref[first : first + 8] = jnp.where(row == here_ref[0], total, 0.0)

    for core in range(halves):
        pl.when(here_ref[0] & 1 == core)(lambda core=core: pack(core))


def first_merge_kernel(size, here_ref, keep_ref, gift_ref, *outs):
    here = here_ref[0]
    core = here & 1
    for k, out in zip(order_of(size), outs):
        chip = target(here, k, size) // 2
        rows = keep_ref.shape[2]
        for source, ref in ((core, keep_ref), (1 - core, gift_ref)):
            out[source, :rows] = ref[0, chip]
            out[source, rows:] = ref[1, chip, : out.shape[1] - rows]


def second_merge_kernel(size, here_ref, square_ref, other_ref, keep_ref, gift_ref, *outs):
    here = here_ref[0]
    core = here & 1
    squares = square_ref[...] + other_ref[...]
    _, _, rows, width = keep_ref.shape
    spots = tiles_of(rows, width)[-(rows * width // 2048) :]
    for k, out in zip(order_of(size), outs):
        out[0] = squares
        if whole_in_first(k):
            continue
        chip = target(here, k, size) // 2
        for source, ref in ((core, keep_ref), (1 - core, gift_ref)):
            for t, spot in enumerate(spots):
                out[1 + source * len(spots) + t] = ref[(1, chip, *spot)]


def sum_kernel(count, *refs):
    total = refs[0][...]
    for ref in refs[1:count]:
        total = total + ref[...]
    refs[-1][...] = total


def decay_kernel(params_ref, decay_ref, out_ref):
    def decay(module, carry):
        out_ref[module] = params_ref[module] - decay_ref[module]
        return carry

    lax.fori_loop(0, out_ref.shape[0], decay, 0)


def plan_kernel(here_ref, ids_ref, plan_ref, module_ref):
    size = ids_ref.shape[1]
    order = order_of(size)
    here = here_ref[0]
    paths = [(origin(here, k, size) // 2) * 2 + half for k in order for half in range(2)]
    targets = [(target(here, k, size) // 2) * 2 + half for k in order for half in range(2)]
    for level in range(LEVELS):
        first = level * LEVEL_MODULES
        for module in range(LEVEL_MODULES):
            module_ref[first + module] = -1
        sources = [ids_ref[level, path] + first for path in paths]
        for i in reversed(range(size)):
            module_ref[sources[i]] = i
        for i in range(size):
            plan_ref[level, i] = module_ref[sources[i]]
            sharers = jnp.int32(0)
            for other in range(size):
                sharers = sharers + jnp.where(sources[other] == sources[i], 1, 0)
            plan_ref[level, size + i] = sharers
            plan_ref[level, 2 * size + i] = paths[i]
            module = ids_ref[level, targets[i]] + first
            plan_ref[level, 3 * size + i] = module
            plan_ref[level, 4 * size + i] = module_ref[module]


def outgoing_kernel(rounds, entries, plan_ref, decayed_ref, *refs):
    firsts, seconds = refs[:rounds], refs[rounds : 2 * rounds]
    outs, (grad_ref, rescale_ref) = refs[2 * rounds : -2], refs[-2:]
    size = 2 * rounds
    rows, width = grad_ref.shape[2:]
    spots = tiles_of(rows, width)
    half = len(spots) // 2
    squares = seconds[0][0]
    for second in seconds[1:]:
        squares = squares + second[0]
    total = jnp.sum(squares, axis=1, keepdims=True)
    rescale_ref[...] = jnp.broadcast_to(1.0 / jnp.sqrt(total / entries + 1e-06), rescale_ref.shape)
    for level in range(LEVELS):
        for i in range(size):
            rescale = jnp.broadcast_to(rescale_ref[pl.ds(plan_ref[level, 2 * size + i], 1), :], (8, 128))
            factor = rescale / jnp.full((8, 128), plan_ref[level, size + i], jnp.int32).astype(jnp.float32)
            for t, spot in enumerate(spots):
                if level == 0 or t < half or whole_in_first(order_of(size)[i // 2]):
                    place = slice(level * rows + spot[0].start, level * rows + spot[0].stop)
                    block = firsts[i // 2][i % 2, place, spot[1]]
                else:
                    block = seconds[i // 2][1 + (i % 2) * half + t - half]
                grad_ref[(level, i, *spot)] = block * factor
        for i in range(1, size):
            leader = plan_ref[level, i]

            @pl.when(leader != i)
            def _():
                grad_ref[level, leader] += grad_ref[level, i]

        for i in range(size):
            decayed = decayed_ref[plan_ref[level, 3 * size + i]]
            outs[i // 2][i % 2, level] = decayed - grad_coef * grad_ref[level, plan_ref[level, 4 * size + i]]


def state_kernel(module_ref, grad_ref, decayed_ref, momentum_ref, new_params_ref, new_momentum_ref, token_ref):
    token_ref[...] = jnp.zeros_like(token_ref)
    count = new_params_ref.shape[0]
    first = pl.program_id(0) * count
    level = first // LEVEL_MODULES
    for place in range(count):
        module = first + place
        leader = module_ref[module]
        taken = jnp.where(leader < 0, 0.0, 1.0)
        grad = taken * grad_ref[level, jnp.maximum(leader, 0)]
        new_momentum_ref[place] = beta_coef * momentum_ref[module] + grad
        new_params_ref[place] = decayed_ref[module] - grad_coef * grad


def give_back_kernel(size, here_ref, *refs):
    here = here_ref[0]
    for j, k in enumerate(order_of(size)):
        for level in range(LEVELS):
            refs[-1][level, origin(here, k, size) // 2] = refs[j][1 - (here & 1), level]


def own_rows_kernel(size, here_ref, *refs):
    here = here_ref[0]
    core = here & 1
    out_ref, sems = refs[-2:]
    copies = []
    for j, k in enumerate(order_of(size)):
        chip = origin(here, k, size) // 2
        for level in range(LEVELS):
            copies.append(
                pltpu.make_async_copy(refs[j].at[core, level], out_ref.at[level, chip, core], sems.at[level, j])
            )
    for copy in copies:
        copy.start()
    for copy in copies:
        copy.wait()


def other_rows_kernel(here_ref, back_ref, held_ref, out_ref, sems):
    del held_ref
    core = here_ref[0] & 1
    copies = []
    for level in range(LEVELS):
        for chip in range(back_ref.shape[1]):
            copies.append(
                pltpu.make_async_copy(
                    back_ref.at[level, chip], out_ref.at[level, chip, 1 - core], sems.at[level, chip]
                )
            )
    for copy in copies:
        copy.start()
    for copy in copies:
        copy.wait()


def local(path_delta, assign, params, momentum):
    own_slab = path_delta[0]
    size = assign.shape[0]
    module_count, _, own_rows, width = params.shape
    shards = lax.axis_size("shard")
    entries = float(own_slab.size * shards)
    state_in = params.reshape(module_count, own_rows, width)
    moment_in = momentum.reshape(module_count, own_rows, width)
    split_slab = own_slab.reshape(LEVELS, size // 2, 2, own_rows, width)
    here = lax.axis_index("path").astype(jnp.int32).reshape(1)
    order = order_of(size)
    rounds = len(order)
    swap = [(i, i ^ 1) for i in range(size)]
    shape = lambda *dims: jax.ShapeDtypeStruct(dims, jnp.float32)
    squares_shape = shape(-(-size // 8) * 8, 128)
    by_chip = shape(LEVELS, rounds, own_rows, width)
    message = shape(2, LEVELS, own_rows, width)

    squares, keep, give = call(pack_kernel, [squares_shape, by_chip, by_chip], [smem, vmem], [vmem] * 3)(
        here, split_slab
    )
    gift = lax.ppermute(give, "path", swap)
    tiles = [squares] + [
        lax.ppermute(squares, "shard", [(i, i ^ step) for i in range(shards)]) for step in range(shards - 1, 0, -1)
    ]
    firsts = call(
        lambda *refs: first_merge_kernel(size, *refs),
        [shape(2, own_rows + (own_rows if whole_in_first(k) else own_rows // 2), width) for k in order],
        [smem, vmem, vmem],
        [vmem] * rounds,
    )(here, keep, gift)
    firsts = [move(firsts[j], k, size) for j, k in enumerate(order)]
    decay = moment_coef * moment_in
    decayed = call(decay_kernel, shape(*state_in.shape), [vmem, vmem], vmem)(state_in, decay)
    plan, leaders = call(
        plan_kernel,
        [
            jax.ShapeDtypeStruct((LEVELS, 5 * size), jnp.int32),
            jax.ShapeDtypeStruct((module_count,), jnp.int32),
        ],
        [smem, smem],
        [smem, smem],
    )(here, assign.T)
    squares = call(
        lambda *refs: sum_kernel(shards, *refs), squares_shape, [vmem] * shards + [anywhere], vmem
    )(*tiles, decay)
    other = lax.ppermute(squares, "path", swap)
    seconds = call(
        lambda *refs: second_merge_kernel(size, *refs),
        [shape(1 if whole_in_first(k) else 1 + own_rows * width // 1024, 8, 128) for k in order],
        [smem] + [vmem] * 4,
        [vmem] * rounds,
    )(here, squares, other, keep, gift)
    seconds = [move(seconds[j], k, size) for j, k in enumerate(order)]

    *outgoing, grad = call(
        lambda *refs: outgoing_kernel(rounds, entries, *refs),
        [message] * rounds + [shape(LEVELS, size, own_rows, width)],
        [smem] + [vmem] * (1 + 2 * rounds),
        [vmem] * (rounds + 1),
        scratch_shapes=[pltpu.VMEM(squares_shape.shape, jnp.float32)],
    )(plan, decayed, *firsts, *seconds)
    returned = [move(outgoing[j], k, size) for j, k in enumerate(order)]
    block = LEVEL_MODULES // 2
    state_block = pl.BlockSpec((block, own_rows, width), lambda i: (i, 0, 0))
    new_state, new_moment, done = call(
        state_kernel,
        [shape(*state_in.shape)] * 2 + [shape(8, 128)],
        [smem, vmem, vmem, vmem],
        [state_block, state_block, vmem],
        grid=(module_count // block,),
    )(leaders, grad, decayed, moment_in)
    back = call(
        lambda *refs: give_back_kernel(size, *refs), by_chip, [smem] + [vmem] * rounds + [anywhere], vmem
    )(here, *returned, done)
    back = lax.ppermute(back, "path", swap)
    sems = [pltpu.SemaphoreType.DMA((LEVELS, rounds))]
    path_params = call(
        lambda *refs: own_rows_kernel(size, *refs),
        shape(*split_slab.shape),
        [smem] + [anywhere] * rounds,
        anywhere,
        scratch_shapes=sems,
    )(here, *returned)
    path_params = call(
        other_rows_kernel,
        shape(*split_slab.shape),
        [smem, anywhere, anywhere],
        anywhere,
        scratch_shapes=sems,
        input_output_aliases={2: 0},
    )(here, back, path_params)
    return (path_params.reshape(path_delta.shape), new_state[:, None], new_moment[:, None])


def local_wide(path_delta, assign, params, momentum):
    own_slab = path_delta[0]
    path_count = assign.shape[0]
    module_count, _, own_rows, width = params.shape
    entries = float(own_slab.size * lax.axis_size("shard"))
    total_sq = lax.psum(jnp.sum(own_slab * own_slab), "shard")
    scaled = own_slab * (1.0 / jnp.sqrt(total_sq / entries + 1e-06))
    received = lax.all_to_all(
        scaled.reshape(LEVELS, path_count, own_rows, width), "path", split_axis=1, concat_axis=1, tiled=True
    )
    flat_ids = (assign + LEVEL_MODULES * jnp.arange(LEVELS, dtype=jnp.int32)[None, :]).T.reshape(-1)
    member = (jnp.arange(module_count, dtype=jnp.int32)[:, None] == flat_ids[None, :]).astype(jnp.float32)
    mean = member / jnp.maximum(jnp.sum(member, axis=1), 1.0)[:, None]
    grad = jnp.einsum(
        "mp,prd->mrd", mean, received.reshape(-1, own_rows, width), precision=lax.Precision.HIGHEST
    )
    new_moment = beta_coef * momentum[:, 0] + grad
    new_state = params[:, 0] - outer_rate * (grad + beta_coef * new_moment)
    outgoing = jnp.take(new_state, flat_ids, axis=0).reshape(LEVELS, path_count, own_rows, width)
    returned = lax.all_to_all(outgoing, "path", split_axis=1, concat_axis=1, tiled=True)
    return (returned.reshape(path_delta.shape), new_state[:, None], new_moment[:, None])


def solution(mesh):
    in_specs = (
        P("path", None, "shard", None),
        P(),
        P(None, "shard", "path", None),
        P(None, "shard", "path", None),
    )
    out_specs = (
        P("path", None, "shard", None),
        P(None, "shard", "path", None),
        P(None, "shard", "path", None),
    )
    chosen = local if 4 <= mesh.shape["path"] <= MOST_UNROLLED else local_wide
    return jax.shard_map(chosen, mesh=mesh, in_specs=in_specs, out_specs=out_specs, check_vma=False)
```

```python
import jax
import jax.numpy as jnp
from jax import lax
from jax.experimental import pallas as pl
from jax.experimental.pallas import tpu as pltpu
from jax.sharding import PartitionSpec as P

LEVEL_MODULES = 16
LEVELS = 2
MOST_UNROLLED = 8
EIGHTHS = 3

outer_rate = 0.7
beta_coef = 0.9
moment_coef = outer_rate * beta_coef * beta_coef
grad_coef = outer_rate * (1.0 + beta_coef)

VMEM_LIMIT = 16 * 1024 * 1024

vmem = pl.BlockSpec(memory_space=pltpu.VMEM)
smem = pl.BlockSpec(memory_space=pltpu.SMEM)
anywhere = pl.BlockSpec(memory_space=pl.ANY)


def call(kernel, out_shape, in_specs, out_specs, **more):
    return pl.pallas_call(
        kernel,
        out_shape=out_shape,
        in_specs=in_specs,
        out_specs=out_specs,
        compiler_params=pltpu.CompilerParams(vmem_limit_bytes=VMEM_LIMIT),
        **more,
    )


def mirrored(k, size):
    if size < 8:
        return k
    return (k & ~6) | ((k & 2) << 1) | ((k & 4) >> 1)


def target(here, k, size):
    if isinstance(here, int):
        return here ^ (mirrored(k, size) if here & 1 else k)
    return here ^ jnp.where(here & 1 == 1, mirrored(k, size), k)


def origin(here, k, size):
    if isinstance(here, int):
        return here ^ (mirrored(k, size) if (here ^ k) & 1 else k)
    return here ^ jnp.where((here ^ k) & 1 == 1, mirrored(k, size), k)


def order_of(size):
    return sorted(range(2, size, 2), key=lambda k: (-bin(k).count("1"), k)) + [0]


def move(array, k, size):
    if k == 0:
        return array
    return lax.ppermute(array, "path", [(i, target(i, k, size)) for i in range(size)])


def tiles_of(rows, width):
    return [(slice(row, row + 8), slice(lane, lane + 128)) for row in range(0, rows, 8) for lane in range(0, width, 128)]


def pack_kernel(here_ref, delta_ref, square_ref, keep_ref, give_ref):
    levels, chips, halves, rows, width = delta_ref.shape

    def pack(core):
        totals = [jnp.zeros((8, 128), jnp.float32) for _ in range(4)]
        for level in range(levels):
            for chip in range(chips):
                for t, spot in enumerate(tiles_of(rows, width)):
                    kept = delta_ref[(level, chip, core, *spot)]
                    given = delta_ref[(level, chip, 1 - core, *spot)]
                    keep_ref[(level, chip, *spot)] = kept
                    give_ref[(level, chip, *spot)] = given
                    totals[t % 4] = totals[t % 4] + (kept * kept + given * given)
        total = jnp.sum((totals[0] + totals[1]) + (totals[2] + totals[3]), axis=0, keepdims=True)
        for first in range(0, square_ref.shape[0], 8):
            row = lax.broadcasted_iota(jnp.int32, (8, 128), 0) + first
            square_ref[first : first + 8] = jnp.where(row == here_ref[0], total, 0.0)

    for core in range(halves):
        pl.when(here_ref[0] & 1 == core)(lambda core=core: pack(core))


def in_first(count):
    return count * EIGHTHS // 8


def first_merge_kernel(size, here_ref, keep_ref, gift_ref, *outs):
    here = here_ref[0]
    core = here & 1
    spots = tiles_of(*keep_ref.shape[2:])
    sent = [(0, spot) for spot in spots] + [(1, spot) for spot in spots[: in_first(len(spots))]]
    for k, out in zip(order_of(size), outs):
        chip = target(here, k, size) // 2
        for source, ref in ((core, keep_ref), (1 - core, gift_ref)):
            for t, (level, spot) in enumerate(sent):
                out[source * len(sent) + t] = ref[(level, chip, *spot)]


def second_merge_kernel(size, here_ref, square_ref, other_ref, keep_ref, gift_ref, *outs):
    here = here_ref[0]
    core = here & 1
    squares = square_ref[...] + other_ref[...]
    spots = tiles_of(*keep_ref.shape[2:])
    spots = spots[in_first(len(spots)) :]
    for k, out in zip(order_of(size), outs):
        chip = target(here, k, size) // 2
        out[0] = squares
        for source, ref in ((core, keep_ref), (1 - core, gift_ref)):
            for t, spot in enumerate(spots):
                out[1 + source * len(spots) + t] = ref[(1, chip, *spot)]


def sum_kernel(count, *refs):
    total = refs[0][...]
    for ref in refs[1:count]:
        total = total + ref[...]
    refs[-1][...] = total


def decay_kernel(params_ref, decay_ref, out_ref):
    def decay(module, carry):
        out_ref[module] = params_ref[module] - decay_ref[module]
        return carry

    lax.fori_loop(0, out_ref.shape[0], decay, 0)


def plan_kernel(here_ref, ids_ref, plan_ref, module_ref):
    size = ids_ref.shape[1]
    order = order_of(size)
    here = here_ref[0]
    paths = [(origin(here, k, size) // 2) * 2 + half for k in order for half in range(2)]
    targets = [(target(here, k, size) // 2) * 2 + half for k in order for half in range(2)]
    for level in range(LEVELS):
        first = level * LEVEL_MODULES
        for module in range(LEVEL_MODULES):
            module_ref[first + module] = -1
        sources = [ids_ref[level, path] + first for path in paths]
        for i in reversed(range(size)):
            module_ref[sources[i]] = i
        for i in range(size):
            plan_ref[level, i] = module_ref[sources[i]]
            sharers = jnp.int32(0)
            for other in range(size):
                sharers = sharers + jnp.where(sources[other] == sources[i], 1, 0)
            plan_ref[level, size + i] = sharers
            plan_ref[level, 2 * size + i] = paths[i]
            module = ids_ref[level, targets[i]] + first
            plan_ref[level, 3 * size + i] = module
            plan_ref[level, 4 * size + i] = module_ref[module]


def outgoing_kernel(rounds, entries, plan_ref, decayed_ref, *refs):
    firsts, seconds = refs[:rounds], refs[rounds : 2 * rounds]
    outs, (grad_ref, rescale_ref) = refs[2 * rounds : -2], refs[-2:]
    size = 2 * rounds
    rows, width = grad_ref.shape[2:]
    spots = tiles_of(rows, width)
    count, early = len(spots), in_first(len(spots))
    squares = seconds[0][0]
    for second in seconds[1:]:
        squares = squares + second[0]
    total = jnp.sum(squares, axis=1, keepdims=True)
    rescale_ref[...] = jnp.broadcast_to(1.0 / jnp.sqrt(total / entries + 1e-06), rescale_ref.shape)
    for level in range(LEVELS):
        for i in range(size):
            rescale = jnp.broadcast_to(rescale_ref[pl.ds(plan_ref[level, 2 * size + i], 1), :], (8, 128))
            factor = rescale / jnp.full((8, 128), plan_ref[level, size + i], jnp.int32).astype(jnp.float32)
            for t, spot in enumerate(spots):
                if level == 0 or t < early:
                    block = firsts[i // 2][(i % 2) * (count + early) + level * count + t]
                else:
                    block = seconds[i // 2][1 + (i % 2) * (count - early) + t - early]
                grad_ref[(level, i, *spot)] = block * factor
        for i in range(1, size):
            leader = plan_ref[level, i]

            @pl.when(leader != i)
            def _():
                grad_ref[level, leader] += grad_ref[level, i]

        for i in range(size):
            decayed = decayed_ref[plan_ref[level, 3 * size + i]]
            outs[i // 2][i % 2, level] = decayed - grad_coef * grad_ref[level, plan_ref[level, 4 * size + i]]


def state_kernel(module_ref, grad_ref, decayed_ref, momentum_ref, new_params_ref, new_momentum_ref, token_ref):
    token_ref[...] = jnp.zeros_like(token_ref)
    count = new_params_ref.shape[0]
    first = pl.program_id(0) * count
    level = first // LEVEL_MODULES
    for place in range(count):
        module = first + place
        leader = module_ref[module]
        taken = jnp.where(leader < 0, 0.0, 1.0)
        grad = taken * grad_ref[level, jnp.maximum(leader, 0)]
        new_momentum_ref[place] = beta_coef * momentum_ref[module] + grad
        new_params_ref[place] = decayed_ref[module] - grad_coef * grad


def give_back_kernel(size, here_ref, *refs):
    here = here_ref[0]
    for j, k in enumerate(order_of(size)):
        for level in range(LEVELS):
            refs[-1][level, origin(here, k, size) // 2] = refs[j][1 - (here & 1), level]


def own_rows_kernel(size, here_ref, *refs):
    here = here_ref[0]
    core = here & 1
    out_ref, sems = refs[-2:]
    copies = []
    for j, k in enumerate(order_of(size)):
        chip = origin(here, k, size) // 2
        for level in range(LEVELS):
            copies.append(
                pltpu.make_async_copy(refs[j].at[core, level], out_ref.at[level, chip, core], sems.at[level, j])
            )
    for copy in copies:
        copy.start()
    for copy in copies:
        copy.wait()


def other_rows_kernel(here_ref, back_ref, held_ref, out_ref, sems):
    del held_ref
    core = here_ref[0] & 1
    copies = []
    for level in range(LEVELS):
        for chip in range(back_ref.shape[1]):
            copies.append(
                pltpu.make_async_copy(
                    back_ref.at[level, chip], out_ref.at[level, chip, 1 - core], sems.at[level, chip]
                )
            )
    for copy in copies:
        copy.start()
    for copy in copies:
        copy.wait()


def local(path_delta, assign, params, momentum):
    own_slab = path_delta[0]
    size = assign.shape[0]
    module_count, _, own_rows, width = params.shape
    shards = lax.axis_size("shard")
    entries = float(own_slab.size * shards)
    state_in = params.reshape(module_count, own_rows, width)
    moment_in = momentum.reshape(module_count, own_rows, width)
    split_slab = own_slab.reshape(LEVELS, size // 2, 2, own_rows, width)
    here = lax.axis_index("path").astype(jnp.int32).reshape(1)
    order = order_of(size)
    rounds = len(order)
    swap = [(i, i ^ 1) for i in range(size)]
    shape = lambda *dims: jax.ShapeDtypeStruct(dims, jnp.float32)
    squares_shape = shape(-(-size // 8) * 8, 128)
    by_chip = shape(LEVELS, rounds, own_rows, width)
    message = shape(2, LEVELS, own_rows, width)
    count = own_rows * width // 1024

    squares, keep, give = call(pack_kernel, [squares_shape, by_chip, by_chip], [smem, vmem], [vmem] * 3)(
        here, split_slab
    )
    gift = lax.ppermute(give, "path", swap)
    tiles = [squares] + [
        lax.ppermute(squares, "shard", [(i, i ^ step) for i in range(shards)]) for step in range(shards - 1, 0, -1)
    ]
    firsts = call(
        lambda *refs: first_merge_kernel(size, *refs),
        [shape(2 * (count + in_first(count)), 8, 128)] * rounds,
        [smem, vmem, vmem],
        [vmem] * rounds,
    )(here, keep, gift)
    firsts = [move(firsts[j], k, size) for j, k in enumerate(order)]
    decay = moment_coef * moment_in
    decayed = call(decay_kernel, shape(*state_in.shape), [vmem, vmem], vmem)(state_in, decay)
    plan, leaders = call(
        plan_kernel,
        [
            jax.ShapeDtypeStruct((LEVELS, 5 * size), jnp.int32),
            jax.ShapeDtypeStruct((module_count,), jnp.int32),
        ],
        [smem, smem],
        [smem, smem],
    )(here, assign.T)
    squares = call(
        lambda *refs: sum_kernel(shards, *refs), squares_shape, [vmem] * shards + [anywhere], vmem
    )(*tiles, decay)
    other = lax.ppermute(squares, "path", swap)
    seconds = call(
        lambda *refs: second_merge_kernel(size, *refs),
        [shape(1 + 2 * (count - in_first(count)), 8, 128)] * rounds,
        [smem] + [vmem] * 4,
        [vmem] * rounds,
    )(here, squares, other, keep, gift)
    seconds = [move(seconds[j], k, size) for j, k in enumerate(order)]

    *outgoing, grad = call(
        lambda *refs: outgoing_kernel(rounds, entries, *refs),
        [message] * rounds + [shape(LEVELS, size, own_rows, width)],
        [smem] + [vmem] * (1 + 2 * rounds),
        [vmem] * (rounds + 1),
        scratch_shapes=[pltpu.VMEM(squares_shape.shape, jnp.float32)],
    )(plan, decayed, *firsts, *seconds)
    returned = [move(outgoing[j], k, size) for j, k in enumerate(order)]
    block = LEVEL_MODULES // 2
    state_block = pl.BlockSpec((block, own_rows, width), lambda i: (i, 0, 0))
    new_state, new_moment, done = call(
        state_kernel,
        [shape(*state_in.shape)] * 2 + [shape(8, 128)],
        [smem, vmem, vmem, vmem],
        [state_block, state_block, vmem],
        grid=(module_count // block,),
    )(leaders, grad, decayed, moment_in)
    back = call(
        lambda *refs: give_back_kernel(size, *refs), by_chip, [smem] + [vmem] * rounds + [anywhere], vmem
    )(here, *returned, done)
    back = lax.ppermute(back, "path", swap)
    sems = [pltpu.SemaphoreType.DMA((LEVELS, rounds))]
    path_params = call(
        lambda *refs: own_rows_kernel(size, *refs),
        shape(*split_slab.shape),
        [smem] + [anywhere] * rounds,
        anywhere,
        scratch_shapes=sems,
    )(here, *returned)
    path_params = call(
        other_rows_kernel,
        shape(*split_slab.shape),
        [smem, anywhere, anywhere],
        anywhere,
        scratch_shapes=sems,
        input_output_aliases={2: 0},
    )(here, back, path_params)
    return (path_params.reshape(path_delta.shape), new_state[:, None], new_moment[:, None])


def local_wide(path_delta, assign, params, momentum):
    own_slab = path_delta[0]
    path_count = assign.shape[0]
    module_count, _, own_rows, width = params.shape
    entries = float(own_slab.size * lax.axis_size("shard"))
    total_sq = lax.psum(jnp.sum(own_slab * own_slab), "shard")
    scaled = own_slab * (1.0 / jnp.sqrt(total_sq / entries + 1e-06))
    received = lax.all_to_all(
        scaled.reshape(LEVELS, path_count, own_rows, width), "path", split_axis=1, concat_axis=1, tiled=True
    )
    flat_ids = (assign + LEVEL_MODULES * jnp.arange(LEVELS, dtype=jnp.int32)[None, :]).T.reshape(-1)
    member = (jnp.arange(module_count, dtype=jnp.int32)[:, None] == flat_ids[None, :]).astype(jnp.float32)
    mean = member / jnp.maximum(jnp.sum(member, axis=1), 1.0)[:, None]
    grad = jnp.einsum(
        "mp,prd->mrd", mean, received.reshape(-1, own_rows, width), precision=lax.Precision.HIGHEST
    )
    new_moment = beta_coef * momentum[:, 0] + grad
    new_state = params[:, 0] - outer_rate * (grad + beta_coef * new_moment)
    outgoing = jnp.take(new_state, flat_ids, axis=0).reshape(LEVELS, path_count, own_rows, width)
    returned = lax.all_to_all(outgoing, "path", split_axis=1, concat_axis=1, tiled=True)
    return (returned.reshape(path_delta.shape), new_state[:, None], new_moment[:, None])


def solution(mesh):
    in_specs = (
        P("path", None, "shard", None),
        P(),
        P(None, "shard", "path", None),
        P(None, "shard", "path", None),
    )
    out_specs = (
        P("path", None, "shard", None),
        P(None, "shard", "path", None),
        P(None, "shard", "path", None),
    )
    chosen = local if 4 <= mesh.shape["path"] <= MOST_UNROLLED else local_wide
    return jax.shard_map(chosen, mesh=mesh, in_specs=in_specs, out_specs=out_specs, check_vma=False)
```

```python
import jax
import jax.numpy as jnp
from jax import lax
from jax.experimental import pallas as pl
from jax.experimental.pallas import tpu as pltpu
from jax.sharding import PartitionSpec as P

LEVEL_MODULES = 16
LEVELS = 2
MOST_UNROLLED = 8
EIGHTHS = 5

outer_rate = 0.7
beta_coef = 0.9
moment_coef = outer_rate * beta_coef * beta_coef
grad_coef = outer_rate * (1.0 + beta_coef)

VMEM_LIMIT = 16 * 1024 * 1024

vmem = pl.BlockSpec(memory_space=pltpu.VMEM)
smem = pl.BlockSpec(memory_space=pltpu.SMEM)
anywhere = pl.BlockSpec(memory_space=pl.ANY)


def call(kernel, out_shape, in_specs, out_specs, **more):
    return pl.pallas_call(
        kernel,
        out_shape=out_shape,
        in_specs=in_specs,
        out_specs=out_specs,
        compiler_params=pltpu.CompilerParams(vmem_limit_bytes=VMEM_LIMIT),
        **more,
    )


def mirrored(k, size):
    if size < 8:
        return k
    return (k & ~6) | ((k & 2) << 1) | ((k & 4) >> 1)


def target(here, k, size):
    if isinstance(here, int):
        return here ^ (mirrored(k, size) if here & 1 else k)
    return here ^ jnp.where(here & 1 == 1, mirrored(k, size), k)


def origin(here, k, size):
    if isinstance(here, int):
        return here ^ (mirrored(k, size) if (here ^ k) & 1 else k)
    return here ^ jnp.where((here ^ k) & 1 == 1, mirrored(k, size), k)


def order_of(size):
    return sorted(range(2, size, 2), key=lambda k: (-bin(k).count("1"), k)) + [0]


def move(array, k, size):
    if k == 0:
        return array
    return lax.ppermute(array, "path", [(i, target(i, k, size)) for i in range(size)])


def tiles_of(rows, width):
    return [(slice(row, row + 8), slice(lane, lane + 128)) for row in range(0, rows, 8) for lane in range(0, width, 128)]


def pack_kernel(here_ref, delta_ref, square_ref, keep_ref, give_ref):
    levels, chips, halves, rows, width = delta_ref.shape

    def pack(core):
        totals = [jnp.zeros((8, 128), jnp.float32) for _ in range(4)]
        for level in range(levels):
            for chip in range(chips):
                for t, spot in enumerate(tiles_of(rows, width)):
                    kept = delta_ref[(level, chip, core, *spot)]
                    given = delta_ref[(level, chip, 1 - core, *spot)]
                    keep_ref[(level, chip, *spot)] = kept
                    give_ref[(level, chip, *spot)] = given
                    totals[t % 4] = totals[t % 4] + (kept * kept + given * given)
        total = jnp.sum((totals[0] + totals[1]) + (totals[2] + totals[3]), axis=0, keepdims=True)
        for first in range(0, square_ref.shape[0], 8):
            row = lax.broadcasted_iota(jnp.int32, (8, 128), 0) + first
            square_ref[first : first + 8] = jnp.where(row == here_ref[0], total, 0.0)

    for core in range(halves):
        pl.when(here_ref[0] & 1 == core)(lambda core=core: pack(core))


def in_first(count):
    return count * EIGHTHS // 8


def first_merge_kernel(size, here_ref, keep_ref, gift_ref, *outs):
    here = here_ref[0]
    core = here & 1
    spots = tiles_of(*keep_ref.shape[2:])
    sent = [(0, spot) for spot in spots] + [(1, spot) for spot in spots[: in_first(len(spots))]]
    for k, out in zip(order_of(size), outs):
        chip = target(here, k, size) // 2
        for source, ref in ((core, keep_ref), (1 - core, gift_ref)):
            for t, (level, spot) in enumerate(sent):
                out[source * len(sent) + t] = ref[(level, chip, *spot)]


def second_merge_kernel(size, here_ref, square_ref, other_ref, keep_ref, gift_ref, *outs):
    here = here_ref[0]
    core = here & 1
    squares = square_ref[...] + other_ref[...]
    spots = tiles_of(*keep_ref.shape[2:])
    spots = spots[in_first(len(spots)) :]
    for k, out in zip(order_of(size), outs):
        chip = target(here, k, size) // 2
        out[0] = squares
        for source, ref in ((core, keep_ref), (1 - core, gift_ref)):
            for t, spot in enumerate(spots):
                out[1 + source * len(spots) + t] = ref[(1, chip, *spot)]


def add_kernel(a_ref, b_ref, out_ref):
    out_ref[...] = a_ref[...] + b_ref[...]


def decay_kernel(params_ref, momentum_ref, out_ref):
    def decay(module, carry):
        out_ref[module] = params_ref[module] - moment_coef * momentum_ref[module]
        return carry

    lax.fori_loop(0, out_ref.shape[0], decay, 0)


def plan_kernel(here_ref, ids_ref, plan_ref, module_ref):
    size = ids_ref.shape[1]
    order = order_of(size)
    here = here_ref[0]
    paths = [(origin(here, k, size) // 2) * 2 + half for k in order for half in range(2)]
    targets = [(target(here, k, size) // 2) * 2 + half for k in order for half in range(2)]
    for level in range(LEVELS):
        first = level * LEVEL_MODULES
        for module in range(LEVEL_MODULES):
            module_ref[first + module] = -1
        sources = [ids_ref[level, path] + first for path in paths]
        for i in reversed(range(size)):
            module_ref[sources[i]] = i
        for i in range(size):
            plan_ref[level, i] = module_ref[sources[i]]
            sharers = jnp.int32(0)
            for other in range(size):
                sharers = sharers + jnp.where(sources[other] == sources[i], 1, 0)
            plan_ref[level, size + i] = sharers
            plan_ref[level, 2 * size + i] = paths[i]
            module = ids_ref[level, targets[i]] + first
            plan_ref[level, 3 * size + i] = module
            plan_ref[level, 4 * size + i] = module_ref[module]


def outgoing_kernel(rounds, entries, plan_ref, decayed_ref, *refs):
    firsts, seconds = refs[:rounds], refs[rounds : 2 * rounds]
    outs, (grad_ref, rescale_ref) = refs[2 * rounds : -2], refs[-2:]
    size = 2 * rounds
    rows, width = grad_ref.shape[2:]
    spots = tiles_of(rows, width)
    count, early = len(spots), in_first(len(spots))
    squares = seconds[0][0]
    for second in seconds[1:]:
        squares = squares + second[0]
    total = jnp.sum(squares, axis=1, keepdims=True)
    rescale_ref[...] = jnp.broadcast_to(1.0 / jnp.sqrt(total / entries + 1e-06), rescale_ref.shape)
    for level in range(LEVELS):
        for i in range(size):
            rescale = jnp.broadcast_to(rescale_ref[pl.ds(plan_ref[level, 2 * size + i], 1), :], (8, 128))
            factor = rescale / jnp.full((8, 128), plan_ref[level, size + i], jnp.int32).astype(jnp.float32)
            for t, spot in enumerate(spots):
                if level == 0 or t < early:
                    block = firsts[i // 2][(i % 2) * (count + early) + level * count + t]
                else:
                    block = seconds[i // 2][1 + (i % 2) * (count - early) + t - early]
                grad_ref[(level, i, *spot)] = block * factor
        for i in range(1, size):
            leader = plan_ref[level, i]

            @pl.when(leader != i)
            def _():
                grad_ref[level, leader] += grad_ref[level, i]

        for i in range(size):
            decayed = decayed_ref[plan_ref[level, 3 * size + i]]
            outs[i // 2][i % 2, level] = decayed - grad_coef * grad_ref[level, plan_ref[level, 4 * size + i]]


def state_kernel(module_ref, grad_ref, decayed_ref, momentum_ref, new_params_ref, new_momentum_ref, token_ref):
    token_ref[...] = jnp.zeros_like(token_ref)
    count = new_params_ref.shape[0]
    first = pl.program_id(0) * count
    level = first // LEVEL_MODULES
    for place in range(count):
        module = first + place
        leader = module_ref[module]
        taken = jnp.where(leader < 0, 0.0, 1.0)
        grad = taken * grad_ref[level, jnp.maximum(leader, 0)]
        new_momentum_ref[place] = beta_coef * momentum_ref[module] + grad
        new_params_ref[place] = decayed_ref[module] - grad_coef * grad


def give_back_kernel(size, here_ref, *refs):
    here = here_ref[0]
    for j, k in enumerate(order_of(size)):
        for level in range(LEVELS):
            refs[-1][level, origin(here, k, size) // 2] = refs[j][1 - (here & 1), level]


def own_rows_kernel(size, here_ref, *refs):
    here = here_ref[0]
    core = here & 1
    out_ref, sems = refs[-2:]
    copies = []
    for j, k in enumerate(order_of(size)):
        chip = origin(here, k, size) // 2
        for level in range(LEVELS):
            copies.append(
                pltpu.make_async_copy(refs[j].at[core, level], out_ref.at[level, chip, core], sems.at[level, j])
            )
    for copy in copies:
        copy.start()
    for copy in copies:
        copy.wait()


def other_rows_kernel(here_ref, back_ref, held_ref, out_ref, sems):
    del held_ref
    core = here_ref[0] & 1
    copies = []
    for level in range(LEVELS):
        for chip in range(back_ref.shape[1]):
            copies.append(
                pltpu.make_async_copy(
                    back_ref.at[level, chip], out_ref.at[level, chip, 1 - core], sems.at[level, chip]
                )
            )
    for copy in copies:
        copy.start()
    for copy in copies:
        copy.wait()


def local(path_delta, assign, params, momentum):
    own_slab = path_delta[0]
    size = assign.shape[0]
    module_count, _, own_rows, width = params.shape
    shards = lax.axis_size("shard")
    entries = float(own_slab.size * shards)
    state_in = params.reshape(module_count, own_rows, width)
    moment_in = momentum.reshape(module_count, own_rows, width)
    split_slab = own_slab.reshape(LEVELS, size // 2, 2, own_rows, width)
    here = lax.axis_index("path").astype(jnp.int32).reshape(1)
    order = order_of(size)
    rounds = len(order)
    swap = [(i, i ^ 1) for i in range(size)]
    shape = lambda *dims: jax.ShapeDtypeStruct(dims, jnp.float32)
    squares_shape = shape(-(-size // 8) * 8, 128)
    by_chip = shape(LEVELS, rounds, own_rows, width)
    message = shape(2, LEVELS, own_rows, width)
    count = own_rows * width // 1024

    squares, keep, give = call(pack_kernel, [squares_shape, by_chip, by_chip], [smem, vmem], [vmem] * 3)(
        here, split_slab
    )
    gift = lax.ppermute(give, "path", swap)
    firsts = call(
        lambda *refs: first_merge_kernel(size, *refs),
        [shape(2 * (count + in_first(count)), 8, 128)] * rounds,
        [smem, vmem, vmem],
        [vmem] * rounds,
    )(here, keep, gift)
    firsts = [move(firsts[j], k, size) for j, k in enumerate(order)]
    decayed = call(decay_kernel, shape(*state_in.shape), [vmem, vmem], vmem)(state_in, moment_in)
    plan, leaders = call(
        plan_kernel,
        [
            jax.ShapeDtypeStruct((LEVELS, 5 * size), jnp.int32),
            jax.ShapeDtypeStruct((module_count,), jnp.int32),
        ],
        [smem, smem],
        [smem, smem],
    )(here, assign.T)
    step = shards // 2
    while step:
        other = lax.ppermute(squares, "shard", [(i, i ^ step) for i in range(shards)])
        squares = call(add_kernel, squares_shape, [vmem, vmem], vmem)(squares, other)
        step //= 2
    other = lax.ppermute(squares, "path", swap)
    seconds = call(
        lambda *refs: second_merge_kernel(size, *refs),
        [shape(1 + 2 * (count - in_first(count)), 8, 128)] * rounds,
        [smem] + [vmem] * 4,
        [vmem] * rounds,
    )(here, squares, other, keep, gift)
    seconds = [move(seconds[j], k, size) for j, k in enumerate(order)]

    *outgoing, grad = call(
        lambda *refs: outgoing_kernel(rounds, entries, *refs),
        [message] * rounds + [shape(LEVELS, size, own_rows, width)],
        [smem] + [vmem] * (1 + 2 * rounds),
        [vmem] * (rounds + 1),
        scratch_shapes=[pltpu.VMEM(squares_shape.shape, jnp.float32)],
    )(plan, decayed, *firsts, *seconds)
    returned = [move(outgoing[j], k, size) for j, k in enumerate(order)]
    block = LEVEL_MODULES // 2
    state_block = pl.BlockSpec((block, own_rows, width), lambda i: (i, 0, 0))
    new_state, new_moment, done = call(
        state_kernel,
        [shape(*state_in.shape)] * 2 + [shape(8, 128)],
        [smem, vmem, vmem, vmem],
        [state_block, state_block, vmem],
        grid=(module_count // block,),
    )(leaders, grad, decayed, moment_in)
    back = call(
        lambda *refs: give_back_kernel(size, *refs), by_chip, [smem] + [vmem] * rounds + [anywhere], vmem
    )(here, *returned, done)
    back = lax.ppermute(back, "path", swap)
    sems = [pltpu.SemaphoreType.DMA((LEVELS, rounds))]
    path_params = call(
        lambda *refs: own_rows_kernel(size, *refs),
        shape(*split_slab.shape),
        [smem] + [anywhere] * rounds,
        anywhere,
        scratch_shapes=sems,
    )(here, *returned)
    path_params = call(
        other_rows_kernel,
        shape(*split_slab.shape),
        [smem, anywhere, anywhere],
        anywhere,
        scratch_shapes=sems,
        input_output_aliases={2: 0},
    )(here, back, path_params)
    return (path_params.reshape(path_delta.shape), new_state[:, None], new_moment[:, None])


def local_wide(path_delta, assign, params, momentum):
    own_slab = path_delta[0]
    path_count = assign.shape[0]
    module_count, _, own_rows, width = params.shape
    entries = float(own_slab.size * lax.axis_size("shard"))
    total_sq = lax.psum(jnp.sum(own_slab * own_slab), "shard")
    scaled = own_slab * (1.0 / jnp.sqrt(total_sq / entries + 1e-06))
    received = lax.all_to_all(
        scaled.reshape(LEVELS, path_count, own_rows, width), "path", split_axis=1, concat_axis=1, tiled=True
    )
    flat_ids = (assign + LEVEL_MODULES * jnp.arange(LEVELS, dtype=jnp.int32)[None, :]).T.reshape(-1)
    member = (jnp.arange(module_count, dtype=jnp.int32)[:, None] == flat_ids[None, :]).astype(jnp.float32)
    mean = member / jnp.maximum(jnp.sum(member, axis=1), 1.0)[:, None]
    grad = jnp.einsum(
        "mp,prd->mrd", mean, received.reshape(-1, own_rows, width), precision=lax.Precision.HIGHEST
    )
    new_moment = beta_coef * momentum[:, 0] + grad
    new_state = params[:, 0] - outer_rate * (grad + beta_coef * new_moment)
    outgoing = jnp.take(new_state, flat_ids, axis=0).reshape(LEVELS, path_count, own_rows, width)
    returned = lax.all_to_all(outgoing, "path", split_axis=1, concat_axis=1, tiled=True)
    return (returned.reshape(path_delta.shape), new_state[:, None], new_moment[:, None])


def solution(mesh):
    in_specs = (
        P("path", None, "shard", None),
        P(),
        P(None, "shard", "path", None),
        P(None, "shard", "path", None),
    )
    out_specs = (
        P("path", None, "shard", None),
        P(None, "shard", "path", None),
        P(None, "shard", "path", None),
    )
    chosen = local if 4 <= mesh.shape["path"] <= MOST_UNROLLED else local_wide
    return jax.shard_map(chosen, mesh=mesh, in_specs=in_specs, out_specs=out_specs, check_vma=False)
```

```python
import jax
import jax.numpy as jnp
from jax import lax
from jax.experimental import pallas as pl
from jax.experimental.pallas import tpu as pltpu
from jax.sharding import PartitionSpec as P

LEVEL_MODULES = 16
LEVELS = 2
MOST_UNROLLED = 8
EIGHTHS = 3

outer_rate = 0.7
beta_coef = 0.9
moment_coef = outer_rate * beta_coef * beta_coef
grad_coef = outer_rate * (1.0 + beta_coef)

VMEM_LIMIT = 16 * 1024 * 1024

vmem = pl.BlockSpec(memory_space=pltpu.VMEM)
smem = pl.BlockSpec(memory_space=pltpu.SMEM)
anywhere = pl.BlockSpec(memory_space=pl.ANY)


def call(kernel, out_shape, in_specs, out_specs, **more):
    return pl.pallas_call(
        kernel,
        out_shape=out_shape,
        in_specs=in_specs,
        out_specs=out_specs,
        compiler_params=pltpu.CompilerParams(vmem_limit_bytes=VMEM_LIMIT),
        **more,
    )


def mirrored(k, size):
    if size < 8:
        return k
    return (k & ~6) | ((k & 2) << 1) | ((k & 4) >> 1)


def target(here, k, size):
    if isinstance(here, int):
        return here ^ (mirrored(k, size) if here & 1 else k)
    return here ^ jnp.where(here & 1 == 1, mirrored(k, size), k)


def origin(here, k, size):
    if isinstance(here, int):
        return here ^ (mirrored(k, size) if (here ^ k) & 1 else k)
    return here ^ jnp.where((here ^ k) & 1 == 1, mirrored(k, size), k)


def order_of(size):
    return sorted(range(2, size, 2), key=lambda k: (-bin(k).count("1"), k)) + [0]


def move(array, k, size):
    if k == 0:
        return array
    return lax.ppermute(array, "path", [(i, target(i, k, size)) for i in range(size)])


def tiles_of(rows, width):
    return [(slice(row, row + 8), slice(lane, lane + 128)) for row in range(0, rows, 8) for lane in range(0, width, 128)]


def pack_kernel(here_ref, delta_ref, square_ref, keep_ref, give_ref):
    levels, chips, halves, rows, width = delta_ref.shape

    def pack(core):
        totals = [jnp.zeros((8, 128), jnp.float32) for _ in range(4)]
        for level in range(levels):
            for chip in range(chips):
                for t, spot in enumerate(tiles_of(rows, width)):
                    kept = delta_ref[(level, chip, core, *spot)]
                    given = delta_ref[(level, chip, 1 - core, *spot)]
                    keep_ref[(level, chip, *spot)] = kept
                    give_ref[(level, chip, *spot)] = given
                    totals[t % 4] = totals[t % 4] + (kept * kept + given * given)
        total = jnp.sum((totals[0] + totals[1]) + (totals[2] + totals[3]), axis=0, keepdims=True)
        for first in range(0, square_ref.shape[0], 8):
            row = lax.broadcasted_iota(jnp.int32, (8, 128), 0) + first
            square_ref[first : first + 8] = jnp.where(row == here_ref[0], total, 0.0)

    for core in range(halves):
        pl.when(here_ref[0] & 1 == core)(lambda core=core: pack(core))


def in_first(count):
    return count * EIGHTHS // 8


def first_merge_kernel(size, here_ref, keep_ref, gift_ref, *outs):
    here = here_ref[0]
    core = here & 1
    spots = tiles_of(*keep_ref.shape[2:])
    sent = [(0, spot) for spot in spots] + [(1, spot) for spot in spots[: in_first(len(spots))]]
    for k, out in zip(order_of(size), outs):
        chip = target(here, k, size) // 2
        for source, ref in ((core, keep_ref), (1 - core, gift_ref)):
            for t, (level, spot) in enumerate(sent):
                out[source * len(sent) + t] = ref[(level, chip, *spot)]


def second_merge_kernel(size, here_ref, square_ref, other_ref, keep_ref, gift_ref, *outs):
    here = here_ref[0]
    core = here & 1
    squares = square_ref[...] + other_ref[...]
    spots = tiles_of(*keep_ref.shape[2:])
    spots = spots[in_first(len(spots)) :]
    for k, out in zip(order_of(size), outs):
        chip = target(here, k, size) // 2
        out[0] = squares
        for source, ref in ((core, keep_ref), (1 - core, gift_ref)):
            for t, spot in enumerate(spots):
                out[1 + source * len(spots) + t] = ref[(1, chip, *spot)]


def sum_kernel(count, *refs):
    total = refs[0][...]
    for ref in refs[1:count]:
        total = total + ref[...]
    refs[-1][...] = total


def decay_kernel(params_ref, decay_ref, out_ref):
    def decay(module, carry):
        out_ref[module] = params_ref[module] - decay_ref[module]
        return carry

    lax.fori_loop(0, out_ref.shape[0], decay, 0)


def plan_kernel(here_ref, ids_ref, plan_ref, module_ref):
    size = ids_ref.shape[1]
    order = order_of(size)
    here = here_ref[0]
    paths = [(origin(here, k, size) // 2) * 2 + half for k in order for half in range(2)]
    targets = [(target(here, k, size) // 2) * 2 + half for k in order for half in range(2)]
    for level in range(LEVELS):
        first = level * LEVEL_MODULES
        for module in range(LEVEL_MODULES):
            module_ref[first + module] = -1
        sources = [ids_ref[level, path] + first for path in paths]
        for i in reversed(range(size)):
            module_ref[sources[i]] = i
        for i in range(size):
            plan_ref[level, i] = module_ref[sources[i]]
            sharers = jnp.int32(0)
            for other in range(size):
                sharers = sharers + jnp.where(sources[other] == sources[i], 1, 0)
            plan_ref[level, size + i] = sharers
            plan_ref[level, 2 * size + i] = paths[i]
            module = ids_ref[level, targets[i]] + first
            plan_ref[level, 3 * size + i] = module
            plan_ref[level, 4 * size + i] = module_ref[module]


def outgoing_kernel(rounds, entries, plan_ref, decayed_ref, *refs):
    firsts, seconds = refs[:rounds], refs[rounds : 2 * rounds]
    outs, (grad_ref, rescale_ref) = refs[2 * rounds : -2], refs[-2:]
    size = 2 * rounds
    rows, width = grad_ref.shape[2:]
    spots = tiles_of(rows, width)
    count, early = len(spots), in_first(len(spots))
    squares = seconds[0][0]
    for second in seconds[1:]:
        squares = squares + second[0]
    total = jnp.sum(squares, axis=1, keepdims=True)
    rescale_ref[...] = jnp.broadcast_to(1.0 / jnp.sqrt(total / entries + 1e-06), rescale_ref.shape)
    for level in range(LEVELS):
        for i in range(size):
            rescale = jnp.broadcast_to(rescale_ref[pl.ds(plan_ref[level, 2 * size + i], 1), :], (8, 128))
            factor = rescale / jnp.full((8, 128), plan_ref[level, size + i], jnp.int32).astype(jnp.float32)
            for t, spot in enumerate(spots):
                if level == 0 or t < early:
                    block = firsts[i // 2][(i % 2) * (count + early) + level * count + t]
                else:
                    block = seconds[i // 2][1 + (i % 2) * (count - early) + t - early]
                grad_ref[(level, i, *spot)] = block * factor
        for i in range(1, size):
            leader = plan_ref[level, i]

            @pl.when(leader != i)
            def _():
                grad_ref[level, leader] += grad_ref[level, i]

        for i in range(size):
            decayed = decayed_ref[plan_ref[level, 3 * size + i]]
            outs[i // 2][i % 2, level] = decayed - grad_coef * grad_ref[level, plan_ref[level, 4 * size + i]]


def state_kernel(module_ref, grad_ref, decayed_ref, momentum_ref, new_params_ref, new_momentum_ref, token_ref):
    token_ref[...] = jnp.zeros_like(token_ref)
    count = new_params_ref.shape[0]
    first = pl.program_id(0) * count
    level = first // LEVEL_MODULES
    for place in range(count):
        module = first + place
        leader = module_ref[module]
        taken = jnp.where(leader < 0, 0.0, 1.0)
        grad = taken * grad_ref[level, jnp.maximum(leader, 0)]
        new_momentum_ref[place] = beta_coef * momentum_ref[module] + grad
        new_params_ref[place] = decayed_ref[module] - grad_coef * grad


def give_back_kernel(count, here_ref, *refs):
    for i in range(count):
        refs[-1][i] = refs[i][1 - (here_ref[0] & 1)]


def first_rows_kernel(size, first, here_ref, back_ref, *refs):
    here = here_ref[0]
    core = here & 1
    out_ref, sems = refs[-2:]
    copies = []
    for j, k in enumerate(order_of(size)):
        chip = origin(here, k, size) // 2
        for level in range(LEVELS):
            copies.append(
                pltpu.make_async_copy(refs[j].at[core, level], out_ref.at[level, chip, core], sems.at[0, level, j])
            )
    for i, k in enumerate(first):
        chip = origin(here ^ 1, k, size) // 2
        for level in range(LEVELS):
            copies.append(
                pltpu.make_async_copy(
                    back_ref.at[i, level], out_ref.at[level, chip, 1 - core], sems.at[1, level, i]
                )
            )
    for copy in copies:
        copy.start()
    for copy in copies:
        copy.wait()


def last_rows_kernel(size, last, here_ref, back_ref, held_ref, out_ref, sems):
    del held_ref
    here = here_ref[0]
    copies = []
    for i, k in enumerate(last):
        chip = origin(here ^ 1, k, size) // 2
        for level in range(LEVELS):
            copies.append(
                pltpu.make_async_copy(
                    back_ref.at[i, level], out_ref.at[level, chip, 1 - (here & 1)], sems.at[level, i]
                )
            )
    for copy in copies:
        copy.start()
    for copy in copies:
        copy.wait()


def local(path_delta, assign, params, momentum):
    own_slab = path_delta[0]
    size = assign.shape[0]
    module_count, _, own_rows, width = params.shape
    shards = lax.axis_size("shard")
    entries = float(own_slab.size * shards)
    state_in = params.reshape(module_count, own_rows, width)
    moment_in = momentum.reshape(module_count, own_rows, width)
    split_slab = own_slab.reshape(LEVELS, size // 2, 2, own_rows, width)
    here = lax.axis_index("path").astype(jnp.int32).reshape(1)
    order = order_of(size)
    rounds = len(order)
    swap = [(i, i ^ 1) for i in range(size)]
    shape = lambda *dims: jax.ShapeDtypeStruct(dims, jnp.float32)
    squares_shape = shape(-(-size // 8) * 8, 128)
    by_chip = shape(LEVELS, rounds, own_rows, width)
    message = shape(2, LEVELS, own_rows, width)
    count = own_rows * width // 1024

    squares, keep, give = call(pack_kernel, [squares_shape, by_chip, by_chip], [smem, vmem], [vmem] * 3)(
        here, split_slab
    )
    gift = lax.ppermute(give, "path", swap)
    tiles = [squares] + [
        lax.ppermute(squares, "shard", [(i, i ^ step) for i in range(shards)]) for step in range(shards - 1, 0, -1)
    ]
    firsts = call(
        lambda *refs: first_merge_kernel(size, *refs),
        [shape(2 * (count + in_first(count)), 8, 128)] * rounds,
        [smem, vmem, vmem],
        [vmem] * rounds,
    )(here, keep, gift)
    firsts = [move(firsts[j], k, size) for j, k in enumerate(order)]
    decay = moment_coef * moment_in
    decayed = call(decay_kernel, shape(*state_in.shape), [vmem, vmem], vmem)(state_in, decay)
    plan, leaders = call(
        plan_kernel,
        [
            jax.ShapeDtypeStruct((LEVELS, 5 * size), jnp.int32),
            jax.ShapeDtypeStruct((module_count,), jnp.int32),
        ],
        [smem, smem],
        [smem, smem],
    )(here, assign.T)
    squares = call(
        lambda *refs: sum_kernel(shards, *refs), squares_shape, [vmem] * shards + [anywhere], vmem
    )(*tiles, decay)
    other = lax.ppermute(squares, "path", swap)
    seconds = call(
        lambda *refs: second_merge_kernel(size, *refs),
        [shape(1 + 2 * (count - in_first(count)), 8, 128)] * rounds,
        [smem] + [vmem] * 4,
        [vmem] * rounds,
    )(here, squares, other, keep, gift)
    seconds = [move(seconds[j], k, size) for j, k in enumerate(order)]

    *outgoing, grad = call(
        lambda *refs: outgoing_kernel(rounds, entries, *refs),
        [message] * rounds + [shape(LEVELS, size, own_rows, width)],
        [smem] + [vmem] * (1 + 2 * rounds),
        [vmem] * (rounds + 1),
        scratch_shapes=[pltpu.VMEM(squares_shape.shape, jnp.float32)],
    )(plan, decayed, *firsts, *seconds)
    returned = [move(outgoing[j], k, size) for j, k in enumerate(order)]
    block = LEVEL_MODULES // 2
    state_block = pl.BlockSpec((block, own_rows, width), lambda i: (i, 0, 0))
    new_state, new_moment, done = call(
        state_kernel,
        [shape(*state_in.shape)] * 2 + [shape(8, 128)],
        [smem, vmem, vmem, vmem],
        [state_block, state_block, vmem],
        grid=(module_count // block,),
    )(leaders, grad, decayed, moment_in)
    first, last = [*order[:-2], order[-1]], order[-2:-1]
    blocks = dict(zip(order, returned))
    backs = []
    for part in (first, last):
        back = call(
            lambda *refs, count=len(part): give_back_kernel(count, *refs),
            shape(len(part), LEVELS, own_rows, width),
            [smem] + [vmem] * len(part) + [anywhere],
            vmem,
        )(here, *[blocks[k] for k in part], done)
        backs.append(lax.ppermute(back, "path", swap))
    path_params = call(
        lambda *refs: first_rows_kernel(size, first, *refs),
        shape(*split_slab.shape),
        [smem] + [anywhere] * (1 + rounds),
        anywhere,
        scratch_shapes=[pltpu.SemaphoreType.DMA((2, LEVELS, rounds))],
    )(here, backs[0], *returned)
    path_params = call(
        lambda *refs: last_rows_kernel(size, last, *refs),
        shape(*split_slab.shape),
        [smem, anywhere, anywhere],
        anywhere,
        scratch_shapes=[pltpu.SemaphoreType.DMA((LEVELS, len(last)))],
        input_output_aliases={2: 0},
    )(here, backs[1], path_params)
    return (path_params.reshape(path_delta.shape), new_state[:, None], new_moment[:, None])


def local_wide(path_delta, assign, params, momentum):
    own_slab = path_delta[0]
    path_count = assign.shape[0]
    module_count, _, own_rows, width = params.shape
    entries = float(own_slab.size * lax.axis_size("shard"))
    total_sq = lax.psum(jnp.sum(own_slab * own_slab), "shard")
    scaled = own_slab * (1.0 / jnp.sqrt(total_sq / entries + 1e-06))
    received = lax.all_to_all(
        scaled.reshape(LEVELS, path_count, own_rows, width), "path", split_axis=1, concat_axis=1, tiled=True
    )
    flat_ids = (assign + LEVEL_MODULES * jnp.arange(LEVELS, dtype=jnp.int32)[None, :]).T.reshape(-1)
    member = (jnp.arange(module_count, dtype=jnp.int32)[:, None] == flat_ids[None, :]).astype(jnp.float32)
    mean = member / jnp.maximum(jnp.sum(member, axis=1), 1.0)[:, None]
    grad = jnp.einsum(
        "mp,prd->mrd", mean, received.reshape(-1, own_rows, width), precision=lax.Precision.HIGHEST
    )
    new_moment = beta_coef * momentum[:, 0] + grad
    new_state = params[:, 0] - outer_rate * (grad + beta_coef * new_moment)
    outgoing = jnp.take(new_state, flat_ids, axis=0).reshape(LEVELS, path_count, own_rows, width)
    returned = lax.all_to_all(outgoing, "path", split_axis=1, concat_axis=1, tiled=True)
    return (returned.reshape(path_delta.shape), new_state[:, None], new_moment[:, None])


def solution(mesh):
    in_specs = (
        P("path", None, "shard", None),
        P(),
        P(None, "shard", "path", None),
        P(None, "shard", "path", None),
    )
    out_specs = (
        P("path", None, "shard", None),
        P(None, "shard", "path", None),
        P(None, "shard", "path", None),
    )
    chosen = local if 4 <= mesh.shape["path"] <= MOST_UNROLLED else local_wide
    return jax.shard_map(chosen, mesh=mesh, in_specs=in_specs, out_specs=out_specs, check_vma=False)
```

```python
import jax
import jax.numpy as jnp
from jax import lax
from jax.experimental import pallas as pl
from jax.experimental.pallas import tpu as pltpu
from jax.sharding import PartitionSpec as P

LEVEL_MODULES = 16
LEVELS = 2
MOST_UNROLLED = 8
EIGHTHS = 3

outer_rate = 0.7
beta_coef = 0.9
moment_coef = outer_rate * beta_coef * beta_coef
grad_coef = outer_rate * (1.0 + beta_coef)

VMEM_LIMIT = 16 * 1024 * 1024

vmem = pl.BlockSpec(memory_space=pltpu.VMEM)
smem = pl.BlockSpec(memory_space=pltpu.SMEM)
anywhere = pl.BlockSpec(memory_space=pl.ANY)


def call(kernel, out_shape, in_specs, out_specs, **more):
    return pl.pallas_call(
        kernel,
        out_shape=out_shape,
        in_specs=in_specs,
        out_specs=out_specs,
        compiler_params=pltpu.CompilerParams(vmem_limit_bytes=VMEM_LIMIT),
        **more,
    )


def mirrored(k, size):
    if size < 8:
        return k
    return (k & ~6) | ((k & 2) << 1) | ((k & 4) >> 1)


def target(here, k, size):
    if isinstance(here, int):
        return here ^ (mirrored(k, size) if here & 1 else k)
    return here ^ jnp.where(here & 1 == 1, mirrored(k, size), k)


def origin(here, k, size):
    if isinstance(here, int):
        return here ^ (mirrored(k, size) if (here ^ k) & 1 else k)
    return here ^ jnp.where((here ^ k) & 1 == 1, mirrored(k, size), k)


def order_of(size):
    return sorted(range(2, size, 2), key=lambda k: (-bin(k).count("1"), k)) + [0]


def move(array, k, size):
    if k == 0:
        return array
    return lax.ppermute(array, "path", [(i, target(i, k, size)) for i in range(size)])


def tiles_of(rows, width):
    return [(slice(row, row + 8), slice(lane, lane + 128)) for row in range(0, rows, 8) for lane in range(0, width, 128)]


def pack_kernel(here_ref, delta_ref, square_ref, keep_ref, give_ref):
    levels, chips, halves, rows, width = delta_ref.shape

    def pack(core):
        totals = [jnp.zeros((8, 128), jnp.float32) for _ in range(4)]
        for level in range(levels):
            for chip in range(chips):
                for t, spot in enumerate(tiles_of(rows, width)):
                    kept = delta_ref[(level, chip, core, *spot)]
                    given = delta_ref[(level, chip, 1 - core, *spot)]
                    keep_ref[(level, chip, *spot)] = kept
                    give_ref[(level, chip, *spot)] = given
                    totals[t % 4] = totals[t % 4] + (kept * kept + given * given)
        total = jnp.sum((totals[0] + totals[1]) + (totals[2] + totals[3]), axis=0, keepdims=True)
        for first in range(0, square_ref.shape[0], 8):
            row = lax.broadcasted_iota(jnp.int32, (8, 128), 0) + first
            square_ref[first : first + 8] = jnp.where(row == here_ref[0], total, 0.0)

    for core in range(halves):
        pl.when(here_ref[0] & 1 == core)(lambda core=core: pack(core))


def in_first(count):
    return count * EIGHTHS // 8


def first_merge_kernel(size, here_ref, keep_ref, gift_ref, *outs):
    here = here_ref[0]
    core = here & 1
    spots = tiles_of(*keep_ref.shape[2:])
    sent = [(0, spot) for spot in spots] + [(1, spot) for spot in spots[: in_first(len(spots))]]
    for k, out in zip(order_of(size), outs):
        chip = target(here, k, size) // 2
        for source, ref in ((core, keep_ref), (1 - core, gift_ref)):
            for t, (level, spot) in enumerate(sent):
                out[source * len(sent) + t] = ref[(level, chip, *spot)]


def second_merge_kernel(size, here_ref, square_ref, other_ref, keep_ref, gift_ref, *outs):
    here = here_ref[0]
    core = here & 1
    squares = square_ref[...] + other_ref[...]
    spots = tiles_of(*keep_ref.shape[2:])
    spots = spots[in_first(len(spots)) :]
    for k, out in zip(order_of(size), outs):
        chip = target(here, k, size) // 2
        out[0] = squares
        for source, ref in ((core, keep_ref), (1 - core, gift_ref)):
            for t, spot in enumerate(spots):
                out[1 + source * len(spots) + t] = ref[(1, chip, *spot)]


def sum_kernel(count, *refs):
    total = refs[0][...]
    for ref in refs[1:count]:
        total = total + ref[...]
    refs[-1][...] = total


def decay_kernel(params_ref, decay_ref, out_ref):
    def decay(module, carry):
        out_ref[module] = params_ref[module] - decay_ref[module]
        return carry

    lax.fori_loop(0, out_ref.shape[0], decay, 0)


def plan_kernel(here_ref, ids_ref, plan_ref, module_ref):
    size = ids_ref.shape[1]
    order = order_of(size)
    here = here_ref[0]
    paths = [(origin(here, k, size) // 2) * 2 + half for k in order for half in range(2)]
    targets = [(target(here, k, size) // 2) * 2 + half for k in order for half in range(2)]
    for level in range(LEVELS):
        first = level * LEVEL_MODULES
        for module in range(LEVEL_MODULES):
            module_ref[first + module] = -1
        sources = [ids_ref[level, path] + first for path in paths]
        for i in reversed(range(size)):
            module_ref[sources[i]] = i
        for i in range(size):
            plan_ref[level, i] = module_ref[sources[i]]
            sharers = jnp.int32(0)
            for other in range(size):
                sharers = sharers + jnp.where(sources[other] == sources[i], 1, 0)
            plan_ref[level, size + i] = sharers
            plan_ref[level, 2 * size + i] = paths[i]
            module = ids_ref[level, targets[i]] + first
            plan_ref[level, 3 * size + i] = module
            plan_ref[level, 4 * size + i] = module_ref[module]


def outgoing_kernel(rounds, entries, plan_ref, decayed_ref, *refs):
    firsts, seconds = refs[:rounds], refs[rounds : 2 * rounds]
    outs, (grad_ref, rescale_ref) = refs[2 * rounds : -2], refs[-2:]
    size = 2 * rounds
    rows, width = grad_ref.shape[2:]
    spots = tiles_of(rows, width)
    count, early = len(spots), in_first(len(spots))
    squares = seconds[0][0]
    for second in seconds[1:]:
        squares = squares + second[0]
    total = jnp.sum(squares, axis=1, keepdims=True)
    rescale_ref[...] = jnp.broadcast_to(1.0 / jnp.sqrt(total / entries + 1e-06), rescale_ref.shape)
    for level in range(LEVELS):
        for i in range(size):
            rescale = jnp.broadcast_to(rescale_ref[pl.ds(plan_ref[level, 2 * size + i], 1), :], (8, 128))
            factor = rescale / jnp.full((8, 128), plan_ref[level, size + i], jnp.int32).astype(jnp.float32)
            for t, spot in enumerate(spots):
                if level == 0 or t < early:
                    block = firsts[i // 2][(i % 2) * (count + early) + level * count + t]
                else:
                    block = seconds[i // 2][1 + (i % 2) * (count - early) + t - early]
                grad_ref[(level, i, *spot)] = block * factor
        for i in range(1, size):
            leader = plan_ref[level, i]

            @pl.when(leader != i)
            def _():
                grad_ref[level, leader] += grad_ref[level, i]

        for i in range(size):
            decayed = decayed_ref[plan_ref[level, 3 * size + i]]
            outs[i // 2][i % 2, level] = decayed - grad_coef * grad_ref[level, plan_ref[level, 4 * size + i]]


def state_kernel(module_ref, grad_ref, decayed_ref, momentum_ref, new_params_ref, new_momentum_ref, token_ref):
    token_ref[...] = jnp.zeros_like(token_ref)
    count = new_params_ref.shape[0]
    first = pl.program_id(0) * count
    level = first // LEVEL_MODULES
    for place in range(count):
        module = first + place
        leader = module_ref[module]
        taken = jnp.where(leader < 0, 0.0, 1.0)
        grad = taken * grad_ref[level, jnp.maximum(leader, 0)]
        new_momentum_ref[place] = beta_coef * momentum_ref[module] + grad
        new_params_ref[place] = decayed_ref[module] - grad_coef * grad


def give_back_kernel(here_ref, block_ref, done_ref, out_ref):
    del done_ref
    out_ref[...] = block_ref[1 - (here_ref[0] & 1)]


def first_rows_kernel(size, first, here_ref, *refs):
    backs, refs = refs[: len(first)], refs[len(first) :]
    here = here_ref[0]
    core = here & 1
    out_ref, sems = refs[-2:]
    copies = []
    for j, k in enumerate(order_of(size)):
        chip = origin(here, k, size) // 2
        for level in range(LEVELS):
            copies.append(
                pltpu.make_async_copy(refs[j].at[core, level], out_ref.at[level, chip, core], sems.at[0, level, j])
            )
    for i, k in enumerate(first):
        chip = origin(here ^ 1, k, size) // 2
        for level in range(LEVELS):
            copies.append(
                pltpu.make_async_copy(
                    backs[i].at[level], out_ref.at[level, chip, 1 - core], sems.at[1, level, i]
                )
            )
    for copy in copies:
        copy.start()
    for copy in copies:
        copy.wait()


def last_rows_kernel(size, last, here_ref, back_ref, held_ref, out_ref, sems):
    del held_ref
    here = here_ref[0]
    chip = origin(here ^ 1, last, size) // 2
    copies = [
        pltpu.make_async_copy(back_ref.at[level], out_ref.at[level, chip, 1 - (here & 1)], sems.at[level])
        for level in range(LEVELS)
    ]
    for copy in copies:
        copy.start()
    for copy in copies:
        copy.wait()


def local(path_delta, assign, params, momentum):
    own_slab = path_delta[0]
    size = assign.shape[0]
    module_count, _, own_rows, width = params.shape
    shards = lax.axis_size("shard")
    entries = float(own_slab.size * shards)
    state_in = params.reshape(module_count, own_rows, width)
    moment_in = momentum.reshape(module_count, own_rows, width)
    split_slab = own_slab.reshape(LEVELS, size // 2, 2, own_rows, width)
    here = lax.axis_index("path").astype(jnp.int32).reshape(1)
    order = order_of(size)
    rounds = len(order)
    swap = [(i, i ^ 1) for i in range(size)]
    shape = lambda *dims: jax.ShapeDtypeStruct(dims, jnp.float32)
    squares_shape = shape(-(-size // 8) * 8, 128)
    by_chip = shape(LEVELS, rounds, own_rows, width)
    message = shape(2, LEVELS, own_rows, width)
    count = own_rows * width // 1024

    squares, keep, give = call(pack_kernel, [squares_shape, by_chip, by_chip], [smem, vmem], [vmem] * 3)(
        here, split_slab
    )
    gift = lax.ppermute(give, "path", swap)
    tiles = [squares] + [
        lax.ppermute(squares, "shard", [(i, i ^ step) for i in range(shards)]) for step in range(shards - 1, 0, -1)
    ]
    firsts = call(
        lambda *refs: first_merge_kernel(size, *refs),
        [shape(2 * (count + in_first(count)), 8, 128)] * rounds,
        [smem, vmem, vmem],
        [vmem] * rounds,
    )(here, keep, gift)
    firsts = [move(firsts[j], k, size) for j, k in enumerate(order)]
    decay = moment_coef * moment_in
    decayed = call(decay_kernel, shape(*state_in.shape), [vmem, vmem], vmem)(state_in, decay)
    plan, leaders = call(
        plan_kernel,
        [
            jax.ShapeDtypeStruct((LEVELS, 5 * size), jnp.int32),
            jax.ShapeDtypeStruct((module_count,), jnp.int32),
        ],
        [smem, smem],
        [smem, smem],
    )(here, assign.T)
    squares = call(
        lambda *refs: sum_kernel(shards, *refs), squares_shape, [vmem] * shards + [anywhere], vmem
    )(*tiles, decay)
    other = lax.ppermute(squares, "path", swap)
    seconds = call(
        lambda *refs: second_merge_kernel(size, *refs),
        [shape(1 + 2 * (count - in_first(count)), 8, 128)] * rounds,
        [smem] + [vmem] * 4,
        [vmem] * rounds,
    )(here, squares, other, keep, gift)
    seconds = [move(seconds[j], k, size) for j, k in enumerate(order)]

    *outgoing, grad = call(
        lambda *refs: outgoing_kernel(rounds, entries, *refs),
        [message] * rounds + [shape(LEVELS, size, own_rows, width)],
        [smem] + [vmem] * (1 + 2 * rounds),
        [vmem] * (rounds + 1),
        scratch_shapes=[pltpu.VMEM(squares_shape.shape, jnp.float32)],
    )(plan, decayed, *firsts, *seconds)
    returned = [move(outgoing[j], k, size) for j, k in enumerate(order)]
    block = LEVEL_MODULES // 2
    state_block = pl.BlockSpec((block, own_rows, width), lambda i: (i, 0, 0))
    new_state, new_moment, done = call(
        state_kernel,
        [shape(*state_in.shape)] * 2 + [shape(8, 128)],
        [smem, vmem, vmem, vmem],
        [state_block, state_block, vmem],
        grid=(module_count // block,),
    )(leaders, grad, decayed, moment_in)
    blocks = dict(zip(order, returned))
    backs = {}
    for k in (0, *order[:-1]):
        back = call(
            give_back_kernel, shape(LEVELS, own_rows, width), [smem, vmem, anywhere], vmem
        )(here, blocks[k], done)
        backs[k] = lax.ppermute(back, "path", swap)
    first, last = (0, *order[:-2]), order[-2]
    path_params = call(
        lambda *refs: first_rows_kernel(size, first, *refs),
        shape(*split_slab.shape),
        [smem] + [anywhere] * (len(first) + rounds),
        anywhere,
        scratch_shapes=[pltpu.SemaphoreType.DMA((2, LEVELS, rounds))],
    )(here, *[backs[k] for k in first], *returned)
    path_params = call(
        lambda *refs: last_rows_kernel(size, last, *refs),
        shape(*split_slab.shape),
        [smem, anywhere, anywhere],
        anywhere,
        scratch_shapes=[pltpu.SemaphoreType.DMA((LEVELS,))],
        input_output_aliases={2: 0},
    )(here, backs[last], path_params)
    return (path_params.reshape(path_delta.shape), new_state[:, None], new_moment[:, None])


def local_wide(path_delta, assign, params, momentum):
    own_slab = path_delta[0]
    path_count = assign.shape[0]
    module_count, _, own_rows, width = params.shape
    entries = float(own_slab.size * lax.axis_size("shard"))
    total_sq = lax.psum(jnp.sum(own_slab * own_slab), "shard")
    scaled = own_slab * (1.0 / jnp.sqrt(total_sq / entries + 1e-06))
    received = lax.all_to_all(
        scaled.reshape(LEVELS, path_count, own_rows, width), "path", split_axis=1, concat_axis=1, tiled=True
    )
    flat_ids = (assign + LEVEL_MODULES * jnp.arange(LEVELS, dtype=jnp.int32)[None, :]).T.reshape(-1)
    member = (jnp.arange(module_count, dtype=jnp.int32)[:, None] == flat_ids[None, :]).astype(jnp.float32)
    mean = member / jnp.maximum(jnp.sum(member, axis=1), 1.0)[:, None]
    grad = jnp.einsum(
        "mp,prd->mrd", mean, received.reshape(-1, own_rows, width), precision=lax.Precision.HIGHEST
    )
    new_moment = beta_coef * momentum[:, 0] + grad
    new_state = params[:, 0] - outer_rate * (grad + beta_coef * new_moment)
    outgoing = jnp.take(new_state, flat_ids, axis=0).reshape(LEVELS, path_count, own_rows, width)
    returned = lax.all_to_all(outgoing, "path", split_axis=1, concat_axis=1, tiled=True)
    return (returned.reshape(path_delta.shape), new_state[:, None], new_moment[:, None])


def solution(mesh):
    in_specs = (
        P("path", None, "shard", None),
        P(),
        P(None, "shard", "path", None),
        P(None, "shard", "path", None),
    )
    out_specs = (
        P("path", None, "shard", None),
        P(None, "shard", "path", None),
        P(None, "shard", "path", None),
    )
    chosen = local if 4 <= mesh.shape["path"] <= MOST_UNROLLED else local_wide
    return jax.shard_map(chosen, mesh=mesh, in_specs=in_specs, out_specs=out_specs, check_vma=False)
```

```python
import jax
import jax.numpy as jnp
from jax import lax
from jax.experimental import pallas as pl
from jax.experimental.pallas import tpu as pltpu
from jax.sharding import PartitionSpec as P

LEVEL_MODULES = 16
LEVELS = 2
MOST_UNROLLED = 8
EIGHTHS = 3

outer_rate = 0.7
beta_coef = 0.9
moment_coef = outer_rate * beta_coef * beta_coef
grad_coef = outer_rate * (1.0 + beta_coef)

VMEM_LIMIT = 16 * 1024 * 1024

vmem = pl.BlockSpec(memory_space=pltpu.VMEM)
smem = pl.BlockSpec(memory_space=pltpu.SMEM)
anywhere = pl.BlockSpec(memory_space=pl.ANY)


def call(kernel, out_shape, in_specs, out_specs, **more):
    return pl.pallas_call(
        kernel,
        out_shape=out_shape,
        in_specs=in_specs,
        out_specs=out_specs,
        compiler_params=pltpu.CompilerParams(vmem_limit_bytes=VMEM_LIMIT),
        **more,
    )


def mirrored(k, size):
    if size < 8:
        return k
    return (k & ~6) | ((k & 2) << 1) | ((k & 4) >> 1)


def target(here, k, size):
    if isinstance(here, int):
        return here ^ (mirrored(k, size) if here & 1 else k)
    return here ^ jnp.where(here & 1 == 1, mirrored(k, size), k)


def origin(here, k, size):
    if isinstance(here, int):
        return here ^ (mirrored(k, size) if (here ^ k) & 1 else k)
    return here ^ jnp.where((here ^ k) & 1 == 1, mirrored(k, size), k)


def order_of(size):
    return sorted(range(2, size, 2), key=lambda k: (-bin(k).count("1"), k)) + [0]


def move(array, k, size):
    if k == 0:
        return array
    return lax.ppermute(array, "path", [(i, target(i, k, size)) for i in range(size)])


def tiles_of(rows, width):
    return [(slice(row, row + 8), slice(lane, lane + 128)) for row in range(0, rows, 8) for lane in range(0, width, 128)]


def pack_kernel(here_ref, delta_ref, square_ref, keep_ref, give_ref):
    levels, chips, halves, rows, width = delta_ref.shape

    def pack(core):
        totals = [jnp.zeros((8, 128), jnp.float32) for _ in range(4)]
        for level in range(levels):
            for chip in range(chips):
                for t, spot in enumerate(tiles_of(rows, width)):
                    kept = delta_ref[(level, chip, core, *spot)]
                    given = delta_ref[(level, chip, 1 - core, *spot)]
                    keep_ref[(level, chip, *spot)] = kept
                    give_ref[(level, chip, *spot)] = given
                    totals[t % 4] = totals[t % 4] + (kept * kept + given * given)
        total = jnp.sum((totals[0] + totals[1]) + (totals[2] + totals[3]), axis=0, keepdims=True)
        for first in range(0, square_ref.shape[0], 8):
            row = lax.broadcasted_iota(jnp.int32, (8, 128), 0) + first
            square_ref[first : first + 8] = jnp.where(row == here_ref[0], total, 0.0)

    for core in range(halves):
        pl.when(here_ref[0] & 1 == core)(lambda core=core: pack(core))


def in_first(count):
    return count * EIGHTHS // 8


def first_merge_kernel(size, here_ref, keep_ref, gift_ref, *outs):
    here = here_ref[0]
    core = here & 1
    spots = tiles_of(*keep_ref.shape[2:])
    sent = [(0, spot) for spot in spots] + [(1, spot) for spot in spots[: in_first(len(spots))]]
    for k, out in zip(order_of(size), outs):
        chip = target(here, k, size) // 2
        for source, ref in ((core, keep_ref), (1 - core, gift_ref)):
            for t, (level, spot) in enumerate(sent):
                out[source * len(sent) + t] = ref[(level, chip, *spot)]


def second_merge_kernel(size, here_ref, square_ref, other_ref, keep_ref, gift_ref, *outs):
    here = here_ref[0]
    core = here & 1
    squares = square_ref[...] + other_ref[...]
    spots = tiles_of(*keep_ref.shape[2:])
    spots = spots[in_first(len(spots)) :]
    for k, out in zip(order_of(size), outs):
        chip = target(here, k, size) // 2
        out[0] = squares
        for source, ref in ((core, keep_ref), (1 - core, gift_ref)):
            for t, spot in enumerate(spots):
                out[1 + source * len(spots) + t] = ref[(1, chip, *spot)]


def sum_kernel(count, *refs):
    total = refs[0][...]
    for ref in refs[1:count]:
        total = total + ref[...]
    refs[-1][...] = total


def decay_kernel(params_ref, decay_ref, out_ref):
    def decay(module, carry):
        out_ref[module] = params_ref[module] - decay_ref[module]
        return carry

    lax.fori_loop(0, out_ref.shape[0], decay, 0)


def plan_kernel(here_ref, ids_ref, plan_ref, module_ref):
    size = ids_ref.shape[1]
    order = order_of(size)
    here = here_ref[0]
    paths = [(origin(here, k, size) // 2) * 2 + half for k in order for half in range(2)]
    targets = [(target(here, k, size) // 2) * 2 + half for k in order for half in range(2)]
    for level in range(LEVELS):
        first = level * LEVEL_MODULES
        for module in range(LEVEL_MODULES):
            module_ref[first + module] = -1
        sources = [ids_ref[level, path] + first for path in paths]
        for i in reversed(range(size)):
            module_ref[sources[i]] = i
        for i in range(size):
            plan_ref[level, i] = module_ref[sources[i]]
            sharers = jnp.int32(0)
            for other in range(size):
                sharers = sharers + jnp.where(sources[other] == sources[i], 1, 0)
            plan_ref[level, size + i] = sharers
            plan_ref[level, 2 * size + i] = paths[i]
            module = ids_ref[level, targets[i]] + first
            plan_ref[level, 3 * size + i] = module
            plan_ref[level, 4 * size + i] = module_ref[module]


def outgoing_kernel(rounds, entries, plan_ref, decayed_ref, *refs):
    firsts, seconds = refs[:rounds], refs[rounds : 2 * rounds]
    outs, (grad_ref, rescale_ref) = refs[2 * rounds : -2], refs[-2:]
    size = 2 * rounds
    rows, width = grad_ref.shape[2:]
    spots = tiles_of(rows, width)
    count, early = len(spots), in_first(len(spots))
    squares = seconds[0][0]
    for second in seconds[1:]:
        squares = squares + second[0]
    total = jnp.sum(squares, axis=1, keepdims=True)
    rescale_ref[...] = jnp.broadcast_to(1.0 / jnp.sqrt(total / entries + 1e-06), rescale_ref.shape)
    for level in range(LEVELS):
        for i in range(size):
            rescale = jnp.broadcast_to(rescale_ref[pl.ds(plan_ref[level, 2 * size + i], 1), :], (8, 128))
            factor = rescale / jnp.full((8, 128), plan_ref[level, size + i], jnp.int32).astype(jnp.float32)
            for t, spot in enumerate(spots):
                if level == 0 or t < early:
                    block = firsts[i // 2][(i % 2) * (count + early) + level * count + t]
                else:
                    block = seconds[i // 2][1 + (i % 2) * (count - early) + t - early]
                grad_ref[(level, i, *spot)] = block * factor
        for i in range(1, size):
            leader = plan_ref[level, i]

            @pl.when(leader != i)
            def _():
                grad_ref[level, leader] += grad_ref[level, i]

        for i in range(size):
            decayed = decayed_ref[plan_ref[level, 3 * size + i]]
            outs[i // 2][i % 2, level] = decayed - grad_coef * grad_ref[level, plan_ref[level, 4 * size + i]]


def state_kernel(module_ref, grad_ref, decayed_ref, momentum_ref, new_params_ref, new_momentum_ref, token_ref):
    token_ref[...] = jnp.zeros_like(token_ref)
    count = new_params_ref.shape[0]
    first = pl.program_id(0) * count
    level = first // LEVEL_MODULES
    for place in range(count):
        module = first + place
        leader = module_ref[module]
        taken = jnp.where(leader < 0, 0.0, 1.0)
        grad = taken * grad_ref[level, jnp.maximum(leader, 0)]
        new_momentum_ref[place] = beta_coef * momentum_ref[module] + grad
        new_params_ref[place] = decayed_ref[module] - grad_coef * grad


def give_back_kernel(here_ref, block_ref, done_ref, out_ref):
    del done_ref
    out_ref[...] = block_ref[1 - (here_ref[0] & 1)]


def first_rows_kernel(size, first, here_ref, *refs):
    backs, refs = refs[: len(first)], refs[len(first) :]
    here = here_ref[0]
    core = here & 1
    out_ref, sems = refs[-2:]
    copies = []
    for j, k in enumerate(order_of(size)):
        chip = origin(here, k, size) // 2
        for level in range(LEVELS):
            copies.append(
                pltpu.make_async_copy(refs[j].at[core, level], out_ref.at[level, chip, core], sems.at[0, level, j])
            )
    for i, k in enumerate(first):
        chip = origin(here ^ 1, k, size) // 2
        for level in range(LEVELS):
            copies.append(
                pltpu.make_async_copy(
                    backs[i].at[level], out_ref.at[level, chip, 1 - core], sems.at[1, level, i]
                )
            )
    for copy in copies:
        copy.start()
    for copy in copies:
        copy.wait()


def last_rows_kernel(size, last, here_ref, *refs):
    here = here_ref[0]
    out_ref, sems = refs[-2:]
    copies = []
    for i, k in enumerate(last):
        chip = origin(here ^ 1, k, size) // 2
        for level in range(LEVELS):
            copies.append(
                pltpu.make_async_copy(
                    refs[i].at[level], out_ref.at[level, chip, 1 - (here & 1)], sems.at[level, i]
                )
            )
    for copy in copies:
        copy.start()
    for copy in copies:
        copy.wait()


def local(path_delta, assign, params, momentum):
    own_slab = path_delta[0]
    size = assign.shape[0]
    module_count, _, own_rows, width = params.shape
    shards = lax.axis_size("shard")
    entries = float(own_slab.size * shards)
    state_in = params.reshape(module_count, own_rows, width)
    moment_in = momentum.reshape(module_count, own_rows, width)
    split_slab = own_slab.reshape(LEVELS, size // 2, 2, own_rows, width)
    here = lax.axis_index("path").astype(jnp.int32).reshape(1)
    order = order_of(size)
    rounds = len(order)
    swap = [(i, i ^ 1) for i in range(size)]
    shape = lambda *dims: jax.ShapeDtypeStruct(dims, jnp.float32)
    squares_shape = shape(-(-size // 8) * 8, 128)
    by_chip = shape(LEVELS, rounds, own_rows, width)
    message = shape(2, LEVELS, own_rows, width)
    count = own_rows * width // 1024

    squares, keep, give = call(pack_kernel, [squares_shape, by_chip, by_chip], [smem, vmem], [vmem] * 3)(
        here, split_slab
    )
    gift = lax.ppermute(give, "path", swap)
    tiles = [squares] + [
        lax.ppermute(squares, "shard", [(i, i ^ step) for i in range(shards)]) for step in range(shards - 1, 0, -1)
    ]
    firsts = call(
        lambda *refs: first_merge_kernel(size, *refs),
        [shape(2 * (count + in_first(count)), 8, 128)] * rounds,
        [smem, vmem, vmem],
        [vmem] * rounds,
    )(here, keep, gift)
    firsts = [move(firsts[j], k, size) for j, k in enumerate(order)]
    decay = moment_coef * moment_in
    decayed = call(decay_kernel, shape(*state_in.shape), [vmem, vmem], vmem)(state_in, decay)
    plan, leaders = call(
        plan_kernel,
        [
            jax.ShapeDtypeStruct((LEVELS, 5 * size), jnp.int32),
            jax.ShapeDtypeStruct((module_count,), jnp.int32),
        ],
        [smem, smem],
        [smem, smem],
    )(here, assign.T)
    squares = call(
        lambda *refs: sum_kernel(shards, *refs), squares_shape, [vmem] * shards + [anywhere], vmem
    )(*tiles, decay)
    other = lax.ppermute(squares, "path", swap)
    seconds = call(
        lambda *refs: second_merge_kernel(size, *refs),
        [shape(1 + 2 * (count - in_first(count)), 8, 128)] * rounds,
        [smem] + [vmem] * 4,
        [vmem] * rounds,
    )(here, squares, other, keep, gift)
    seconds = [move(seconds[j], k, size) for j, k in enumerate(order)]

    *outgoing, grad = call(
        lambda *refs: outgoing_kernel(rounds, entries, *refs),
        [message] * rounds + [shape(LEVELS, size, own_rows, width)],
        [smem] + [vmem] * (1 + 2 * rounds),
        [vmem] * (rounds + 1),
        scratch_shapes=[pltpu.VMEM(squares_shape.shape, jnp.float32)],
    )(plan, decayed, *firsts, *seconds)
    returned = [move(outgoing[j], k, size) for j, k in enumerate(order)]
    block = LEVEL_MODULES // 2
    state_block = pl.BlockSpec((block, own_rows, width), lambda i: (i, 0, 0))
    new_state, new_moment, done = call(
        state_kernel,
        [shape(*state_in.shape)] * 2 + [shape(8, 128)],
        [smem, vmem, vmem, vmem],
        [state_block, state_block, vmem],
        grid=(module_count // block,),
    )(leaders, grad, decayed, moment_in)
    blocks = dict(zip(order, returned))
    backs = {}
    for k in (0, *order[:-1]):
        back = call(
            give_back_kernel, shape(LEVELS, own_rows, width), [smem, vmem, anywhere], vmem
        )(here, blocks[k], done)
        backs[k] = lax.ppermute(back, "path", swap)
    first, last = (0, *order[:-3]), order[-3:-1]
    path_params = call(
        lambda *refs: first_rows_kernel(size, first, *refs),
        shape(*split_slab.shape),
        [smem] + [anywhere] * (len(first) + rounds),
        anywhere,
        scratch_shapes=[pltpu.SemaphoreType.DMA((2, LEVELS, rounds))],
    )(here, *[backs[k] for k in first], *returned)
    path_params = call(
        lambda *refs: last_rows_kernel(size, last, *refs),
        shape(*split_slab.shape),
        [smem] + [anywhere] * (len(last) + 1),
        anywhere,
        scratch_shapes=[pltpu.SemaphoreType.DMA((LEVELS, len(last)))],
        input_output_aliases={1 + len(last): 0},
    )(here, *[backs[k] for k in last], path_params)
    return (path_params.reshape(path_delta.shape), new_state[:, None], new_moment[:, None])


def local_wide(path_delta, assign, params, momentum):
    own_slab = path_delta[0]
    path_count = assign.shape[0]
    module_count, _, own_rows, width = params.shape
    entries = float(own_slab.size * lax.axis_size("shard"))
    total_sq = lax.psum(jnp.sum(own_slab * own_slab), "shard")
    scaled = own_slab * (1.0 / jnp.sqrt(total_sq / entries + 1e-06))
    received = lax.all_to_all(
        scaled.reshape(LEVELS, path_count, own_rows, width), "path", split_axis=1, concat_axis=1, tiled=True
    )
    flat_ids = (assign + LEVEL_MODULES * jnp.arange(LEVELS, dtype=jnp.int32)[None, :]).T.reshape(-1)
    member = (jnp.arange(module_count, dtype=jnp.int32)[:, None] == flat_ids[None, :]).astype(jnp.float32)
    mean = member / jnp.maximum(jnp.sum(member, axis=1), 1.0)[:, None]
    grad = jnp.einsum(
        "mp,prd->mrd", mean, received.reshape(-1, own_rows, width), precision=lax.Precision.HIGHEST
    )
    new_moment = beta_coef * momentum[:, 0] + grad
    new_state = params[:, 0] - outer_rate * (grad + beta_coef * new_moment)
    outgoing = jnp.take(new_state, flat_ids, axis=0).reshape(LEVELS, path_count, own_rows, width)
    returned = lax.all_to_all(outgoing, "path", split_axis=1, concat_axis=1, tiled=True)
    return (returned.reshape(path_delta.shape), new_state[:, None], new_moment[:, None])


def solution(mesh):
    in_specs = (
        P("path", None, "shard", None),
        P(),
        P(None, "shard", "path", None),
        P(None, "shard", "path", None),
    )
    out_specs = (
        P("path", None, "shard", None),
        P(None, "shard", "path", None),
        P(None, "shard", "path", None),
    )
    chosen = local if 4 <= mesh.shape["path"] <= MOST_UNROLLED else local_wide
    return jax.shard_map(chosen, mesh=mesh, in_specs=in_specs, out_specs=out_specs, check_vma=False)
```

```python
import jax
import jax.numpy as jnp
from jax import lax
from jax.experimental import pallas as pl
from jax.experimental.pallas import tpu as pltpu
from jax.sharding import PartitionSpec as P

LEVEL_MODULES = 16
LEVELS = 2
MOST_UNROLLED = 8
EIGHTHS = 3

outer_rate = 0.7
beta_coef = 0.9
moment_coef = outer_rate * beta_coef * beta_coef
grad_coef = outer_rate * (1.0 + beta_coef)

VMEM_LIMIT = 16 * 1024 * 1024

vmem = pl.BlockSpec(memory_space=pltpu.VMEM)
smem = pl.BlockSpec(memory_space=pltpu.SMEM)
anywhere = pl.BlockSpec(memory_space=pl.ANY)


def call(kernel, out_shape, in_specs, out_specs, **more):
    return pl.pallas_call(
        kernel,
        out_shape=out_shape,
        in_specs=in_specs,
        out_specs=out_specs,
        compiler_params=pltpu.CompilerParams(vmem_limit_bytes=VMEM_LIMIT),
        **more,
    )


def mirrored(k, size):
    if size < 8:
        return k
    return (k & ~6) | ((k & 2) << 1) | ((k & 4) >> 1)


def target(here, k, size):
    if isinstance(here, int):
        return here ^ (mirrored(k, size) if here & 1 else k)
    return here ^ jnp.where(here & 1 == 1, mirrored(k, size), k)


def origin(here, k, size):
    if isinstance(here, int):
        return here ^ (mirrored(k, size) if (here ^ k) & 1 else k)
    return here ^ jnp.where((here ^ k) & 1 == 1, mirrored(k, size), k)


def order_of(size):
    return sorted(range(2, size, 2), key=lambda k: (-bin(k).count("1"), k)) + [0]


def move(array, k, size):
    if k == 0:
        return array
    return lax.ppermute(array, "path", [(i, target(i, k, size)) for i in range(size)])


def tiles_of(rows, width):
    return [(slice(row, row + 8), slice(lane, lane + 128)) for row in range(0, rows, 8) for lane in range(0, width, 128)]


def pack_kernel(here_ref, delta_ref, square_ref, keep_ref, give_ref):
    levels, chips, halves, rows, width = delta_ref.shape

    def pack(core):
        totals = [jnp.zeros((8, 128), jnp.float32) for _ in range(4)]
        for level in range(levels):
            for chip in range(chips):
                for t, spot in enumerate(tiles_of(rows, width)):
                    kept = delta_ref[(level, chip, core, *spot)]
                    given = delta_ref[(level, chip, 1 - core, *spot)]
                    keep_ref[(level, chip, *spot)] = kept
                    give_ref[(level, chip, *spot)] = given
                    totals[t % 4] = totals[t % 4] + (kept * kept + given * given)
        total = jnp.sum((totals[0] + totals[1]) + (totals[2] + totals[3]), axis=0, keepdims=True)
        for first in range(0, square_ref.shape[0], 8):
            row = lax.broadcasted_iota(jnp.int32, (8, 128), 0) + first
            square_ref[first : first + 8] = jnp.where(row == here_ref[0], total, 0.0)

    for core in range(halves):
        pl.when(here_ref[0] & 1 == core)(lambda core=core: pack(core))


def in_first(count):
    return count * EIGHTHS // 8


def first_merge_kernel(size, here_ref, keep_ref, gift_ref, *outs):
    here = here_ref[0]
    core = here & 1
    spots = tiles_of(*keep_ref.shape[2:])
    sent = [(0, spot) for spot in spots] + [(1, spot) for spot in spots[: in_first(len(spots))]]
    for k, out in zip(order_of(size), outs):
        chip = target(here, k, size) // 2
        for source, ref in ((core, keep_ref), (1 - core, gift_ref)):
            for t, (level, spot) in enumerate(sent):
                out[source * len(sent) + t] = ref[(level, chip, *spot)]


def second_merge_kernel(size, here_ref, square_ref, other_ref, keep_ref, gift_ref, *outs):
    here = here_ref[0]
    core = here & 1
    squares = square_ref[...] + other_ref[...]
    spots = tiles_of(*keep_ref.shape[2:])
    spots = spots[in_first(len(spots)) :]
    for k, out in zip(order_of(size), outs):
        chip = target(here, k, size) // 2
        out[0] = squares
        for source, ref in ((core, keep_ref), (1 - core, gift_ref)):
            for t, spot in enumerate(spots):
                out[1 + source * len(spots) + t] = ref[(1, chip, *spot)]


def sum_kernel(count, *refs):
    total = refs[0][...]
    for ref in refs[1:count]:
        total = total + ref[...]
    refs[-1][...] = total


def decay_kernel(params_ref, decay_ref, out_ref):
    def decay(module, carry):
        out_ref[module] = params_ref[module] - decay_ref[module]
        return carry

    lax.fori_loop(0, out_ref.shape[0], decay, 0)


def plan_kernel(here_ref, ids_ref, plan_ref, module_ref):
    size = ids_ref.shape[1]
    order = order_of(size)
    here = here_ref[0]
    paths = [(origin(here, k, size) // 2) * 2 + half for k in order for half in range(2)]
    targets = [(target(here, k, size) // 2) * 2 + half for k in order for half in range(2)]
    for level in range(LEVELS):
        first = level * LEVEL_MODULES
        for module in range(LEVEL_MODULES):
            module_ref[first + module] = -1
        sources = [ids_ref[level, path] + first for path in paths]
        for i in reversed(range(size)):
            module_ref[sources[i]] = i
        for i in range(size):
            plan_ref[level, i] = module_ref[sources[i]]
            sharers = jnp.int32(0)
            for other in range(size):
                sharers = sharers + jnp.where(sources[other] == sources[i], 1, 0)
            plan_ref[level, size + i] = sharers
            plan_ref[level, 2 * size + i] = paths[i]
            module = ids_ref[level, targets[i]] + first
            plan_ref[level, 3 * size + i] = module
            plan_ref[level, 4 * size + i] = module_ref[module]


def outgoing_kernel(rounds, entries, plan_ref, decayed_ref, *refs):
    firsts, seconds = refs[:rounds], refs[rounds : 2 * rounds]
    outs, (grad_ref, rescale_ref) = refs[2 * rounds : -2], refs[-2:]
    size = 2 * rounds
    rows, width = grad_ref.shape[2:]
    spots = tiles_of(rows, width)
    count, early = len(spots), in_first(len(spots))
    squares = seconds[0][0]
    for second in seconds[1:]:
        squares = squares + second[0]
    total = jnp.sum(squares, axis=1, keepdims=True)
    rescale_ref[...] = jnp.broadcast_to(1.0 / jnp.sqrt(total / entries + 1e-06), rescale_ref.shape)
    for level in range(LEVELS):
        for i in range(size):
            rescale = jnp.broadcast_to(rescale_ref[pl.ds(plan_ref[level, 2 * size + i], 1), :], (8, 128))
            factor = rescale / jnp.full((8, 128), plan_ref[level, size + i], jnp.int32).astype(jnp.float32)
            for t, spot in enumerate(spots):
                if level == 0 or t < early:
                    block = firsts[i // 2][(i % 2) * (count + early) + level * count + t]
                else:
                    block = seconds[i // 2][1 + (i % 2) * (count - early) + t - early]
                grad_ref[(level, i, *spot)] = block * factor
        for i in range(1, size):
            leader = plan_ref[level, i]

            @pl.when(leader != i)
            def _():
                grad_ref[level, leader] += grad_ref[level, i]

        for i in range(size):
            decayed = decayed_ref[plan_ref[level, 3 * size + i]]
            outs[i // 2][i % 2, level] = decayed - grad_coef * grad_ref[level, plan_ref[level, 4 * size + i]]


def state_kernel(module_ref, grad_ref, decayed_ref, momentum_ref, new_params_ref, new_momentum_ref, token_ref):
    token_ref[...] = jnp.zeros_like(token_ref)
    count = new_params_ref.shape[0]
    first = pl.program_id(0) * count
    level = first // LEVEL_MODULES
    for place in range(count):
        module = first + place
        leader = module_ref[module]
        taken = jnp.where(leader < 0, 0.0, 1.0)
        grad = taken * grad_ref[level, jnp.maximum(leader, 0)]
        new_momentum_ref[place] = beta_coef * momentum_ref[module] + grad
        new_params_ref[place] = decayed_ref[module] - grad_coef * grad


def give_back_kernel(size, here_ref, *refs):
    here = here_ref[0]
    for j, k in enumerate(order_of(size)):
        for level in range(LEVELS):
            refs[-1][level, origin(here, k, size) // 2] = refs[j][1 - (here & 1), level]


def own_rows_kernel(size, here_ref, *refs):
    here = here_ref[0]
    core = here & 1
    out_ref, sems = refs[-2:]
    copies = []
    for j, k in enumerate(order_of(size)):
        chip = origin(here, k, size) // 2
        for level in range(LEVELS):
            copies.append(
                pltpu.make_async_copy(refs[j].at[core, level], out_ref.at[level, chip, core], sems.at[level, j])
            )
    for copy in copies:
        copy.start()
    for copy in copies:
        copy.wait()


def other_rows_kernel(here_ref, back_ref, held_ref, out_ref, sems):
    del held_ref
    core = here_ref[0] & 1
    copies = []
    for level in range(LEVELS):
        for chip in range(back_ref.shape[1]):
            copies.append(
                pltpu.make_async_copy(
                    back_ref.at[level, chip], out_ref.at[level, chip, 1 - core], sems.at[level, chip]
                )
            )
    for copy in copies:
        copy.start()
    for copy in copies:
        copy.wait()


def local(path_delta, assign, params, momentum):
    own_slab = path_delta[0]
    size = assign.shape[0]
    module_count, _, own_rows, width = params.shape
    shards = lax.axis_size("shard")
    entries = float(own_slab.size * shards)
    state_in = params.reshape(module_count, own_rows, width)
    moment_in = momentum.reshape(module_count, own_rows, width)
    split_slab = own_slab.reshape(LEVELS, size // 2, 2, own_rows, width)
    here = lax.axis_index("path").astype(jnp.int32).reshape(1)
    order = order_of(size)
    rounds = len(order)
    swap = [(i, i ^ 1) for i in range(size)]
    shape = lambda *dims: jax.ShapeDtypeStruct(dims, jnp.float32)
    squares_shape = shape(-(-size // 8) * 8, 128)
    by_chip = shape(LEVELS, rounds, own_rows, width)
    message = shape(2, LEVELS, own_rows, width)
    count = own_rows * width // 1024

    squares, keep, give = call(pack_kernel, [squares_shape, by_chip, by_chip], [smem, vmem], [vmem] * 3)(
        here, split_slab
    )
    gift = lax.ppermute(give, "path", swap)
    tiles = [squares] + [
        lax.ppermute(squares, "shard", [(i, i ^ step) for i in range(shards)]) for step in range(1, shards)
    ]
    firsts = call(
        lambda *refs: first_merge_kernel(size, *refs),
        [shape(2 * (count + in_first(count)), 8, 128)] * rounds,
        [smem, vmem, vmem],
        [vmem] * rounds,
    )(here, keep, gift)
    firsts = [move(firsts[j], k, size) for j, k in enumerate(order)]
    decay = moment_coef * moment_in
    decayed = call(decay_kernel, shape(*state_in.shape), [vmem, vmem], vmem)(state_in, decay)
    plan, leaders = call(
        plan_kernel,
        [
            jax.ShapeDtypeStruct((LEVELS, 5 * size), jnp.int32),
            jax.ShapeDtypeStruct((module_count,), jnp.int32),
        ],
        [smem, smem],
        [smem, smem],
    )(here, assign.T)
    squares = call(
        lambda *refs: sum_kernel(shards, *refs), squares_shape, [vmem] * shards + [anywhere], vmem
    )(*tiles, decay)
    other = lax.ppermute(squares, "path", swap)
    seconds = call(
        lambda *refs: second_merge_kernel(size, *refs),
        [shape(1 + 2 * (count - in_first(count)), 8, 128)] * rounds,
        [smem] + [vmem] * 4,
        [vmem] * rounds,
    )(here, squares, other, keep, gift)
    seconds = [move(seconds[j], k, size) for j, k in enumerate(order)]

    *outgoing, grad = call(
        lambda *refs: outgoing_kernel(rounds, entries, *refs),
        [message] * rounds + [shape(LEVELS, size, own_rows, width)],
        [smem] + [vmem] * (1 + 2 * rounds),
        [vmem] * (rounds + 1),
        scratch_shapes=[pltpu.VMEM(squares_shape.shape, jnp.float32)],
    )(plan, decayed, *firsts, *seconds)
    returned = [move(outgoing[j], k, size) for j, k in enumerate(order)]
    block = LEVEL_MODULES // 2
    state_block = pl.BlockSpec((block, own_rows, width), lambda i: (i, 0, 0))
    new_state, new_moment, done = call(
        state_kernel,
        [shape(*state_in.shape)] * 2 + [shape(8, 128)],
        [smem, vmem, vmem, vmem],
        [state_block, state_block, vmem],
        grid=(module_count // block,),
    )(leaders, grad, decayed, moment_in)
    back = call(
        lambda *refs: give_back_kernel(size, *refs), by_chip, [smem] + [vmem] * rounds + [anywhere], vmem
    )(here, *returned, done)
    back = lax.ppermute(back, "path", swap)
    sems = [pltpu.SemaphoreType.DMA((LEVELS, rounds))]
    path_params = call(
        lambda *refs: own_rows_kernel(size, *refs),
        shape(*split_slab.shape),
        [smem] + [anywhere] * rounds,
        anywhere,
        scratch_shapes=sems,
    )(here, *returned)
    path_params = call(
        other_rows_kernel,
        shape(*split_slab.shape),
        [smem, anywhere, anywhere],
        anywhere,
        scratch_shapes=sems,
        input_output_aliases={2: 0},
    )(here, back, path_params)
    return (path_params.reshape(path_delta.shape), new_state[:, None], new_moment[:, None])


def local_wide(path_delta, assign, params, momentum):
    own_slab = path_delta[0]
    path_count = assign.shape[0]
    module_count, _, own_rows, width = params.shape
    entries = float(own_slab.size * lax.axis_size("shard"))
    total_sq = lax.psum(jnp.sum(own_slab * own_slab), "shard")
    scaled = own_slab * (1.0 / jnp.sqrt(total_sq / entries + 1e-06))
    received = lax.all_to_all(
        scaled.reshape(LEVELS, path_count, own_rows, width), "path", split_axis=1, concat_axis=1, tiled=True
    )
    flat_ids = (assign + LEVEL_MODULES * jnp.arange(LEVELS, dtype=jnp.int32)[None, :]).T.reshape(-1)
    member = (jnp.arange(module_count, dtype=jnp.int32)[:, None] == flat_ids[None, :]).astype(jnp.float32)
    mean = member / jnp.maximum(jnp.sum(member, axis=1), 1.0)[:, None]
    grad = jnp.einsum(
        "mp,prd->mrd", mean, received.reshape(-1, own_rows, width), precision=lax.Precision.HIGHEST
    )
    new_moment = beta_coef * momentum[:, 0] + grad
    new_state = params[:, 0] - outer_rate * (grad + beta_coef * new_moment)
    outgoing = jnp.take(new_state, flat_ids, axis=0).reshape(LEVELS, path_count, own_rows, width)
    returned = lax.all_to_all(outgoing, "path", split_axis=1, concat_axis=1, tiled=True)
    return (returned.reshape(path_delta.shape), new_state[:, None], new_moment[:, None])


def solution(mesh):
    in_specs = (
        P("path", None, "shard", None),
        P(),
        P(None, "shard", "path", None),
        P(None, "shard", "path", None),
    )
    out_specs = (
        P("path", None, "shard", None),
        P(None, "shard", "path", None),
        P(None, "shard", "path", None),
    )
    chosen = local if 4 <= mesh.shape["path"] <= MOST_UNROLLED else local_wide
    return jax.shard_map(chosen, mesh=mesh, in_specs=in_specs, out_specs=out_specs, check_vma=False)
```

```python
import jax
import jax.numpy as jnp
from jax import lax
from jax.experimental import pallas as pl
from jax.experimental.pallas import tpu as pltpu
from jax.sharding import PartitionSpec as P

LEVEL_MODULES = 16
LEVELS = 2
MOST_UNROLLED = 8
EIGHTHS = 3

outer_rate = 0.7
beta_coef = 0.9
moment_coef = outer_rate * beta_coef * beta_coef
grad_coef = outer_rate * (1.0 + beta_coef)

VMEM_LIMIT = 16 * 1024 * 1024

vmem = pl.BlockSpec(memory_space=pltpu.VMEM)
smem = pl.BlockSpec(memory_space=pltpu.SMEM)
anywhere = pl.BlockSpec(memory_space=pl.ANY)


def call(kernel, out_shape, in_specs, out_specs, **more):
    return pl.pallas_call(
        kernel,
        out_shape=out_shape,
        in_specs=in_specs,
        out_specs=out_specs,
        compiler_params=pltpu.CompilerParams(vmem_limit_bytes=VMEM_LIMIT),
        **more,
    )


def mirrored(k, size):
    if size < 8:
        return k
    return (k & ~6) | ((k & 2) << 1) | ((k & 4) >> 1)


def target(here, k, size):
    if isinstance(here, int):
        return here ^ (mirrored(k, size) if here & 1 else k)
    return here ^ jnp.where(here & 1 == 1, mirrored(k, size), k)


def origin(here, k, size):
    if isinstance(here, int):
        return here ^ (mirrored(k, size) if (here ^ k) & 1 else k)
    return here ^ jnp.where((here ^ k) & 1 == 1, mirrored(k, size), k)


def order_of(size):
    return sorted(range(2, size, 2), key=lambda k: (-bin(k).count("1"), k)) + [0]


def move(array, k, size):
    if k == 0:
        return array
    return lax.ppermute(array, "path", [(i, target(i, k, size)) for i in range(size)])


def tiles_of(rows, width):
    return [(slice(row, row + 8), slice(lane, lane + 128)) for row in range(0, rows, 8) for lane in range(0, width, 128)]


def pack_kernel(here_ref, delta_ref, square_ref, keep_ref, give_ref):
    levels, chips, halves, rows, width = delta_ref.shape

    def pack(core):
        totals = [jnp.zeros((8, 128), jnp.float32) for _ in range(4)]
        for level in range(levels):
            for chip in range(chips):
                for t, spot in enumerate(tiles_of(rows, width)):
                    kept = delta_ref[(level, chip, core, *spot)]
                    given = delta_ref[(level, chip, 1 - core, *spot)]
                    keep_ref[(level, chip, *spot)] = kept
                    give_ref[(level, chip, *spot)] = given
                    totals[t % 4] = totals[t % 4] + (kept * kept + given * given)
        total = jnp.sum((totals[0] + totals[1]) + (totals[2] + totals[3]), axis=0, keepdims=True)
        for first in range(0, square_ref.shape[0], 8):
            row = lax.broadcasted_iota(jnp.int32, (8, 128), 0) + first
            square_ref[first : first + 8] = jnp.where(row == here_ref[0], total, 0.0)

    for core in range(halves):
        pl.when(here_ref[0] & 1 == core)(lambda core=core: pack(core))


def in_first(count):
    return count * EIGHTHS // 8


def first_merge_kernel(size, here_ref, keep_ref, gift_ref, *outs):
    here = here_ref[0]
    core = here & 1
    spots = tiles_of(*keep_ref.shape[2:])
    sent = [(0, spot) for spot in spots] + [(1, spot) for spot in spots[: in_first(len(spots))]]
    for k, out in zip(order_of(size), outs):
        chip = target(here, k, size) // 2
        for source, ref in ((core, keep_ref), (1 - core, gift_ref)):
            for t, (level, spot) in enumerate(sent):
                out[source * len(sent) + t] = ref[(level, chip, *spot)]


def second_merge_kernel(size, here_ref, square_ref, other_ref, keep_ref, gift_ref, *outs):
    here = here_ref[0]
    core = here & 1
    squares = square_ref[...] + other_ref[...]
    spots = tiles_of(*keep_ref.shape[2:])
    spots = spots[in_first(len(spots)) :]
    for k, out in zip(order_of(size), outs):
        chip = target(here, k, size) // 2
        out[0] = squares
        for source, ref in ((core, keep_ref), (1 - core, gift_ref)):
            for t, spot in enumerate(spots):
                out[1 + source * len(spots) + t] = ref[(1, chip, *spot)]


def sum_kernel(count, *refs):
    total = refs[0][...]
    for ref in refs[1:count]:
        total = total + ref[...]
    refs[-1][...] = total


def decay_kernel(params_ref, decay_ref, out_ref):
    def decay(module, carry):
        out_ref[module] = params_ref[module] - decay_ref[module]
        return carry

    lax.fori_loop(0, out_ref.shape[0], decay, 0)


def plan_kernel(here_ref, ids_ref, plan_ref, module_ref):
    size = ids_ref.shape[1]
    order = order_of(size)
    here = here_ref[0]
    paths = [(origin(here, k, size) // 2) * 2 + half for k in order for half in range(2)]
    targets = [(target(here, k, size) // 2) * 2 + half for k in order for half in range(2)]
    for level in range(LEVELS):
        first = level * LEVEL_MODULES
        for module in range(LEVEL_MODULES):
            module_ref[first + module] = -1
        sources = [ids_ref[level, path] + first for path in paths]
        for i in reversed(range(size)):
            module_ref[sources[i]] = i
        for i in range(size):
            plan_ref[level, i] = module_ref[sources[i]]
            sharers = jnp.int32(0)
            for other in range(size):
                sharers = sharers + jnp.where(sources[other] == sources[i], 1, 0)
            plan_ref[level, size + i] = sharers
            plan_ref[level, 2 * size + i] = paths[i]
            module = ids_ref[level, targets[i]] + first
            plan_ref[level, 3 * size + i] = module
            plan_ref[level, 4 * size + i] = module_ref[module]


def outgoing_kernel(rounds, entries, plan_ref, decayed_ref, *refs):
    firsts, seconds = refs[:rounds], refs[rounds : 2 * rounds]
    outs, (grad_ref, rescale_ref) = refs[2 * rounds : -2], refs[-2:]
    size = 2 * rounds
    rows, width = grad_ref.shape[2:]
    spots = tiles_of(rows, width)
    count, early = len(spots), in_first(len(spots))
    squares = seconds[0][0]
    for second in seconds[1:]:
        squares = squares + second[0]
    total = jnp.sum(squares, axis=1, keepdims=True)
    rescale_ref[...] = jnp.broadcast_to(1.0 / jnp.sqrt(total / entries + 1e-06), rescale_ref.shape)
    for level in range(LEVELS):
        for i in range(size):
            rescale = jnp.broadcast_to(rescale_ref[pl.ds(plan_ref[level, 2 * size + i], 1), :], (8, 128))
            factor = rescale / jnp.full((8, 128), plan_ref[level, size + i], jnp.int32).astype(jnp.float32)
            for t, spot in enumerate(spots):
                if level == 0 or t < early:
                    block = firsts[i // 2][(i % 2) * (count + early) + level * count + t]
                else:
                    block = seconds[i // 2][1 + (i % 2) * (count - early) + t - early]
                grad_ref[(level, i, *spot)] = block * factor
        for i in range(1, size):
            leader = plan_ref[level, i]

            @pl.when(leader != i)
            def _():
                grad_ref[level, leader] += grad_ref[level, i]

        for i in range(size):
            decayed = decayed_ref[plan_ref[level, 3 * size + i]]
            outs[i // 2][i % 2, level] = decayed - grad_coef * grad_ref[level, plan_ref[level, 4 * size + i]]


def state_kernel(module_ref, grad_ref, decayed_ref, momentum_ref, new_params_ref, new_momentum_ref, token_ref):
    token_ref[...] = jnp.zeros_like(token_ref)
    count = new_params_ref.shape[0]
    first = pl.program_id(0) * count
    level = first // LEVEL_MODULES
    for place in range(count):
        module = first + place
        leader = module_ref[module]
        taken = jnp.where(leader < 0, 0.0, 1.0)
        grad = taken * grad_ref[level, jnp.maximum(leader, 0)]
        new_momentum_ref[place] = beta_coef * momentum_ref[module] + grad
        new_params_ref[place] = decayed_ref[module] - grad_coef * grad


def give_back_kernel(size, here_ref, *refs):
    here = here_ref[0]
    for j, k in enumerate(order_of(size)):
        for level in range(LEVELS):
            refs[-1][level, origin(here, k, size) // 2] = refs[j][1 - (here & 1), level]


def own_rows_kernel(size, here_ref, *refs):
    here = here_ref[0]
    core = here & 1
    out_ref, sems = refs[-2:]
    copies = []
    for j, k in enumerate(order_of(size)):
        chip = origin(here, k, size) // 2
        for level in range(LEVELS):
            copies.append(
                pltpu.make_async_copy(refs[j].at[core, level], out_ref.at[level, chip, core], sems.at[level, j])
            )
    for copy in copies:
        copy.start()
    for copy in copies:
        copy.wait()


def other_rows_kernel(here_ref, back_ref, held_ref, out_ref, sems):
    del held_ref
    core = here_ref[0] & 1
    copies = [
        pltpu.make_async_copy(back_ref.at[level], out_ref.at[level, :, 1 - core], sems.at[level, 0])
        for level in range(LEVELS)
    ]
    for copy in copies:
        copy.start()
    for copy in copies:
        copy.wait()


def local(path_delta, assign, params, momentum):
    own_slab = path_delta[0]
    size = assign.shape[0]
    module_count, _, own_rows, width = params.shape
    shards = lax.axis_size("shard")
    entries = float(own_slab.size * shards)
    state_in = params.reshape(module_count, own_rows, width)
    moment_in = momentum.reshape(module_count, own_rows, width)
    split_slab = own_slab.reshape(LEVELS, size // 2, 2, own_rows, width)
    here = lax.axis_index("path").astype(jnp.int32).reshape(1)
    order = order_of(size)
    rounds = len(order)
    swap = [(i, i ^ 1) for i in range(size)]
    shape = lambda *dims: jax.ShapeDtypeStruct(dims, jnp.float32)
    squares_shape = shape(-(-size // 8) * 8, 128)
    by_chip = shape(LEVELS, rounds, own_rows, width)
    message = shape(2, LEVELS, own_rows, width)
    count = own_rows * width // 1024

    squares, keep, give = call(pack_kernel, [squares_shape, by_chip, by_chip], [smem, vmem], [vmem] * 3)(
        here, split_slab
    )
    gift = lax.ppermute(give, "path", swap)
    tiles = [squares] + [
        lax.ppermute(squares, "shard", [(i, i ^ step) for i in range(shards)]) for step in range(shards - 1, 0, -1)
    ]
    firsts = call(
        lambda *refs: first_merge_kernel(size, *refs),
        [shape(2 * (count + in_first(count)), 8, 128)] * rounds,
        [smem, vmem, vmem],
        [vmem] * rounds,
    )(here, keep, gift)
    firsts = [move(firsts[j], k, size) for j, k in enumerate(order)]
    decay = moment_coef * moment_in
    decayed = call(decay_kernel, shape(*state_in.shape), [vmem, vmem], vmem)(state_in, decay)
    plan, leaders = call(
        plan_kernel,
        [
            jax.ShapeDtypeStruct((LEVELS, 5 * size), jnp.int32),
            jax.ShapeDtypeStruct((module_count,), jnp.int32),
        ],
        [smem, smem],
        [smem, smem],
    )(here, assign.T)
    squares = call(
        lambda *refs: sum_kernel(shards, *refs), squares_shape, [vmem] * shards + [anywhere], vmem
    )(*tiles, decay)
    other = lax.ppermute(squares, "path", swap)
    seconds = call(
        lambda *refs: second_merge_kernel(size, *refs),
        [shape(1 + 2 * (count - in_first(count)), 8, 128)] * rounds,
        [smem] + [vmem] * 4,
        [vmem] * rounds,
    )(here, squares, other, keep, gift)
    seconds = [move(seconds[j], k, size) for j, k in enumerate(order)]

    *outgoing, grad = call(
        lambda *refs: outgoing_kernel(rounds, entries, *refs),
        [message] * rounds + [shape(LEVELS, size, own_rows, width)],
        [smem] + [vmem] * (1 + 2 * rounds),
        [vmem] * (rounds + 1),
        scratch_shapes=[pltpu.VMEM(squares_shape.shape, jnp.float32)],
    )(plan, decayed, *firsts, *seconds)
    returned = [move(outgoing[j], k, size) for j, k in enumerate(order)]
    block = LEVEL_MODULES // 2
    state_block = pl.BlockSpec((block, own_rows, width), lambda i: (i, 0, 0))
    new_state, new_moment, done = call(
        state_kernel,
        [shape(*state_in.shape)] * 2 + [shape(8, 128)],
        [smem, vmem, vmem, vmem],
        [state_block, state_block, vmem],
        grid=(module_count // block,),
    )(leaders, grad, decayed, moment_in)
    back = call(
        lambda *refs: give_back_kernel(size, *refs), by_chip, [smem] + [vmem] * rounds + [anywhere], vmem
    )(here, *returned, done)
    back = lax.ppermute(back, "path", swap)
    sems = [pltpu.SemaphoreType.DMA((LEVELS, rounds))]
    path_params = call(
        lambda *refs: own_rows_kernel(size, *refs),
        shape(*split_slab.shape),
        [smem] + [anywhere] * rounds,
        anywhere,
        scratch_shapes=sems,
    )(here, *returned)
    path_params = call(
        other_rows_kernel,
        shape(*split_slab.shape),
        [smem, anywhere, anywhere],
        anywhere,
        scratch_shapes=sems,
        input_output_aliases={2: 0},
    )(here, back, path_params)
    return (path_params.reshape(path_delta.shape), new_state[:, None], new_moment[:, None])


def local_wide(path_delta, assign, params, momentum):
    own_slab = path_delta[0]
    path_count = assign.shape[0]
    module_count, _, own_rows, width = params.shape
    entries = float(own_slab.size * lax.axis_size("shard"))
    total_sq = lax.psum(jnp.sum(own_slab * own_slab), "shard")
    scaled = own_slab * (1.0 / jnp.sqrt(total_sq / entries + 1e-06))
    received = lax.all_to_all(
        scaled.reshape(LEVELS, path_count, own_rows, width), "path", split_axis=1, concat_axis=1, tiled=True
    )
    flat_ids = (assign + LEVEL_MODULES * jnp.arange(LEVELS, dtype=jnp.int32)[None, :]).T.reshape(-1)
    member = (jnp.arange(module_count, dtype=jnp.int32)[:, None] == flat_ids[None, :]).astype(jnp.float32)
    mean = member / jnp.maximum(jnp.sum(member, axis=1), 1.0)[:, None]
    grad = jnp.einsum(
        "mp,prd->mrd", mean, received.reshape(-1, own_rows, width), precision=lax.Precision.HIGHEST
    )
    new_moment = beta_coef * momentum[:, 0] + grad
    new_state = params[:, 0] - outer_rate * (grad + beta_coef * new_moment)
    outgoing = jnp.take(new_state, flat_ids, axis=0).reshape(LEVELS, path_count, own_rows, width)
    returned = lax.all_to_all(outgoing, "path", split_axis=1, concat_axis=1, tiled=True)
    return (returned.reshape(path_delta.shape), new_state[:, None], new_moment[:, None])


def solution(mesh):
    in_specs = (
        P("path", None, "shard", None),
        P(),
        P(None, "shard", "path", None),
        P(None, "shard", "path", None),
    )
    out_specs = (
        P("path", None, "shard", None),
        P(None, "shard", "path", None),
        P(None, "shard", "path", None),
    )
    chosen = local if 4 <= mesh.shape["path"] <= MOST_UNROLLED else local_wide
    return jax.shard_map(chosen, mesh=mesh, in_specs=in_specs, out_specs=out_specs, check_vma=False)
```

```python
import jax
import jax.numpy as jnp
from jax import lax
from jax.experimental import pallas as pl
from jax.experimental.pallas import tpu as pltpu
from jax.sharding import PartitionSpec as P

LEVEL_MODULES = 16
LEVELS = 2
MOST_UNROLLED = 8
EIGHTHS = 3

outer_rate = 0.7
beta_coef = 0.9
moment_coef = outer_rate * beta_coef * beta_coef
grad_coef = outer_rate * (1.0 + beta_coef)

VMEM_LIMIT = 16 * 1024 * 1024

vmem = pl.BlockSpec(memory_space=pltpu.VMEM)
smem = pl.BlockSpec(memory_space=pltpu.SMEM)
anywhere = pl.BlockSpec(memory_space=pl.ANY)


def call(kernel, out_shape, in_specs, out_specs, **more):
    return pl.pallas_call(
        kernel,
        out_shape=out_shape,
        in_specs=in_specs,
        out_specs=out_specs,
        compiler_params=pltpu.CompilerParams(vmem_limit_bytes=VMEM_LIMIT),
        **more,
    )


def mirrored(k, size):
    if size < 8:
        return k
    return (k & ~6) | ((k & 2) << 1) | ((k & 4) >> 1)


def target(here, k, size):
    if isinstance(here, int):
        return here ^ (mirrored(k, size) if here & 1 else k)
    return here ^ jnp.where(here & 1 == 1, mirrored(k, size), k)


def origin(here, k, size):
    if isinstance(here, int):
        return here ^ (mirrored(k, size) if (here ^ k) & 1 else k)
    return here ^ jnp.where((here ^ k) & 1 == 1, mirrored(k, size), k)


def order_of(size):
    return sorted(range(2, size, 2), key=lambda k: (-bin(k).count("1"), k)) + [0]


def move(array, k, size):
    if k == 0:
        return array
    return lax.ppermute(array, "path", [(i, target(i, k, size)) for i in range(size)])


def tiles_of(rows, width):
    return [(slice(row, row + 8), slice(lane, lane + 128)) for row in range(0, rows, 8) for lane in range(0, width, 128)]


def pack_kernel(here_ref, delta_ref, square_ref, keep_ref, give_ref):
    levels, chips, halves, rows, width = delta_ref.shape

    def pack(core):
        totals = [jnp.zeros((8, 128), jnp.float32) for _ in range(4)]
        for level in range(levels):
            for chip in range(chips):
                for t, spot in enumerate(tiles_of(rows, width)):
                    kept = delta_ref[(level, chip, core, *spot)]
                    given = delta_ref[(level, chip, 1 - core, *spot)]
                    keep_ref[(level, chip, *spot)] = kept
                    give_ref[(level, chip, *spot)] = given
                    totals[t % 4] = totals[t % 4] + (kept * kept + given * given)
        total = jnp.sum((totals[0] + totals[1]) + (totals[2] + totals[3]), axis=0, keepdims=True)
        for first in range(0, square_ref.shape[0], 8):
            row = lax.broadcasted_iota(jnp.int32, (8, 128), 0) + first
            square_ref[first : first + 8] = jnp.where(row == here_ref[0], total, 0.0)

    for core in range(halves):
        pl.when(here_ref[0] & 1 == core)(lambda core=core: pack(core))


def in_first(count):
    return count * EIGHTHS // 8


def first_merge_kernel(size, here_ref, keep_ref, gift_ref, *outs):
    here = here_ref[0]
    core = here & 1
    spots = tiles_of(*keep_ref.shape[2:])
    sent = [(0, spot) for spot in spots] + [(1, spot) for spot in spots[: in_first(len(spots))]]
    for k, out in zip(order_of(size), outs):
        chip = target(here, k, size) // 2
        for source, ref in ((core, keep_ref), (1 - core, gift_ref)):
            for t, (level, spot) in enumerate(sent):
                out[source * len(sent) + t] = ref[(level, chip, *spot)]


def second_merge_kernel(size, here_ref, square_ref, other_ref, keep_ref, gift_ref, *outs):
    here = here_ref[0]
    core = here & 1
    squares = square_ref[...] + other_ref[...]
    spots = tiles_of(*keep_ref.shape[2:])
    spots = spots[in_first(len(spots)) :]
    for k, out in zip(order_of(size), outs):
        chip = target(here, k, size) // 2
        out[0] = squares
        for source, ref in ((core, keep_ref), (1 - core, gift_ref)):
            for t, spot in enumerate(spots):
                out[1 + source * len(spots) + t] = ref[(1, chip, *spot)]


def sum_kernel(count, *refs):
    total = refs[0][...]
    for ref in refs[1:count]:
        total = total + ref[...]
    refs[-1][...] = total


def decay_kernel(params_ref, decay_ref, out_ref):
    def decay(module, carry):
        out_ref[module] = params_ref[module] - decay_ref[module]
        return carry

    lax.fori_loop(0, out_ref.shape[0], decay, 0)


def plan_kernel(here_ref, ids_ref, plan_ref, module_ref):
    size = ids_ref.shape[1]
    order = order_of(size)
    here = here_ref[0]
    paths = [(origin(here, k, size) // 2) * 2 + half for k in order for half in range(2)]
    targets = [(target(here, k, size) // 2) * 2 + half for k in order for half in range(2)]
    for level in range(LEVELS):
        first = level * LEVEL_MODULES
        for module in range(LEVEL_MODULES):
            module_ref[first + module] = -1
        sources = [ids_ref[level, path] + first for path in paths]
        for i in reversed(range(size)):
            module_ref[sources[i]] = i
        for i in range(size):
            plan_ref[level, i] = module_ref[sources[i]]
            sharers = jnp.int32(0)
            for other in range(size):
                sharers = sharers + jnp.where(sources[other] == sources[i], 1, 0)
            plan_ref[level, size + i] = sharers
            plan_ref[level, 2 * size + i] = paths[i]
            module = ids_ref[level, targets[i]] + first
            plan_ref[level, 3 * size + i] = module
            plan_ref[level, 4 * size + i] = module_ref[module]


def outgoing_kernel(rounds, entries, plan_ref, decayed_ref, *refs):
    firsts, seconds = refs[:rounds], refs[rounds : 2 * rounds]
    outs, (grad_ref, rescale_ref) = refs[2 * rounds : -2], refs[-2:]
    size = 2 * rounds
    rows, width = grad_ref.shape[2:]
    spots = tiles_of(rows, width)
    count, early = len(spots), in_first(len(spots))
    squares = seconds[0][0]
    for second in seconds[1:]:
        squares = squares + second[0]
    total = jnp.sum(squares, axis=1, keepdims=True)
    rescale_ref[...] = jnp.broadcast_to(1.0 / jnp.sqrt(total / entries + 1e-06), rescale_ref.shape)
    for level in range(LEVELS):
        for i in range(size):
            rescale = jnp.broadcast_to(rescale_ref[pl.ds(plan_ref[level, 2 * size + i], 1), :], (8, 128))
            factor = rescale / jnp.full((8, 128), plan_ref[level, size + i], jnp.int32).astype(jnp.float32)
            for t, spot in enumerate(spots):
                if level == 0 or t < early:
                    block = firsts[i // 2][(i % 2) * (count + early) + level * count + t]
                else:
                    block = seconds[i // 2][1 + (i % 2) * (count - early) + t - early]
                grad_ref[(level, i, *spot)] = block * factor
        for i in range(1, size):
            leader = plan_ref[level, i]

            @pl.when(leader != i)
            def _():
                grad_ref[level, leader] += grad_ref[level, i]

        for i in range(size):
            decayed = decayed_ref[plan_ref[level, 3 * size + i]]
            outs[i // 2][i % 2, level] = decayed - grad_coef * grad_ref[level, plan_ref[level, 4 * size + i]]


def state_kernel(module_ref, grad_ref, decayed_ref, momentum_ref, new_params_ref, new_momentum_ref, token_ref):
    token_ref[...] = jnp.zeros_like(token_ref)
    count = new_params_ref.shape[0]
    first = pl.program_id(0) * count
    level = first // LEVEL_MODULES
    for place in range(count):
        module = first + place
        leader = module_ref[module]
        taken = jnp.where(leader < 0, 0.0, 1.0)
        grad = taken * grad_ref[level, jnp.maximum(leader, 0)]
        new_momentum_ref[place] = beta_coef * momentum_ref[module] + grad
        new_params_ref[place] = decayed_ref[module] - grad_coef * grad


def give_back_kernel(size, here_ref, *refs):
    here = here_ref[0]
    for j, k in enumerate(order_of(size)):
        for level in range(LEVELS):
            refs[level - LEVELS][origin(here, k, size) // 2] = refs[j][1 - (here & 1), level]


def own_rows_kernel(size, here_ref, *refs):
    here = here_ref[0]
    core = here & 1
    out_ref, sems = refs[-2:]
    copies = []
    for j, k in enumerate(order_of(size)):
        chip = origin(here, k, size) // 2
        for level in range(LEVELS):
            copies.append(
                pltpu.make_async_copy(refs[j].at[core, level], out_ref.at[level, chip, core], sems.at[level, j])
            )
    for copy in copies:
        copy.start()
    for copy in copies:
        copy.wait()


def other_rows_kernel(level, here_ref, back_ref, held_ref, out_ref, sems):
    del held_ref
    core = here_ref[0] & 1
    copies = [
        pltpu.make_async_copy(back_ref.at[chip], out_ref.at[level, chip, 1 - core], sems.at[level, chip])
        for chip in range(back_ref.shape[0])
    ]
    for copy in copies:
        copy.start()
    for copy in copies:
        copy.wait()


def local(path_delta, assign, params, momentum):
    own_slab = path_delta[0]
    size = assign.shape[0]
    module_count, _, own_rows, width = params.shape
    shards = lax.axis_size("shard")
    entries = float(own_slab.size * shards)
    state_in = params.reshape(module_count, own_rows, width)
    moment_in = momentum.reshape(module_count, own_rows, width)
    split_slab = own_slab.reshape(LEVELS, size // 2, 2, own_rows, width)
    here = lax.axis_index("path").astype(jnp.int32).reshape(1)
    order = order_of(size)
    rounds = len(order)
    swap = [(i, i ^ 1) for i in range(size)]
    shape = lambda *dims: jax.ShapeDtypeStruct(dims, jnp.float32)
    squares_shape = shape(-(-size // 8) * 8, 128)
    by_chip = shape(LEVELS, rounds, own_rows, width)
    message = shape(2, LEVELS, own_rows, width)
    count = own_rows * width // 1024

    squares, keep, give = call(pack_kernel, [squares_shape, by_chip, by_chip], [smem, vmem], [vmem] * 3)(
        here, split_slab
    )
    gift = lax.ppermute(give, "path", swap)
    tiles = [squares] + [
        lax.ppermute(squares, "shard", [(i, i ^ step) for i in range(shards)]) for step in range(shards - 1, 0, -1)
    ]
    firsts = call(
        lambda *refs: first_merge_kernel(size, *refs),
        [shape(2 * (count + in_first(count)), 8, 128)] * rounds,
        [smem, vmem, vmem],
        [vmem] * rounds,
    )(here, keep, gift)
    firsts = [move(firsts[j], k, size) for j, k in enumerate(order)]
    decay = moment_coef * moment_in
    decayed = call(decay_kernel, shape(*state_in.shape), [vmem, vmem], vmem)(state_in, decay)
    plan, leaders = call(
        plan_kernel,
        [
            jax.ShapeDtypeStruct((LEVELS, 5 * size), jnp.int32),
            jax.ShapeDtypeStruct((module_count,), jnp.int32),
        ],
        [smem, smem],
        [smem, smem],
    )(here, assign.T)
    squares = call(
        lambda *refs: sum_kernel(shards, *refs), squares_shape, [vmem] * shards + [anywhere], vmem
    )(*tiles, decay)
    other = lax.ppermute(squares, "path", swap)
    seconds = call(
        lambda *refs: second_merge_kernel(size, *refs),
        [shape(1 + 2 * (count - in_first(count)), 8, 128)] * rounds,
        [smem] + [vmem] * 4,
        [vmem] * rounds,
    )(here, squares, other, keep, gift)
    seconds = [move(seconds[j], k, size) for j, k in enumerate(order)]

    *outgoing, grad = call(
        lambda *refs: outgoing_kernel(rounds, entries, *refs),
        [message] * rounds + [shape(LEVELS, size, own_rows, width)],
        [smem] + [vmem] * (1 + 2 * rounds),
        [vmem] * (rounds + 1),
        scratch_shapes=[pltpu.VMEM(squares_shape.shape, jnp.float32)],
    )(plan, decayed, *firsts, *seconds)
    returned = [move(outgoing[j], k, size) for j, k in enumerate(order)]
    block = LEVEL_MODULES // 2
    state_block = pl.BlockSpec((block, own_rows, width), lambda i: (i, 0, 0))
    new_state, new_moment, done = call(
        state_kernel,
        [shape(*state_in.shape)] * 2 + [shape(8, 128)],
        [smem, vmem, vmem, vmem],
        [state_block, state_block, vmem],
        grid=(module_count // block,),
    )(leaders, grad, decayed, moment_in)
    backs = call(
        lambda *refs: give_back_kernel(size, *refs),
        [shape(rounds, own_rows, width)] * LEVELS,
        [smem] + [vmem] * rounds + [anywhere],
        [vmem] * LEVELS,
    )(here, *returned, done)
    backs = [lax.ppermute(back, "path", swap) for back in backs]
    sems = [pltpu.SemaphoreType.DMA((LEVELS, rounds))]
    path_params = call(
        lambda *refs: own_rows_kernel(size, *refs),
        shape(*split_slab.shape),
        [smem] + [anywhere] * rounds,
        anywhere,
        scratch_shapes=sems,
    )(here, *returned)
    for level in range(LEVELS):
        path_params = call(
            lambda *refs, level=level: other_rows_kernel(level, *refs),
            shape(*split_slab.shape),
            [smem, anywhere, anywhere],
            anywhere,
            scratch_shapes=sems,
            input_output_aliases={2: 0},
        )(here, backs[level], path_params)
    return (path_params.reshape(path_delta.shape), new_state[:, None], new_moment[:, None])


def local_wide(path_delta, assign, params, momentum):
    own_slab = path_delta[0]
    path_count = assign.shape[0]
    module_count, _, own_rows, width = params.shape
    entries = float(own_slab.size * lax.axis_size("shard"))
    total_sq = lax.psum(jnp.sum(own_slab * own_slab), "shard")
    scaled = own_slab * (1.0 / jnp.sqrt(total_sq / entries + 1e-06))
    received = lax.all_to_all(
        scaled.reshape(LEVELS, path_count, own_rows, width), "path", split_axis=1, concat_axis=1, tiled=True
    )
    flat_ids = (assign + LEVEL_MODULES * jnp.arange(LEVELS, dtype=jnp.int32)[None, :]).T.reshape(-1)
    member = (jnp.arange(module_count, dtype=jnp.int32)[:, None] == flat_ids[None, :]).astype(jnp.float32)
    mean = member / jnp.maximum(jnp.sum(member, axis=1), 1.0)[:, None]
    grad = jnp.einsum(
        "mp,prd->mrd", mean, received.reshape(-1, own_rows, width), precision=lax.Precision.HIGHEST
    )
    new_moment = beta_coef * momentum[:, 0] + grad
    new_state = params[:, 0] - outer_rate * (grad + beta_coef * new_moment)
    outgoing = jnp.take(new_state, flat_ids, axis=0).reshape(LEVELS, path_count, own_rows, width)
    returned = lax.all_to_all(outgoing, "path", split_axis=1, concat_axis=1, tiled=True)
    return (returned.reshape(path_delta.shape), new_state[:, None], new_moment[:, None])


def solution(mesh):
    in_specs = (
        P("path", None, "shard", None),
        P(),
        P(None, "shard", "path", None),
        P(None, "shard", "path", None),
    )
    out_specs = (
        P("path", None, "shard", None),
        P(None, "shard", "path", None),
        P(None, "shard", "path", None),
    )
    chosen = local if 4 <= mesh.shape["path"] <= MOST_UNROLLED else local_wide
    return jax.shard_map(chosen, mesh=mesh, in_specs=in_specs, out_specs=out_specs, check_vma=False)
```
